32 devices in a mesh: seq: 8 (over y, x, core), head: 4 (over z).
Axes of the slice: x: 2, y: 2, z: 4, core: 2. Of those that a mesh axis runs over, the one named last changes fastest.
Arguments:
- tokens: bfloat16 [4, 4096, 768], P(None, 'seq'), may hold values from -6 to 6
- memory: bfloat16 [4, 1024, 768], P(None, 'seq'), may hold values from -6 to 6
- seq_lengths: int32 [4, 4], replicated, may hold values from 0 to 4096, as said below
- pack_query: bfloat16 [768, 768], P(None, 'head'), may hold values from -0.4375 to 0.4375
- pack_key: bfloat16 [768, 768], P(None, 'head'), may hold values from -0.21875 to 0.21875
- pack_value: bfloat16 [768, 768], P(None, 'head'), may hold values from -0.21875 to 0.21875
- pack_out: bfloat16 [768, 768], P('head'), may hold values from -0.875 to 0.875
- unpack_query: bfloat16 [768, 768], P(None, 'head'), may hold values from -0.21875 to 0.21875
- unpack_key: bfloat16 [768, 768], P(None, 'head'), may hold values from -0.21875 to 0.21875
- unpack_value: bfloat16 [768, 768], P(None, 'head'), may hold values from -0.21875 to 0.21875
- unpack_out: bfloat16 [768, 768], P('head'), may hold values from -1.75 to 1.75
- ffn_in: bfloat16 [768, 3072], P(None, 'head'), may hold values from -0.21875 to 0.21875
- ffn_in_bias: float32 [3072], P('head'), may hold values from -3 to 3
- ffn_out: bfloat16 [3072, 768], P('head'), may hold values from -0.109375 to 0.109375
- ffn_out_bias: float32 [768], replicated, may hold values from -3 to 3
- mem_gain: float32 [768], replicated, may hold values from 0.5 to 1.5
- mem_bias: float32 [768], replicated, may hold values from -2 to 2
- attn_gain: float32 [768], replicated, may hold values from 0.5 to 1.5
- attn_bias: float32 [768], replicated, may hold values from -2 to 2
- out_gain: float32 [768], replicated, may hold values from 0.5 to 1.5
- out_bias: float32 [768], replicated, may hold values from -2 to 2
- cot_tokens: bfloat16 [4, 4096, 768], P(None, 'seq'), may hold values from -6 to 6
- cot_memory: bfloat16 [4, 1024, 768], P(None, 'seq'), may hold values from -0.59765625 to 0.59765625
Outputs:
- out_tokens: bfloat16 [4, 4096, 768], P(None, 'seq')
- out_memory: bfloat16 [4, 1024, 768], P(None, 'seq')
- grad_tokens: bfloat16 [4, 4096, 768], P(None, 'seq')
- grad_memory: bfloat16 [4, 1024, 768], P(None, 'seq')
- grad_pack_query: float32 [768, 768], P('seq', 'head')
- grad_pack_key: float32 [768, 768], P('seq', 'head')
- grad_pack_value: float32 [768, 768], P('seq', 'head')
- grad_pack_out: float32 [768, 768], P(('head', 'seq'))
- grad_unpack_query: float32 [768, 768], P('seq', 'head')
- grad_unpack_key: float32 [768, 768], P('seq', 'head')
- grad_unpack_value: float32 [768, 768], P('seq', 'head')
- grad_unpack_out: float32 [768, 768], P(('head', 'seq'))
- grad_ffn_in: float32 [768, 3072], P('seq', 'head')
- grad_ffn_in_bias: float32 [3072], P(('head', 'seq'))
- grad_ffn_out: float32 [3072, 768], P(('head', 'seq'))
- grad_ffn_out_bias: float32 [768], P('seq')
- grad_mem_gain: float32 [768], P('seq')
- grad_mem_bias: float32 [768], P('seq')
- grad_attn_gain: float32 [768], P('seq')
- grad_attn_bias: float32 [768], P('seq')
- grad_out_gain: float32 [768], P('seq')
- grad_out_bias: float32 [768], P('seq')
The draws below stay inside these ranges and needn't reach their ends.
Inputs may be any that keep to these rules, and one draw needn't show every extreme that they name: `seq_lengths`: each row lists the lengths of the sequences of one pack in the order in which they lie in it, each a multiple of 1024, then zeros; a row begins with a nonzero length and sums to 4096; in some row a single sequence fills the pack.
All inputs are finite; a program needn't handle non-finite values.
Results may differ from the reference program's by a relative error of at most 0.025.
Values may be sent and summed in bfloat16 or wider, within the bound.
No kernel may reach another device: no remote copies, remote signals or barrier semaphores. Data moves between devices by JAX's collectives and lax.ppermute only.
A program may use at most 192 MiB of HBM per device.

```python
import math
import jax
import jax.numpy as jnp
from jax import lax

D = 768
HEADS = 12
HD = 64
FF = 3072
MEM = 256
SEQ_MIN = 1024
PACK = 4096
PACKS = 4
SLOTS = 4
ROWS = 1024


def drawn_field(key, shape):
    values = jnp.clip(jax.random.normal(key, shape, jnp.float32), -6.0, 6.0)
    return values.astype(jnp.bfloat16)


def draw_tokens(key, part):
    key = jax.random.fold_in(key, 21)
    return drawn_field(key, (PACKS, PACK, D))


def draw_memory(key, part):
    key = jax.random.fold_in(key, 33)
    return drawn_field(key, (PACKS, SLOTS * MEM, D))


def draw_seq_lengths(key, part):
    key = jax.random.fold_in(key, 11)
    cut_key, full_key = jax.random.split(key)
    cut_bits = jax.random.randint(cut_key, (PACKS, SLOTS), 0, 2)
    whole_pack = jax.random.randint(full_key, (), 0, PACKS)
    pack_ids = jnp.arange(PACKS, dtype=jnp.int32)[:, None]
    unit_ids = jnp.arange(SLOTS, dtype=jnp.int32)[None, :]
    starts = jnp.where(unit_ids == 0, 1, jnp.where(pack_ids == whole_pack, 0, cut_bits))
    owner_part = jnp.cumsum(starts, axis=1) - 1
    slot_ids = jnp.arange(SLOTS, dtype=jnp.int32)
    counts = jnp.sum((owner_part[:, :, None] == slot_ids[None, None, :]).astype(jnp.int32), axis=1)
    return (counts * SEQ_MIN).astype(jnp.int32)


def level_of(rng, dims, shards, least, largest):
    gain, own = 1.0, jax.random.fold_in(rng, 6)
    for axis_at, parts in shards:
        draws = jnp.exp(jax.random.uniform(jax.random.fold_in(own, axis_at), (parts,), jnp.float32, least / len(shards), largest / len(shards)))
        gain = gain * jnp.repeat(draws, dims[axis_at] // parts).reshape([-1 if axis == axis_at else 1 for axis in range(len(dims))])
    return gain


def bell_draw(key, extent, scale, reach, cuts=(), held_as=jnp.bfloat16):
    gain = level_of(key, extent, cuts, -0.22, 0.18) if cuts else 1.0
    values = jax.random.normal(key, extent, jnp.float32) * scale * gain
    return jnp.minimum(jnp.maximum(values, -reach), reach).astype(held_as)


def setup_inputs(seed: int = 0) -> dict:
    streams_of = jax.random.split(jax.random.key(seed), 24)
    return {
        "tokens": draw_tokens(jax.random.fold_in(streams_of[23], 71), 0),
        "memory": draw_memory(jax.random.fold_in(streams_of[23], 71), 0),
        "seq_lengths": draw_seq_lengths(jax.random.fold_in(streams_of[23], 71), 0),
        "pack_query": bell_draw(streams_of[3], (D, D), (D // 4) ** -0.5, 0.4375, ((1, 4),)),
        "pack_key": bell_draw(streams_of[4], (D, D), D ** -0.5, 0.21875, ((1, 4),)),
        "pack_value": bell_draw(streams_of[5], (D, D), D ** -0.5, 0.21875, ((1, 4),)),
        "pack_out": bell_draw(streams_of[6], (D, D), (D // 16) ** -0.5, 0.875, ((0, 4),)),
        "unpack_query": bell_draw(streams_of[7], (D, D), D ** -0.5, 0.21875, ((1, 4),)),
        "unpack_key": bell_draw(streams_of[8], (D, D), D ** -0.5, 0.21875, ((1, 4),)),
        "unpack_value": bell_draw(streams_of[9], (D, D), D ** -0.5, 0.21875, ((1, 4),)),
        "unpack_out": bell_draw(streams_of[10], (D, D), (D // 64) ** -0.5, 1.75, ((0, 4),)),
        "ffn_in": bell_draw(streams_of[11], (D, FF), D ** -0.5, 0.21875, ((1, 4),)),
        "ffn_in_bias": bell_draw(streams_of[12], (FF,), 0.5, 3.0, ((0, 4),), jnp.float32),
        "ffn_out": bell_draw(streams_of[13], (FF, D), FF ** -0.5, 0.109375, ((0, 4),)),
        "ffn_out_bias": bell_draw(streams_of[14], (D,), 0.5, 3.0, (), jnp.float32),
        "mem_gain": jnp.clip(1.0 + 0.1 * jax.random.normal(streams_of[15], (D,), jnp.float32), 0.5, 1.5),
        "mem_bias": bell_draw(streams_of[16], (D,), 0.3, 2.0, (), jnp.float32),
        "attn_gain": jnp.clip(1.0 + 0.1 * jax.random.normal(streams_of[17], (D,), jnp.float32), 0.5, 1.5),
        "attn_bias": bell_draw(streams_of[18], (D,), 0.3, 2.0, (), jnp.float32),
        "out_gain": jnp.clip(1.0 + 0.1 * jax.random.normal(streams_of[19], (D,), jnp.float32), 0.5, 1.5),
        "out_bias": bell_draw(streams_of[20], (D,), 0.3, 2.0, (), jnp.float32),
        "cot_tokens": bell_draw(streams_of[21], (PACKS, PACK, D), 1.0, 6.0, ((1, 8),)),
        "cot_memory": bell_draw(streams_of[22], (PACKS, ROWS, D), 0.1, 0.59765625, ((1, 8),)),
    }


@jax.custom_vjp
def low(v):
    return lax.optimization_barrier(v.astype(jnp.bfloat16)).astype(jnp.float32)

@jax.custom_vjp
def low_back(v):
    return v

def low_keep(v):
    return (low(v), None)

def low_pass(kept, grad):
    return (grad,)

def back_keep(v):
    return (v, None)

def back_low(kept, grad):
    return (low(grad),)
low.defvjp(low_keep, low_pass)
low_back.defvjp(back_keep, back_low)

def round_both(values):
    return low_back(low(values))

def matmul_hi(left_op, right_op):
    return jnp.dot(left_op, right_op, precision=lax.Precision.HIGHEST)

def einsum_hi(pattern, left_op, right_op):
    return jnp.einsum(pattern, left_op, right_op, precision=lax.Precision.HIGHEST)

def layer_norm(summed, gain_vec, bias_vec):
    centred = summed - lax.optimization_barrier(jnp.mean(summed, axis=-1, keepdims=True))
    variance = lax.optimization_barrier(jnp.mean(centred * centred, axis=-1, keepdims=True))
    return centred * lax.rsqrt(variance + 1e-05) * gain_vec + bias_vec

def pack_layer(params, token_rows, memory_rows, lengths):
    pack_query, pack_key, pack_value, pack_out, unpack_query, unpack_key, unpack_value, unpack_out, ffn_in, ffn_in_bias, ffn_out, ffn_out_bias, mem_gain, mem_bias, attn_gain, attn_bias, out_gain, out_bias = params
    score_scale = 1.0 / math.sqrt(HD)
    seq_ends = jnp.cumsum(lengths)
    tok_slot = lax.optimization_barrier(jnp.sum((seq_ends[None, :] <= jnp.arange(PACK, dtype=jnp.int32)[:, None]).astype(jnp.int32), axis=1))
    row_slot = jnp.arange(SLOTS * MEM, dtype=jnp.int32) // MEM
    row_mask = row_slot[:, None] == tok_slot[None, :]
    pack_q = round_both(matmul_hi(memory_rows, pack_query)).reshape(SLOTS * MEM, HEADS, HD)
    pack_k = round_both(matmul_hi(token_rows, pack_key)).reshape(PACK, HEADS, HD)
    pack_v = round_both(matmul_hi(token_rows, pack_value)).reshape(PACK, HEADS, HD)
    pack_scores = low_back(score_scale * einsum_hi('rhd,thd->hrt', pack_q, pack_k))
    pack_masked = jnp.where(row_mask[None], pack_scores, -1e+30)
    pack_top = lax.optimization_barrier(jnp.max(pack_masked, axis=2, keepdims=True))
    pack_weights = jnp.where(row_mask[None], jnp.exp(pack_masked - pack_top), 0.0)
    pack_den = lax.optimization_barrier(jnp.sum(pack_weights, axis=2))
    pack_num = low_back(einsum_hi('hrt,thd->rhd', low(pack_weights), pack_v))
    pack_ctx = low(pack_num / jnp.maximum(pack_den, 1.0).T[:, :, None])
    mem_mix = low_back(matmul_hi(pack_ctx.reshape(SLOTS * MEM, D), pack_out))
    mem_result = layer_norm(mem_mix + memory_rows, mem_gain, mem_bias)
    mix_low = low(mem_mix)
    unpack_k = round_both(matmul_hi(mix_low, unpack_key)).reshape(SLOTS * MEM, HEADS, HD)
    unpack_v = round_both(matmul_hi(mix_low, unpack_value)).reshape(SLOTS * MEM, HEADS, HD)
    unpack_q = round_both(matmul_hi(token_rows, unpack_query)).reshape(PACK, HEADS, HD)
    tok_scores = low_back(score_scale * einsum_hi('thd,rhd->htr', unpack_q, unpack_k))
    tok_masked = jnp.where(row_mask.T[None], tok_scores, -1e+30)
    tok_top = lax.optimization_barrier(jnp.max(tok_masked, axis=2, keepdims=True))
    tok_weights = jnp.where(row_mask.T[None], jnp.exp(tok_masked - tok_top), 0.0)
    tok_den = lax.optimization_barrier(jnp.sum(tok_weights, axis=2))
    tok_num = low_back(einsum_hi('htr,rhd->thd', low(tok_weights), unpack_v))
    tok_ctx = low(tok_num / tok_den.T[:, :, None])
    attn_mix = low_back(matmul_hi(tok_ctx.reshape(PACK, D), unpack_out))
    attn_res = layer_norm(attn_mix + token_rows, attn_gain, attn_bias)
    hidden = low_back(matmul_hi(low(attn_res), ffn_in) + ffn_in_bias)
    gelu_out = low(jax.nn.gelu(hidden, approximate=True))
    ffn_mix = low_back(matmul_hi(gelu_out, ffn_out) + ffn_out_bias)
    out_result = layer_norm(ffn_mix + attn_res, out_gain, out_bias)
    return (out_result, mem_result)

def reference(tokens, memory, seq_lengths, pack_query, pack_key, pack_value, pack_out, unpack_query, unpack_key, unpack_value, unpack_out, ffn_in, ffn_in_bias, ffn_out, ffn_out_bias, mem_gain, mem_bias, attn_gain, attn_bias, out_gain, out_bias, cot_tokens, cot_memory):
    params = tuple((weight.astype(jnp.float32) for weight in (pack_query, pack_key, pack_value, pack_out, unpack_query, unpack_key, unpack_value, unpack_out, ffn_in, ffn_in_bias, ffn_out, ffn_out_bias, mem_gain, mem_bias, attn_gain, attn_bias, out_gain, out_bias)))

    def forward(param_set, token_all, memory_all):
        pack_step = jax.checkpoint(pack_layer)
        return lax.map(lambda pack_item: pack_step(param_set, pack_item[0], pack_item[1], pack_item[2]), (token_all, memory_all, seq_lengths))
    outputs, pull_back = jax.vjp(forward, params, tokens.astype(jnp.float32), memory.astype(jnp.float32))
    param_grads, token_grad, memory_grad = pull_back((cot_tokens.astype(jnp.float32), cot_memory.astype(jnp.float32)))
    return (outputs[0].astype(jnp.bfloat16), outputs[1].astype(jnp.bfloat16), token_grad.astype(jnp.bfloat16), memory_grad.astype(jnp.bfloat16), param_grads[0], param_grads[1], param_grads[2], param_grads[3], param_grads[4], param_grads[5], param_grads[6], param_grads[7], param_grads[8], param_grads[9], param_grads[10], param_grads[11], param_grads[12], param_grads[13], param_grads[14], param_grads[15], param_grads[16], param_grads[17])
```

```python
import math

import jax
import jax.numpy as jnp
from jax import lax
from jax.sharding import PartitionSpec as P

HD = 64
MEM = 256
SLOTS = 4
EPSILON = 1e-05
NEG_FILL = -1e30
BF = jnp.bfloat16
F32 = jnp.float32


def norm_forward(summed, gain_vec, bias_vec):
    centre = summed - jnp.mean(summed, axis=-1, keepdims=True)
    inv_std = lax.rsqrt(jnp.mean(centre * centre, axis=-1, keepdims=True) + EPSILON)
    normed = centre * inv_std
    return (normed * gain_vec + bias_vec, normed, inv_std)


def norm_backward(upstream, normed, inv_std, gain_vec):
    scaled = upstream * gain_vec
    centred_grad = (
        scaled
        - jnp.mean(scaled, axis=-1, keepdims=True)
        - normed * jnp.mean(scaled * normed, axis=-1, keepdims=True)
    )
    return (inv_std * centred_grad, jnp.sum(upstream * normed, axis=0), jnp.sum(upstream, axis=0))


def mm(left, right):
    return jnp.dot(left, right, preferred_element_type=F32)


def mm_t(left, right):
    return lax.dot_general(left, right, (((1,), (1,)), ((), ())), preferred_element_type=F32)


def t_mm(left, right):
    return lax.dot_general(left, right, (((0,), (0,)), ((), ())), preferred_element_type=F32)


def ein(pattern, left, right):
    return jnp.einsum(pattern, left, right, preferred_element_type=F32)


def heads_of(values):
    return values.reshape(values.shape[0], -1, HD)


def flat(values):
    return values.reshape(values.shape[0], -1)


def wide(per_head):
    rows, heads = per_head.shape
    return jnp.broadcast_to(per_head[:, :, None], (rows, heads, HD)).reshape(rows, heads * HD)


def parts_of(value):
    first = lax.reduce_precision(value, 8, 7)
    rest = value - first
    second = lax.reduce_precision(rest, 8, 7)
    return [first.astype(BF), second.astype(BF), (rest - second).astype(BF)]


def joined(parts):
    heads = parts.shape[1] // 3
    wide_parts = parts.astype(F32)
    return (
        wide_parts[:, :heads]
        + wide_parts[:, heads : 2 * heads]
        + wide_parts[:, 2 * heads :]
    )


def make_local(axis_seq, axis_head):
    unit = axis_seq // SLOTS

    def swap(value, step):
        return lax.ppermute(value, "seq", [(i, i ^ step) for i in range(axis_seq)])

    def local(
        tokens,
        memory,
        seq_lengths,
        pack_query,
        pack_key,
        pack_value,
        pack_out,
        unpack_query,
        unpack_key,
        unpack_value,
        unpack_out,
        ffn_in,
        ffn_in_bias,
        ffn_out,
        ffn_out_bias,
        mem_gain,
        mem_bias,
        attn_gain,
        attn_bias,
        out_gain,
        out_bias,
        cot_tokens,
        cot_memory,
    ):
        seq_index = lax.axis_index("seq")
        head_index = lax.axis_index("head")
        block_len = tokens.shape[1]
        width = tokens.shape[2]
        heads = width // HD
        scale = 1.0 / math.sqrt(HD)
        my_unit, my_lane = seq_index // unit, seq_index % unit

        def mine(value):
            return lax.dynamic_index_in_dim(value, head_index, 0, keepdims=False)

        def seq_rows(value):
            size = value.shape[0] // axis_seq
            return lax.dynamic_slice_in_dim(value, seq_index * size, size, 0)

        columns = jnp.concatenate(
            [
                seq_rows(w)
                for w in (
                    pack_query,
                    pack_key,
                    pack_value,
                    unpack_query,
                    unpack_key,
                    unpack_value,
                )
            ],
            axis=1,
        )
        columns = lax.all_gather(columns, ("seq", "head"), axis=0)
        columns = columns.reshape(axis_seq, axis_head, -1, 6, width // axis_head)
        columns = columns.transpose(3, 0, 2, 1, 4).reshape(6, width, width)
        w_pq, w_pk, w_pv, w_uq, w_uk, w_uv = [columns[i] for i in range(6)]
        outs = jnp.stack([seq_rows(pack_out), seq_rows(unpack_out)])
        outs = lax.all_gather(outs, ("head", "seq"), axis=0)
        outs = outs.transpose(1, 0, 2, 3).reshape(2, width, width)
        w_po, w_uo = outs[0], outs[1]
        w_fi = lax.all_gather(seq_rows(ffn_in), ("head", "seq"), axis=0)
        w_fi = w_fi.reshape(axis_head, width, -1).transpose(1, 0, 2).reshape(width, -1)
        w_fo = lax.all_gather(seq_rows(ffn_out), ("head", "seq"), axis=0, tiled=True)
        b_fi = lax.all_gather(ffn_in_bias, "head", axis=0, tiled=True)

        tok = mine(tokens)
        mem = mine(memory)
        cot_tok = mine(cot_tokens).astype(F32)
        cot_mem = mine(cot_memory).astype(F32)
        tok_f32 = tok.astype(F32)
        mem_f32 = mem.astype(F32)
        seq_ends = jnp.cumsum(mine(seq_lengths))
        slot = jnp.sum((seq_ends <= seq_index * block_len).astype(jnp.int32))

        def gather_unit(value):
            step = 1
            while step < unit:
                other = swap(value, step)
                low = (my_lane // step) % 2 == 0
                value = jnp.concatenate(
                    [jnp.where(low, value, other), jnp.where(low, other, value)], axis=0
                )
                step *= 2
            return value

        def scatter_unit(value, add):
            step = unit // 2
            while step >= 1:
                half = value.shape[0] // 2
                low = (my_lane // step) % 2 == 0
                keep = jnp.where(low, value[:half], value[half:])
                send = jnp.where(low, value[half:], value[:half])
                value = add([keep, swap(send, step)])
                step //= 2
            return value

        def fetch(value):
            picked = value
            for j in range(1, SLOTS):
                other = swap(value, j * unit)
                picked = jnp.where(slot == (my_unit ^ j), other, picked)
            return gather_unit(picked)

        def deliver(value, empty, add):
            value = scatter_unit(value, add)
            got = [jnp.where(slot == my_unit, value, empty)]
            for j in range(1, SLOTS):
                got.append(swap(jnp.where(slot == (my_unit ^ j), value, empty), j * unit))
            return add(got)

        def sum_rows(values):
            total = values[0].astype(F32)
            for value in values[1:]:
                total = total + value.astype(F32)
            return total.astype(BF)

        lane_pad = -(heads * 3) % 128

        def with_scalars(rows, scalars):
            cols = [rows]
            for scalar in scalars:
                cols += parts_of(scalar)
            pad = -sum(c.shape[1] for c in cols[1:]) % 128
            cols.append(jnp.zeros((rows.shape[0], pad), BF))
            return jnp.concatenate(cols, axis=1)

        def scalars_in(packed, which):
            start = width + which * 3 * heads
            return joined(packed[:, start : start + 3 * heads])

        def blend(values):
            lses = [scalars_in(v, 0) for v in values]
            top = lses[0]
            for lse in lses[1:]:
                top = jnp.maximum(top, lse)
            shares = [jnp.exp(lse - top) for lse in lses]
            total = shares[0]
            for share in shares[1:]:
                total = total + share
            inv = 1.0 / total
            ctx = wide(shares[0] * inv) * values[0][:, :width].astype(F32)
            for share, value in zip(shares[1:], values[1:]):
                ctx = ctx + wide(share * inv) * value[:, :width].astype(F32)
            return with_scalars(ctx.astype(BF), [top + jnp.log(total)])

        mem_slot = fetch(mem)

        q_pack = mm(mem_slot, w_pq).astype(BF)
        k_pack = mm(tok, w_pk).astype(BF)
        v_pack = mm(tok, w_pv).astype(BF)

        def pack_scores():
            return ein("rhd,thd->hrt", heads_of(q_pack), heads_of(k_pack)) * scale

        scores = pack_scores()
        top = jnp.max(scores, axis=2, keepdims=True)
        weights = jnp.exp(scores - top)
        den = jnp.sum(weights, axis=2)
        num = flat(ein("hrt,thd->rhd", weights.astype(BF), heads_of(v_pack)))
        ctx_here = (num * wide(1.0 / den.T)).astype(BF)
        lse_here = (top[:, :, 0] + jnp.log(den)).T
        empty = jnp.concatenate(
            [
                jnp.zeros((1, width), BF),
                jnp.full((1, heads), NEG_FILL, BF),
                jnp.zeros((1, 2 * heads + lane_pad), BF),
            ],
            axis=1,
        )
        blended = deliver(with_scalars(ctx_here, [lse_here]), empty, blend)
        pack_ctx = blended[:, :width]
        pack_lse = scalars_in(blended, 0)
        mem_mix = mm(pack_ctx, w_po)
        mem_result, mem_normed, mem_inv = norm_forward(mem_mix + mem_f32, mem_gain, mem_bias)
        mix_low = mem_mix.astype(BF)
        mix_slot = fetch(mix_low)

        k_un = mm(mix_slot, w_uk).astype(BF)
        v_un = mm(mix_slot, w_uv).astype(BF)
        q_un = mm(tok, w_uq).astype(BF)
        tok_scores = ein("thd,rhd->htr", heads_of(q_un), heads_of(k_un)) * scale
        tok_top = jnp.max(tok_scores, axis=2, keepdims=True)
        tok_weights = jnp.exp(tok_scores - tok_top)
        tok_inv = (1.0 / jnp.sum(tok_weights, axis=2)).T
        tok_num = flat(ein("htr,rhd->thd", tok_weights.astype(BF), heads_of(v_un)))
        tok_ctx = tok_num * wide(tok_inv)
        tok_ctx_low = tok_ctx.astype(BF)
        attn_mix = mm(tok_ctx_low, w_uo)
        attn_result, attn_normed, attn_inv = norm_forward(attn_mix + tok_f32, attn_gain, attn_bias)

        attn_low = attn_result.astype(BF)
        hidden = mm(attn_low, w_fi) + b_fi
        gelu_out, gelu_pull = jax.vjp(lambda pre: jax.nn.gelu(pre, approximate=True), hidden)
        gelu_low = gelu_out.astype(BF)
        ffn_mix = mm(gelu_low, w_fo) + ffn_out_bias
        out_result, out_normed, out_inv = norm_forward(ffn_mix + attn_result, out_gain, out_bias)
        out_tokens = lax.all_gather(out_result.astype(BF), "head", axis=0)
        out_memory = lax.all_gather(mem_result.astype(BF), "head", axis=0)

        grad_sum, grad_out_gain, grad_out_bias = norm_backward(
            cot_tok, out_normed, out_inv, out_gain
        )
        ffn_grad = grad_sum.astype(BF)
        grad_ffn_out_bias = jnp.sum(ffn_grad.astype(F32), axis=0)
        grad_ffn_out = t_mm(gelu_low, ffn_grad).astype(BF)
        grad_hidden = gelu_pull(mm_t(ffn_grad, w_fo))[0].astype(BF)
        grad_ffn_in_bias = jnp.sum(grad_hidden.astype(F32), axis=0)
        grad_ffn_in = t_mm(attn_low, grad_hidden).astype(BF)
        grad_attn = grad_sum + mm_t(grad_hidden, w_fi)
        grad_mixsum, grad_attn_gain, grad_attn_bias = norm_backward(
            grad_attn, attn_normed, attn_inv, attn_gain
        )

        mix_grad = grad_mixsum.astype(BF)
        grad_unpack_out = t_mm(tok_ctx_low, mix_grad).astype(BF)
        ctx_grad = mm_t(mix_grad, w_uo)
        num_grad = (ctx_grad * wide(tok_inv)).astype(BF)
        den_grad = -tok_inv * jnp.sum(heads_of(ctx_grad * tok_ctx), axis=2)
        tok_dweights = ein("thd,rhd->htr", heads_of(num_grad), heads_of(v_un)) + den_grad.T[:, :, None]
        tok_dscores = (tok_weights * tok_dweights).astype(BF)
        uq_grad = flat(ein("htr,rhd->thd", tok_dscores, heads_of(k_un)) * scale).astype(BF)
        uk_part = flat(ein("htr,thd->rhd", tok_dscores, heads_of(q_un)) * scale).astype(BF)
        uv_part = flat(ein("htr,thd->rhd", tok_weights.astype(BF), heads_of(num_grad))).astype(BF)
        mix_part = (mm_t(uk_part, w_uk) + mm_t(uv_part, w_uv)).astype(BF)
        mix_total = deliver(mix_part, jnp.zeros((), BF), sum_rows)
        grad_unpack_query = t_mm(tok, uq_grad).astype(BF)
        grad_unpack_key = t_mm(mix_slot, uk_part).astype(BF)
        grad_unpack_value = t_mm(mix_slot, uv_part).astype(BF)

        grad_memsum, grad_mem_gain, grad_mem_bias = norm_backward(
            cot_mem, mem_normed, mem_inv, mem_gain
        )
        mem_mix_grad = (grad_memsum + mix_total.astype(F32)).astype(BF)
        grad_pack_out = t_mm(pack_ctx, mem_mix_grad).astype(BF)
        pctx_grad = mm_t(mem_mix_grad, w_po)
        delta = jnp.sum(heads_of(pctx_grad * pack_ctx.astype(F32)), axis=2)
        back = fetch(with_scalars(pctx_grad.astype(BF), [pack_lse, delta]))
        pctx_slot = back[:, :width]
        lse_slot = scalars_in(back, 0).T[:, :, None]
        delta_slot = scalars_in(back, 1).T[:, :, None]

        weights_back = jnp.exp(pack_scores() - lse_slot)
        dweights = ein("rhd,thd->hrt", heads_of(pctx_slot), heads_of(v_pack)) - delta_slot
        dscores = (weights_back * dweights).astype(BF)
        pq_part = flat(ein("hrt,thd->rhd", dscores, heads_of(k_pack)) * scale).astype(BF)
        pk_grad = flat(ein("hrt,rhd->thd", dscores, heads_of(q_pack)) * scale).astype(BF)
        pv_grad = flat(ein("hrt,rhd->thd", weights_back.astype(BF), heads_of(pctx_slot))).astype(BF)
        tok_part = mm_t(pk_grad, w_pk) + mm_t(pv_grad, w_pv) + mm_t(uq_grad, w_uq)
        grad_tokens = (tok_part + grad_mixsum).astype(BF)
        grad_tokens = lax.all_gather(grad_tokens, "head", axis=0)
        mem_part = deliver(mm_t(pq_part, w_pq).astype(BF), jnp.zeros((), BF), sum_rows)
        grad_memory = (mem_part.astype(F32) + grad_memsum).astype(BF)
        grad_memory = lax.all_gather(grad_memory, "head", axis=0)
        grad_pack_query = t_mm(mem_slot, pq_part).astype(BF)
        grad_pack_key = t_mm(tok, pk_grad).astype(BF)
        grad_pack_value = t_mm(tok, pv_grad).astype(BF)

        def scatter(value, axis, dim):
            return lax.psum_scatter(value, axis, scatter_dimension=dim, tiled=True)

        col_grads = jnp.stack(
            [
                grad_pack_query,
                grad_pack_key,
                grad_pack_value,
                grad_unpack_query,
                grad_unpack_key,
                grad_unpack_value,
            ]
        )
        col_grads = scatter(col_grads, "seq", 1)
        col_grads = col_grads.reshape(6, -1, axis_head, width // axis_head).transpose(2, 0, 1, 3)
        col_grads = scatter(col_grads, "head", 0)[0].astype(F32)
        out_grads = jnp.stack([grad_pack_out, grad_unpack_out]).reshape(2, axis_head, -1, width)
        out_grads = scatter(scatter(out_grads, "seq", 2), "head", 1)[:, 0].astype(F32)
        fi_grad = scatter(grad_ffn_in, "seq", 0).reshape(-1, axis_head, ffn_in.shape[1])
        fi_grad = scatter(fi_grad.transpose(1, 0, 2), "head", 0)[0].astype(F32)
        fo_grad = scatter(grad_ffn_out.reshape(axis_head, -1, width), "seq", 1)
        fo_grad = scatter(fo_grad, "head", 0)[0].astype(F32)

        small = jnp.concatenate(
            [
                grad_ffn_out_bias,
                grad_mem_gain,
                grad_mem_bias,
                grad_attn_gain,
                grad_attn_bias,
                grad_out_gain,
                grad_out_bias,
                grad_ffn_in_bias,
            ]
        ).reshape(-1, width)
        small = lax.psum(small, ("seq", "head"))
        share = width // axis_seq
        vectors = lax.dynamic_slice_in_dim(small[:7], seq_index * share, share, 1)
        fib = mine(small[7:].reshape(axis_head, -1))
        fib = lax.dynamic_slice_in_dim(fib, seq_index * share, share, 0)
        return (
            out_tokens,
            out_memory,
            grad_tokens,
            grad_memory,
            col_grads[0],
            col_grads[1],
            col_grads[2],
            out_grads[0],
            col_grads[3],
            col_grads[4],
            col_grads[5],
            out_grads[1],
            fi_grad,
            fib,
            fo_grad,
            vectors[0],
            vectors[1],
            vectors[2],
            vectors[3],
            vectors[4],
            vectors[5],
            vectors[6],
        )

    return local


def solution(mesh):
    rows = P(None, "seq", None)
    by_col, by_row, both = P(None, "head"), P("head", None), P("seq", "head")
    wide_rows = P(("head", "seq"), None)
    in_specs = (
        (rows, rows, P())
        + (by_col, by_col, by_col, by_row)
        + (by_col, by_col, by_col, by_row)
        + (by_col, P("head"), by_row)
        + (P(),) * 7
        + (rows, rows)
    )
    out_specs = (
        (rows,) * 4
        + (both, both, both, wide_rows)
        + (both, both, both, wide_rows)
        + (both, P(("head", "seq")), wide_rows)
        + (P("seq"),) * 7
    )
    local = make_local(mesh.shape["seq"], mesh.shape["head"])
    return jax.shard_map(local, mesh=mesh, in_specs=in_specs, out_specs=out_specs, check_vma=False)
```

```python
import math

import jax
import jax.numpy as jnp
from jax import lax
from jax.sharding import PartitionSpec as P

HD = 64
MEM = 256
SLOTS = 4
EPSILON = 1e-05
NEG_FILL = -1e30
BF = jnp.bfloat16
F32 = jnp.float32


def norm_forward(summed, gain_vec, bias_vec):
    centre = summed - jnp.mean(summed, axis=-1, keepdims=True)
    inv_std = lax.rsqrt(jnp.mean(centre * centre, axis=-1, keepdims=True) + EPSILON)
    normed = centre * inv_std
    return (normed * gain_vec + bias_vec, normed, inv_std)


def norm_backward(upstream, normed, inv_std, gain_vec):
    scaled = upstream * gain_vec
    centred_grad = (
        scaled
        - jnp.mean(scaled, axis=-1, keepdims=True)
        - normed * jnp.mean(scaled * normed, axis=-1, keepdims=True)
    )
    return (inv_std * centred_grad, jnp.sum(upstream * normed, axis=0), jnp.sum(upstream, axis=0))


def mm(left, right):
    return jnp.dot(left, right, preferred_element_type=F32)


def mm_t(left, right):
    return lax.dot_general(left, right, (((1,), (1,)), ((), ())), preferred_element_type=F32)


def t_mm(left, right):
    return lax.dot_general(left, right, (((0,), (0,)), ((), ())), preferred_element_type=F32)


def ein(pattern, left, right):
    return jnp.einsum(pattern, left, right, preferred_element_type=F32)


def heads_of(values):
    return values.reshape(values.shape[0], -1, HD)


def flat(values):
    return values.reshape(values.shape[0], -1)


def wide(per_head):
    rows, heads = per_head.shape
    return jnp.broadcast_to(per_head[:, :, None], (rows, heads, HD)).reshape(rows, heads * HD)


def parts_of(value):
    first = lax.reduce_precision(value, 8, 7)
    rest = value - first
    second = lax.reduce_precision(rest, 8, 7)
    return [first.astype(BF), second.astype(BF), (rest - second).astype(BF)]


def joined(parts):
    heads = parts.shape[1] // 3
    wide_parts = parts.astype(F32)
    return (
        wide_parts[:, :heads]
        + wide_parts[:, heads : 2 * heads]
        + wide_parts[:, 2 * heads :]
    )


def make_local(axis_seq, axis_head):
    unit = axis_seq // SLOTS

    def swap(value, step):
        return lax.ppermute(value, "seq", [(i, i ^ step) for i in range(axis_seq)])

    def local(
        tokens,
        memory,
        seq_lengths,
        pack_query,
        pack_key,
        pack_value,
        pack_out,
        unpack_query,
        unpack_key,
        unpack_value,
        unpack_out,
        ffn_in,
        ffn_in_bias,
        ffn_out,
        ffn_out_bias,
        mem_gain,
        mem_bias,
        attn_gain,
        attn_bias,
        out_gain,
        out_bias,
        cot_tokens,
        cot_memory,
    ):
        seq_index = lax.axis_index("seq")
        head_index = lax.axis_index("head")
        block_len = tokens.shape[1]
        width = tokens.shape[2]
        heads = width // HD
        scale = 1.0 / math.sqrt(HD)
        my_unit, my_lane = seq_index // unit, seq_index % unit

        def mine(value):
            return lax.dynamic_index_in_dim(value, head_index, 0, keepdims=False)

        def seq_rows(value):
            size = value.shape[0] // axis_seq
            return lax.dynamic_slice_in_dim(value, seq_index * size, size, 0)

        role = seq_index % 2
        quad = (seq_index // 2) % 4
        first_step = jnp.where(role == 0, 1, 2)
        second_step = 3 - first_step

        def cross(value, order):
            pairs = [(i, i ^ (2 * ((1, 2) if i % 2 == order else (2, 1))[0])) for i in range(axis_seq)]
            return lax.ppermute(value, "seq", pairs)

        def from_planes(value):
            got = [value]
            for j in range(1, axis_head):
                pairs = [(i, (i - j) % axis_head) for i in range(axis_head)]
                got.append(lax.ppermute(value, "head", pairs))
            stacked = jnp.stack(got)
            return jnp.roll(stacked, head_index, axis=0)

        def by_role(zero, one):
            return jnp.where(role == 0, zero, one)

        def quad_rows(value):
            size = value.shape[0] // 4
            return lax.dynamic_slice_in_dim(value, quad * size, size, 0)

        def spread_weights(piece):
            first = cross(piece, 0)
            second = cross(piece, 1)
            third = cross(first, 1)
            mine_set = [piece, first, second, third]
            steps = [0, first_step, second_step, 3]
            mats, rows, cols = piece.shape
            buffer = jnp.zeros((2, mats, 4, rows, cols), piece.dtype)
            for part, step in zip(mine_set, steps):
                buffer = lax.dynamic_update_slice(
                    buffer, part[None, :, None], (role, 0, quad ^ step, 0, 0)
                )
            for part, step in zip(mine_set, [0, second_step, first_step, 3]):
                buffer = lax.dynamic_update_slice(
                    buffer, swap(part, 1)[None, :, None], (1 - role, 0, quad ^ step, 0, 0)
                )
            return buffer.reshape(2, mats, 4 * rows, cols)

        def attention_piece(key_w, value_w, query_w, out_w):
            size = out_w.shape[1] // 4
            out_t = lax.dynamic_slice_in_dim(out_w, quad * size, size, 1).T
            zero = jnp.concatenate([quad_rows(key_w), quad_rows(value_w)], axis=1)
            one = jnp.concatenate([quad_rows(query_w), out_t], axis=1)
            planes = from_planes(by_role(zero, one))
            rows = planes.shape[1]
            planes = planes.reshape(axis_head, rows, 2, -1)
            return planes.transpose(2, 1, 0, 3).reshape(2, rows, -1)

        w_pack = spread_weights(attention_piece(pack_key, pack_value, pack_query, pack_out))
        w_un = spread_weights(attention_piece(unpack_key, unpack_value, unpack_query, unpack_out))
        bias_rows = jnp.stack(parts_of(ffn_in_bias) + [jnp.zeros(ffn_in_bias.shape, BF)] * 13)
        ffn_piece = by_role(quad_rows(ffn_in), quad_rows(ffn_out))
        ffn_piece = from_planes(jnp.concatenate([ffn_piece, bias_rows]))
        split = ffn_piece.shape[1] - 16
        bias_all = ffn_piece[:, split : split + 3].astype(F32)
        b_fi = (bias_all[:, 0] + bias_all[:, 1] + bias_all[:, 2]).reshape(-1)
        w_ffn = spread_weights(ffn_piece[:, :split])
        w_pk, w_pv, w_pq, w_po = w_pack[0, 0], w_pack[0, 1], w_pack[1, 0], w_pack[1, 1]
        w_uk, w_uv, w_uq, w_uo = w_un[0, 0], w_un[0, 1], w_un[1, 0], w_un[1, 1]
        w_fi = w_ffn[0].transpose(1, 0, 2).reshape(width, -1)
        w_fo = w_ffn[1].reshape(-1, width)

        tok = mine(tokens)
        mem = mine(memory)
        cot_tok = mine(cot_tokens).astype(F32)
        cot_mem = mine(cot_memory).astype(F32)
        tok_f32 = tok.astype(F32)
        mem_f32 = mem.astype(F32)
        seq_ends = jnp.cumsum(mine(seq_lengths))
        slot = jnp.sum((seq_ends <= seq_index * block_len).astype(jnp.int32))

        def gather_unit(value):
            step = 1
            while step < unit:
                other = swap(value, step)
                low = (my_lane // step) % 2 == 0
                value = jnp.concatenate(
                    [jnp.where(low, value, other), jnp.where(low, other, value)], axis=0
                )
                step *= 2
            return value

        def scatter_unit(value, add):
            step = unit // 2
            while step >= 1:
                half = value.shape[0] // 2
                low = (my_lane // step) % 2 == 0
                keep = jnp.where(low, value[:half], value[half:])
                send = jnp.where(low, value[half:], value[:half])
                value = add([keep, swap(send, step)])
                step //= 2
            return value

        def fetch(value):
            picked = value
            for j in range(1, SLOTS):
                other = swap(value, j * unit)
                picked = jnp.where(slot == (my_unit ^ j), other, picked)
            return gather_unit(picked)

        def deliver(value, empty, add):
            value = scatter_unit(value, add)
            got = [jnp.where(slot == my_unit, value, empty)]
            for j in range(1, SLOTS):
                got.append(swap(jnp.where(slot == (my_unit ^ j), value, empty), j * unit))
            return add(got)

        def sum_rows(values):
            total = values[0].astype(F32)
            for value in values[1:]:
                total = total + value.astype(F32)
            return total.astype(BF)

        lane_pad = -(heads * 3) % 128

        def with_scalars(rows, scalars):
            cols = [rows]
            for scalar in scalars:
                cols += parts_of(scalar)
            pad = -sum(c.shape[1] for c in cols[1:]) % 128
            cols.append(jnp.zeros((rows.shape[0], pad), BF))
            return jnp.concatenate(cols, axis=1)

        def scalars_in(packed, which):
            start = width + which * 3 * heads
            return joined(packed[:, start : start + 3 * heads])

        def blend(values):
            lses = [scalars_in(v, 0) for v in values]
            top = lses[0]
            for lse in lses[1:]:
                top = jnp.maximum(top, lse)
            shares = [jnp.exp(lse - top) for lse in lses]
            total = shares[0]
            for share in shares[1:]:
                total = total + share
            inv = 1.0 / total
            ctx = wide(shares[0] * inv) * values[0][:, :width].astype(F32)
            for share, value in zip(shares[1:], values[1:]):
                ctx = ctx + wide(share * inv) * value[:, :width].astype(F32)
            return with_scalars(ctx.astype(BF), [top + jnp.log(total)])

        mem_slot = fetch(mem)

        q_pack = mm(mem_slot, w_pq).astype(BF)
        k_pack = mm(tok, w_pk).astype(BF)
        v_pack = mm(tok, w_pv).astype(BF)

        def pack_scores():
            return ein("rhd,thd->hrt", heads_of(q_pack), heads_of(k_pack)) * scale

        scores = pack_scores()
        top = jnp.max(scores, axis=2, keepdims=True)
        weights = jnp.exp(scores - top)
        den = jnp.sum(weights, axis=2)
        num = flat(ein("hrt,thd->rhd", weights.astype(BF), heads_of(v_pack)))
        ctx_here = (num * wide(1.0 / den.T)).astype(BF)
        lse_here = (top[:, :, 0] + jnp.log(den)).T
        empty = jnp.concatenate(
            [
                jnp.zeros((1, width), BF),
                jnp.full((1, heads), NEG_FILL, BF),
                jnp.zeros((1, 2 * heads + lane_pad), BF),
            ],
            axis=1,
        )
        blended = deliver(with_scalars(ctx_here, [lse_here]), empty, blend)
        pack_ctx = blended[:, :width]
        pack_lse = scalars_in(blended, 0)
        mem_mix = mm_t(pack_ctx, w_po)
        mem_result, mem_normed, mem_inv = norm_forward(mem_mix + mem_f32, mem_gain, mem_bias)
        mix_low = mem_mix.astype(BF)
        mix_slot = fetch(mix_low)

        k_un = mm(mix_slot, w_uk).astype(BF)
        v_un = mm(mix_slot, w_uv).astype(BF)
        q_un = mm(tok, w_uq).astype(BF)
        tok_scores = ein("thd,rhd->htr", heads_of(q_un), heads_of(k_un)) * scale
        tok_top = jnp.max(tok_scores, axis=2, keepdims=True)
        tok_weights = jnp.exp(tok_scores - tok_top)
        tok_inv = (1.0 / jnp.sum(tok_weights, axis=2)).T
        tok_num = flat(ein("htr,rhd->thd", tok_weights.astype(BF), heads_of(v_un)))
        tok_ctx = tok_num * wide(tok_inv)
        tok_ctx_low = tok_ctx.astype(BF)
        attn_mix = mm_t(tok_ctx_low, w_uo)
        attn_result, attn_normed, attn_inv = norm_forward(attn_mix + tok_f32, attn_gain, attn_bias)

        attn_low = attn_result.astype(BF)
        hidden = mm(attn_low, w_fi) + b_fi
        gelu_out, gelu_pull = jax.vjp(lambda pre: jax.nn.gelu(pre, approximate=True), hidden)
        gelu_low = gelu_out.astype(BF)
        ffn_mix = mm(gelu_low, w_fo) + ffn_out_bias
        out_result, out_normed, out_inv = norm_forward(ffn_mix + attn_result, out_gain, out_bias)
        outs = jnp.concatenate([out_result.astype(BF), mem_result.astype(BF)])
        outs = lax.all_gather(outs, "head", axis=0)
        out_tokens, out_memory = outs[:, :block_len], outs[:, block_len:]

        grad_sum, grad_out_gain, grad_out_bias = norm_backward(
            cot_tok, out_normed, out_inv, out_gain
        )
        ffn_grad = grad_sum.astype(BF)
        grad_ffn_out_bias = jnp.sum(ffn_grad.astype(F32), axis=0)
        grad_ffn_out = t_mm(gelu_low, ffn_grad).astype(BF)
        grad_hidden = gelu_pull(mm_t(ffn_grad, w_fo))[0].astype(BF)
        grad_ffn_in_bias = jnp.sum(grad_hidden.astype(F32), axis=0)
        grad_ffn_in = t_mm(attn_low, grad_hidden).astype(BF)
        grad_attn = grad_sum + mm_t(grad_hidden, w_fi)
        grad_mixsum, grad_attn_gain, grad_attn_bias = norm_backward(
            grad_attn, attn_normed, attn_inv, attn_gain
        )

        mix_grad = grad_mixsum.astype(BF)
        grad_unpack_out = t_mm(tok_ctx_low, mix_grad).astype(BF)
        ctx_grad = mm(mix_grad, w_uo)
        num_grad = (ctx_grad * wide(tok_inv)).astype(BF)
        den_grad = -tok_inv * jnp.sum(heads_of(ctx_grad * tok_ctx), axis=2)
        tok_dweights = ein("thd,rhd->htr", heads_of(num_grad), heads_of(v_un)) + den_grad.T[:, :, None]
        tok_dscores = (tok_weights * tok_dweights).astype(BF)
        uq_grad = flat(ein("htr,rhd->thd", tok_dscores, heads_of(k_un)) * scale).astype(BF)
        uk_part = flat(ein("htr,thd->rhd", tok_dscores, heads_of(q_un)) * scale).astype(BF)
        uv_part = flat(ein("htr,thd->rhd", tok_weights.astype(BF), heads_of(num_grad))).astype(BF)
        mix_part = (mm_t(uk_part, w_uk) + mm_t(uv_part, w_uv)).astype(BF)
        mix_total = deliver(mix_part, jnp.zeros((), BF), sum_rows)
        grad_unpack_query = t_mm(tok, uq_grad).astype(BF)
        grad_unpack_key = t_mm(mix_slot, uk_part).astype(BF)
        grad_unpack_value = t_mm(mix_slot, uv_part).astype(BF)

        grad_memsum, grad_mem_gain, grad_mem_bias = norm_backward(
            cot_mem, mem_normed, mem_inv, mem_gain
        )
        mem_mix_grad = (grad_memsum + mix_total.astype(F32)).astype(BF)
        grad_pack_out = t_mm(pack_ctx, mem_mix_grad).astype(BF)
        pctx_grad = mm(mem_mix_grad, w_po)
        delta = jnp.sum(heads_of(pctx_grad * pack_ctx.astype(F32)), axis=2)
        back = fetch(with_scalars(pctx_grad.astype(BF), [pack_lse, delta]))
        pctx_slot = back[:, :width]
        lse_slot = scalars_in(back, 0).T[:, :, None]
        delta_slot = scalars_in(back, 1).T[:, :, None]

        weights_back = jnp.exp(pack_scores() - lse_slot)
        dweights = ein("rhd,thd->hrt", heads_of(pctx_slot), heads_of(v_pack)) - delta_slot
        dscores = (weights_back * dweights).astype(BF)
        pq_part = flat(ein("hrt,thd->rhd", dscores, heads_of(k_pack)) * scale).astype(BF)
        pk_grad = flat(ein("hrt,rhd->thd", dscores, heads_of(q_pack)) * scale).astype(BF)
        pv_grad = flat(ein("hrt,rhd->thd", weights_back.astype(BF), heads_of(pctx_slot))).astype(BF)
        tok_part = mm_t(pk_grad, w_pk) + mm_t(pv_grad, w_pv) + mm_t(uq_grad, w_uq)
        grad_tokens = (tok_part + grad_mixsum).astype(BF)
        mem_part = deliver(mm_t(pq_part, w_pq).astype(BF), jnp.zeros((), BF), sum_rows)
        grad_memory = (mem_part.astype(F32) + grad_memsum).astype(BF)
        grads = jnp.concatenate([grad_tokens, grad_memory])
        grads = lax.all_gather(grads, "head", axis=0)
        grad_tokens, grad_memory = grads[:, :block_len], grads[:, block_len:]
        grad_pack_query = t_mm(mem_slot, pq_part).astype(BF)
        grad_pack_key = t_mm(tok, pk_grad).astype(BF)
        grad_pack_value = t_mm(tok, pv_grad).astype(BF)

        def pick(value, index):
            return lax.dynamic_index_in_dim(value, index, 0, keepdims=False)

        def plane_sum(grads):
            keep, send = pick(grads, role), pick(grads, 1 - role)
            total = sum_rows([keep, swap(send, 1)])
            mats, rows, cols = total.shape
            blocks = total.reshape(mats, 4, rows // 4, cols).transpose(1, 0, 2, 3)
            low, high = quad % 2, quad // 2

            def pair(bit):
                zero = by_role(bit, 2 * bit)
                one = by_role(2 + bit, 2 * bit + 1)
                return jnp.stack([pick(blocks, zero), pick(blocks, one)])

            bit = by_role(low, high)
            blocks = sum_rows([pair(bit), cross(pair(1 - bit), 0)])
            bit = by_role(high, low)
            return sum_rows([pick(blocks, bit), cross(pick(blocks, 1 - bit), 1)])

        def head_sum(blocks):
            total = mine(blocks).astype(F32)
            for j in range(1, axis_head):
                pairs = [(i, (i + j) % axis_head) for i in range(axis_head)]
                block = pick(blocks, (head_index + j) % axis_head)
                total = total + lax.ppermute(block, "head", pairs).astype(F32)
            return total

        def own_rows(total):
            half = total.shape[1] // 2
            keep = lax.dynamic_slice_in_dim(total, role * half, half, 1)
            send = lax.dynamic_slice_in_dim(total, (1 - role) * half, half, 1)
            other = swap(send, 1)
            return by_role(keep, other), by_role(other, keep)

        head_cols = width // axis_head

        groups = axis_seq // 8
        peers = [[g * 8 + low for g in range(groups)] for low in range(8)]

        def group_sum(value):
            if groups == 1:
                return value[0]
            return lax.psum_scatter(
                value, "seq", scatter_dimension=0, tiled=False, axis_index_groups=peers
            )

        def out_rows(grad):
            blocks = grad.reshape(axis_head, groups * 4, -1, width)
            return blocks.transpose(1, 0, 2, 3).reshape(width, width)

        def attention_grads(key_g, value_g, query_g, out_g):
            grads = jnp.stack([key_g, value_g, query_g, out_rows(out_g)])
            grads = grads.reshape(2, 2, groups, -1, width).transpose(2, 0, 1, 3, 4)
            total = plane_sum(group_sum(grads))
            rows = total.shape[1]
            by_cols = total.reshape(2, rows, axis_head, head_cols).transpose(2, 0, 1, 3)
            as_rows = total[1].reshape(axis_head, rows, head_cols)
            second = by_role(by_cols[:, 1], as_rows)
            total = head_sum(jnp.stack([by_cols[:, 0], second], axis=1))
            zero, one = own_rows(total)
            return zero[0], zero[1], one[0], one[1].reshape(-1, width)

        un_grads = attention_grads(
            grad_unpack_key, grad_unpack_value, grad_unpack_query, grad_unpack_out
        )
        pack_grads = attention_grads(grad_pack_key, grad_pack_value, grad_pack_query, grad_pack_out)
        fi_blocks = grad_ffn_in.reshape(width, axis_head, -1).transpose(1, 0, 2)
        fo_blocks = grad_ffn_out.reshape(axis_head, -1, width)
        ffn_blocks = jnp.stack([fi_blocks, fo_blocks])
        ffn_blocks = ffn_blocks.reshape(2, axis_head, groups, -1, ffn_in.shape[1])
        ffn_total = head_sum(plane_sum(group_sum(ffn_blocks.transpose(2, 0, 1, 3, 4))))
        fi_grad, fo_grad = own_rows(ffn_total[None])
        fi_grad, fo_grad = fi_grad[0], fo_grad[0]
        small = jnp.concatenate(
            [
                grad_ffn_out_bias,
                grad_mem_gain,
                grad_mem_bias,
                grad_attn_gain,
                grad_attn_bias,
                grad_out_gain,
                grad_out_bias,
                grad_ffn_in_bias,
            ]
        ).reshape(-1, width)
        step = 1
        while step < axis_seq:
            small = small + swap(small, step)
            step *= 2
        vector_total = small
        for j in range(1, axis_head):
            pairs = [(i, (i + j) % axis_head) for i in range(axis_head)]
            vector_total = vector_total + lax.ppermute(small, "head", pairs)
        small = vector_total
        share = width // axis_seq
        vectors = lax.dynamic_slice_in_dim(small[:7], seq_index * share, share, 1)
        fib = mine(small[7:].reshape(axis_head, -1))
        fib = lax.dynamic_slice_in_dim(fib, seq_index * share, share, 0)
        return (
            out_tokens,
            out_memory,
            grad_tokens,
            grad_memory,
            pack_grads[2],
            pack_grads[0],
            pack_grads[1],
            pack_grads[3],
            un_grads[2],
            un_grads[0],
            un_grads[1],
            un_grads[3],
            fi_grad,
            fib,
            fo_grad,
            vectors[0],
            vectors[1],
            vectors[2],
            vectors[3],
            vectors[4],
            vectors[5],
            vectors[6],
        )

    return local


def solution(mesh):
    rows = P(None, "seq", None)
    by_col, by_row, both = P(None, "head"), P("head", None), P("seq", "head")
    wide_rows = P(("head", "seq"), None)
    in_specs = (
        (rows, rows, P())
        + (by_col, by_col, by_col, by_row)
        + (by_col, by_col, by_col, by_row)
        + (by_col, P("head"), by_row)
        + (P(),) * 7
        + (rows, rows)
    )
    out_specs = (
        (rows,) * 4
        + (both, both, both, wide_rows)
        + (both, both, both, wide_rows)
        + (both, P(("head", "seq")), wide_rows)
        + (P("seq"),) * 7
    )
    local = make_local(mesh.shape["seq"], mesh.shape["head"])
    return jax.shard_map(local, mesh=mesh, in_specs=in_specs, out_specs=out_specs, check_vma=False)
```

```python
import functools
import math

import jax
import jax.numpy as jnp
import numpy as np
from jax import lax
from jax.experimental import pallas as pl
from jax.experimental.pallas import tpu as pltpu
from jax.sharding import PartitionSpec as P

HD = 64
SLOTS = 4
EPSILON = 1e-05
NEG_FILL = -1e30
BF = jnp.bfloat16
F32 = jnp.float32


def dot(left, right):
    return jnp.dot(left, right, preferred_element_type=F32)


def dot_nt(left, right):
    return lax.dot_general(left, right, (((1,), (1,)), ((), ())), preferred_element_type=F32)


def dot_tn(left, right):
    return lax.dot_general(left, right, (((0,), (0,)), ((), ())), preferred_element_type=F32)


TILE = 2 * HD
PARTS = 3
MIB = 1024 * 1024
SMALL = pl.CostEstimate(flops=1, bytes_accessed=1, transcendentals=0)


ROLE, WALK, OTHER_WALK, PLANE, SLOT, UNIT, HALF, BIT, OTHER_BIT, INFO = 0, 1, 5, 9, 10, 11, 12, 13, 14, 16


def call(kernel, name, operands, outs, anys=0, scratch=(), flops=0, vmem=None, out_any=0, after=(), smem=1):
    def body(*refs):
        kernel(*refs[: len(operands)], *refs[len(operands) + len(after) :])

    if vmem is None:
        vmem = 60 if anys or name == "attention_weight_grad" else 16
    vm, anywhere = pl.BlockSpec(memory_space=pltpu.VMEM), pl.BlockSpec(memory_space=pl.ANY)
    specs = [pl.BlockSpec(memory_space=pltpu.SMEM)] * smem
    specs += [vm] * (len(operands) - smem - anys) + [anywhere] * (anys + len(after))
    return pl.pallas_call(
        body,
        out_shape=[jax.ShapeDtypeStruct(s, d) for s, d in outs],
        in_specs=specs,
        out_specs=[vm] * (len(outs) - out_any) + [anywhere] * out_any,
        scratch_shapes=list(scratch),
        compiler_params=pltpu.CompilerParams(vmem_limit_bytes=vmem * MIB),
        cost_estimate=SMALL,
        name=name,
    )(*operands, *after)


def info_kernel(places, lengths, info, unit, block_len):
    seq, head = places[0], places[1]
    role, quad = lax.rem(seq, 2), lax.rem(seq // 2, 4)
    first, second = 1 + role, 2 - role
    info[ROLE] = role
    for at, step in enumerate((0, first, second, 3)):
        info[WALK + at] = quad ^ step
    for at, step in enumerate((0, second, first, 3)):
        info[OTHER_WALK + at] = quad ^ step
    info[PLANE] = head
    end = 0
    slot = 0
    for at in range(SLOTS):
        end = end + lengths[head, at]
        slot = slot + (end <= seq * block_len).astype(jnp.int32)
    info[SLOT] = slot
    info[UNIT] = seq // unit
    info[HALF] = lax.rem(seq, unit) // (unit // 2)
    info[BIT] = jnp.where(role == 0, lax.rem(quad, 2), quad // 2)
    info[OTHER_BIT] = jnp.where(role == 0, quad // 2, lax.rem(quad, 2))
    info[INFO - 1] = 0


def planes_kernel(info, first, second, third, fourth, *outs):
    for at, ref in enumerate((first, second, third, fourth)):
        for mat in range(4):
            out = outs[mat // 2]
            out[mat % 2, info[PLANE] ^ at] = ref[mat]


def first_pieces_kernel(places, lengths, memory, *refs, unit, block_len):
    weights, (info, piece, mem, sems) = refs[:8], refs[8:]
    info_kernel(places, lengths, info, unit, block_len)
    copy_mem = pltpu.make_async_copy(memory.at[places[1]], mem, sems.at[4])
    copy_mem.start()
    rows = piece.shape[1]
    at = pl.ds(pl.multiple_of(info[WALK] * rows, rows), rows)
    for role, chosen in enumerate(((0, 1, 4, 5), (2, 3, 6, 7))):

        @pl.when(info[ROLE] == role)
        def _(chosen=chosen):
            copies = [
                pltpu.make_async_copy(weights[which].at[at], piece.at[mat], sems.at[mat])
                for mat, which in enumerate(chosen)
            ]
            for copy in copies:
                copy.start()
            for copy in copies:
                copy.wait()

    copy_mem.wait()


def other_pieces_kernel(info, bias, *refs):
    ffn_in, ffn_out, tokens, cot_tok, cot_mem = refs[:5]
    ffn, tok, cot_t, cot_m, sems = refs[5:]
    plane = info[PLANE]
    copies = []
    for at, (source, to) in enumerate(((tokens, tok), (cot_tok, cot_t), (cot_mem, cot_m))):
        copies.append(pltpu.make_async_copy(source.at[plane], to, sems.at[2 + at]))
    for copy in copies:
        copy.start()
    rows = ffn.shape[0] - 16
    for role, source in enumerate((ffn_in, ffn_out)):

        @pl.when(info[ROLE] == role)
        def _(source=source):
            copy = pltpu.make_async_copy(source, ffn.at[pl.ds(0, rows)], sems.at[5])
            copy.start()
            copy.wait()

    value = bias[...][None]
    parts = []
    for part in range(PARTS):
        low = value.astype(BF).astype(F32)
        parts.append(low)
        value = value - low
    parts.append(jnp.zeros((16 - PARTS, bias.shape[0]), F32))
    ffn[rows:] = jnp.concatenate(parts, axis=0).astype(BF)
    for copy in copies:
        copy.wait()


def vectors_kernel(info, mem_vectors, out_vectors, attn_vectors, hid_vec, out):
    out[...] = jnp.zeros(out.shape, F32)
    out[0:1] = out_vectors[0:1]
    out[1:3] = mem_vectors[0:2]
    out[3:5] = attn_vectors[0:2]
    out[5:7] = out_vectors[1:3]
    for plane in range(hid_vec.shape[0]):
        out[7 + plane : 8 + plane] = hid_vec[plane]


def total_kernel(info, *refs):
    total = refs[0][...]
    for ref in refs[1:-1]:
        total = total + ref[...]
    refs[-1][...] = total


def plane_vectors_kernel(info, first, second, third, fourth, out, held):
    planes = held.shape[0]
    for at, ref in enumerate((first, second, third, fourth)):
        held[info[PLANE] ^ at] = ref[...]
    total = held[0]
    for plane in range(1, planes):
        total = total + held[plane]
    out[...] = total


def memory_total_kernel(info, base, first, second, third, fourth, out):
    total = base[...]
    for ref in (first, second, third, fourth):
        total = total + ref[...].astype(F32)
    out[...] = total.astype(BF)


def pick_kernel(info, first, second, third, fourth, out):
    for at, ref in enumerate((first, second, third, fourth)):

        @pl.when(info[SLOT] == (info[UNIT] ^ at))
        def _(ref=ref):
            out[...] = ref[...]


def tie(value, *after):
    anywhere = pl.BlockSpec(memory_space=pl.ANY)
    return pl.pallas_call(
        lambda *refs: None,
        out_shape=jax.ShapeDtypeStruct(value.shape, value.dtype),
        in_specs=[anywhere] * (1 + len(after)),
        out_specs=anywhere,
        input_output_aliases={0: 0},
        compiler_params=pltpu.CompilerParams(vmem_limit_bytes=16 * MIB),
        cost_estimate=SMALL,
        name="tie",
    )(value, *after)


def stack_kernel(info, first, second, third, fourth, out):
    for at, ref in enumerate((first, second, third, fourth)):
        out[info[PLANE] ^ at] = ref[...]


def put_halves(info, keep, send, value):
    size = keep.shape[0]

    @pl.when(info[HALF] == 0)
    def _():
        keep[...] = value[:size]
        send[...] = value[size:]

    @pl.when(info[HALF] == 1)
    def _():
        keep[...] = value[size:]
        send[...] = value[:size]


def put_slots(info, outs, value, empty):
    for at, out in enumerate(outs):
        here = info[SLOT] == (info[UNIT] ^ at)

        @pl.when(here)
        def _(out=out):
            out[...] = value

        @pl.when(jnp.logical_not(here))
        def _(out=out):
            out[...] = empty


def blend_values(given, sel, width):
    lses = [dot(c[:, width:], sel[0]) for c in given]
    top = lses[0]
    for lse in lses[1:]:
        top = jnp.maximum(top, lse)
    shares = [jnp.exp(lse - top) for lse in lses]
    total = shares[0]
    for share in shares[1:]:
        total = total + share
    inv = 1.0 / total
    low = lax.broadcasted_iota(jnp.int32, (1, TILE), 1) < HD
    tiles = []
    for pair in range(width // TILE):
        cols = slice(pair * TILE, (pair + 1) * TILE)
        ctx = None
        for share, c in zip(shares, given):
            share = share * inv
            weight = jnp.where(
                low, share[:, 2 * pair : 2 * pair + 1], share[:, 2 * pair + 1 : 2 * pair + 2]
            )
            term = weight * c[:, cols].astype(F32)
            ctx = term if ctx is None else ctx + term
        tiles.append(ctx.astype(BF))
    return tiles, top + jnp.log(total)


def blend_kernel(info, keep, got, sel, *outs):
    outs, value = outs[:SLOTS], outs[SLOTS]
    width = value.shape[1] - TILE
    heads = width // HD
    tiles, lse = blend_values((keep, got), sel, width)
    for pair, tile in enumerate(tiles):
        value[:, pair * TILE : (pair + 1) * TILE] = tile
    value[:, width:] = as_parts(lse, heads).astype(BF)
    col = lax.broadcasted_iota(jnp.int32, value.shape, 1)
    fill = jnp.where((col >= width) & (col < width + heads), NEG_FILL, 0.0)
    put_slots(info, outs, value[...], fill.astype(BF))


def sum_kernel(info, keep, got, *outs):
    total = (keep[...].astype(F32) + got[...].astype(F32)).astype(BF)
    put_slots(info, outs, total, jnp.zeros(total.shape, BF))


def start_weights(info, pieces, held, sems, mats=(0, 1)):
    planes = held.shape[2]
    for mat in mats:
        for j in range(4):
            mine = (info[ROLE], info[WALK + j], pieces[j])
            theirs = (1 - info[ROLE], info[OTHER_WALK + j], pieces[4 + j])
            for role, unit, piece in (mine, theirs):
                for plane in range(planes):
                    pltpu.make_async_copy(
                        piece.at[mat, plane],
                        held.at[role, mat, plane, unit],
                        sems.at[role, mat, j * planes + plane],
                    ).start()


def weight(held, sems, pieces, role, mat):
    planes = held.shape[2]
    for j in range(4):
        for plane in range(planes):
            pltpu.make_async_copy(
                pieces[j].at[mat, plane],
                held.at[role, mat, plane, j],
                sems.at[role, mat, j * planes + plane],
            ).wait()
    return matrix(held, role, mat)


def matrix(held, *index):
    block = held[index]
    return block.reshape(-1, block.shape[-1])


def half_masks():
    lane = lax.broadcasted_iota(jnp.int32, (1, TILE), 1)
    low = (lane < HD).astype(F32).astype(BF)
    return low, (lane >= HD).astype(F32).astype(BF)


def put_scalars(rows):
    count = len(rows)
    stack = jnp.concatenate(rows * PARTS, axis=0)
    extra = TILE - stack.shape[0]
    stack = jnp.concatenate([stack, jnp.zeros((extra, stack.shape[1]), F32)], axis=0)
    return stack.T


def as_parts(wide, heads, offset=0):
    first = wide.astype(BF).astype(F32)
    rest = wide - first
    second = rest.astype(BF).astype(F32)
    third = rest - second
    lane = lax.broadcasted_iota(jnp.int32, wide.shape, 1) - offset
    return jnp.where(
        lane < 0,
        0.0,
        jnp.where(
            lane < heads,
            first,
            jnp.where(lane < 2 * heads, second, jnp.where(lane < 3 * heads, third, 0.0)),
        ),
    )


def norm_stats(summed):
    centre = summed - jnp.mean(summed, axis=-1, keepdims=True)
    inv = lax.rsqrt(jnp.mean(centre * centre, axis=-1, keepdims=True) + EPSILON)
    return centre * inv, inv


def norm_pull(upstream, normed, inv, gain):
    scaled = upstream * gain
    return inv * (
        scaled
        - jnp.mean(scaled, axis=-1, keepdims=True)
        - normed * jnp.mean(scaled * normed, axis=-1, keepdims=True)
    )


def head_forward(q_tile, k_tile, v_tile, masks):
    parts, rows = [], []
    for side in range(2):
        scores = dot_nt(k_tile * masks[side], q_tile)
        top = jnp.max(scores, axis=0, keepdims=True)
        weights = jnp.exp(scores - top)
        den = jnp.sum(weights, axis=0, keepdims=True)
        num = dot_tn(v_tile, weights.astype(BF))[side * HD : (side + 1) * HD]
        parts.append(num * (1.0 / den))
        rows.append(top + jnp.log(den))
    return jnp.concatenate(parts, axis=0), rows


def head_backward(q_tile, k_tile, v_tile, g_tile, lses, deltas, masks):
    dq, dk, dv = [], None, None
    for side in range(2):
        q_side, g_side = q_tile * masks[side], g_tile * masks[side]
        weights = jnp.exp(dot_nt(k_tile, q_side) - lses[side])
        dscores = (weights * (dot_nt(v_tile, g_side) - deltas[side])).astype(BF)
        weights = weights.astype(BF)
        dq.append(dot_tn(k_tile, dscores)[side * HD : (side + 1) * HD])
        dk_side, dv_side = dot(dscores, q_side), dot(weights, g_side)
        dk = dk_side if dk is None else dk + dk_side
        dv = dv_side if dv is None else dv + dv_side
    return jnp.concatenate(dq, axis=0), dk, dv


def pack_forward_kernel(
    info, tok, mem, *refs
):
    pieces, (k_out, v_out, q_out, keep, send, packed, held, sems) = refs[:8], refs[8:]
    width = tok.shape[1]
    heads = width // HD
    start_weights(info, pieces, held, sems)
    k_out[...] = dot_nt(tok[...], weight(held, sems, pieces, 0, 0)).astype(BF)
    v_out[...] = dot_nt(tok[...], weight(held, sems, pieces, 0, 1)).astype(BF)
    q_out[...] = dot_nt(mem[...], weight(held, sems, pieces, 1, 0)).astype(BF) * BF(HD**-0.5)
    masks = half_masks()
    rows = []
    for pair in range(heads // 2):
        cols = slice(pair * TILE, (pair + 1) * TILE)
        ctx, pair_rows = head_forward(q_out[:, cols], k_out[:, cols], v_out[:, cols], masks)
        packed[:, cols] = ctx.T.astype(BF)
        rows += pair_rows
    packed[:, width:] = as_parts(put_scalars(rows), heads).astype(BF)
    put_halves(info, keep, send, packed)
    weight(held, sems, pieces, 1, 1)


def start_out_matrix(info, pieces, held, sems):
    planes = held.shape[0]
    for j in range(4):
        for role, piece, unit in ((1, pieces[j], WALK + j), (0, pieces[4 + j], OTHER_WALK + j)):

            @pl.when(info[ROLE] == role)
            def _(piece=piece, unit=unit, j=j):
                for plane in range(planes):
                    pltpu.make_async_copy(
                        piece.at[1, plane], held.at[plane, info[unit]], sems.at[j * planes + plane]
                    ).start()


def out_matrix(pieces, held, sems):
    planes = held.shape[0]
    for j in range(4):
        for plane in range(planes):
            pltpu.make_async_copy(
                pieces[j].at[1, plane], held.at[plane, j], sems.at[j * planes + plane]
            ).wait()
    return matrix(held, Ellipsis)


def memory_kernel(info, c0, c1, c2, c3, sel, mem, cot, gain, bias, *refs):
    pieces, outs = refs[:8], refs[8:]
    result, mix_low, ctx_out, lse_out, grad_sum, vectors, held, sems = outs
    width = mem.shape[1]
    heads = width // HD
    start_out_matrix(info, pieces, held, sems)
    tiles, lse = blend_values((c0, c1, c2, c3), sel, width)
    lse_out[...] = lse
    for pair, tile in enumerate(tiles):
        ctx_out[:, pair * TILE : (pair + 1) * TILE] = tile
    mix = dot(ctx_out[...], out_matrix(pieces, held, sems))
    mix_low[...] = mix.astype(BF)
    normed, inv_std = norm_stats(mix + mem[...].astype(F32))
    gain_row = gain[...][None]
    result[...] = (normed * gain_row + bias[...][None]).astype(BF)
    upstream = cot[...].astype(F32)
    grad_sum[...] = norm_pull(upstream, normed, inv_std, gain_row)
    vectors[0:1] = jnp.sum(upstream * normed, axis=0, keepdims=True)
    vectors[1:2] = jnp.sum(upstream, axis=0, keepdims=True)


def unpack_forward_kernel(info, tok, mix, *refs):
    pieces, outs = refs[:8], refs[8:]
    k_out, v_out, q_out, ctx_out, lse_out, normed_out, inv_out, held, sems = outs
    width = tok.shape[1]
    heads = width // HD
    start_weights(info, pieces, held, sems)
    k_out[...] = dot_nt(mix[...], weight(held, sems, pieces, 0, 0)).astype(BF)
    v_out[...] = dot_nt(mix[...], weight(held, sems, pieces, 0, 1)).astype(BF)
    q_out[...] = dot_nt(tok[...], weight(held, sems, pieces, 1, 0)).astype(BF) * BF(HD**-0.5)
    masks = half_masks()
    for pair in range(heads // 2):
        cols = slice(pair * TILE, (pair + 1) * TILE)
        ctx, rows = head_forward(q_out[:, cols], k_out[:, cols], v_out[:, cols], masks)
        ctx_out[:, cols] = ctx.T.astype(BF)
        lse_out[2 * pair : 2 * pair + 1] = rows[0]
        lse_out[2 * pair + 1 : 2 * pair + 2] = rows[1]
    summed = dot(ctx_out[...], weight(held, sems, pieces, 1, 1)) + tok[...].astype(F32)
    normed, inv = norm_stats(summed)
    normed_out[...] = normed
    inv_out[...] = inv


GELU_A = math.sqrt(2.0 / math.pi)
GELU_B = 0.044715


def start_ffn(info, pieces, held, sems):
    planes, rows = held.shape[1], held.shape[2]
    quarter = rows // 4
    for plane in range(planes):
        for j, role in enumerate((info[ROLE], 1 - info[ROLE])):
            for part in range(4):
                at = pl.ds(part * quarter, quarter)
                pltpu.make_async_copy(
                    pieces[j].at[plane, at], held.at[role, plane, at], sems.at[plane, 4 * j + part]
                ).start()


def wait_ffn(pieces, held, sems, plane):
    rows = held.shape[2]
    quarter = rows // 4
    for j in range(2):
        for part in range(4):
            at = pl.ds(part * quarter, quarter)
            pltpu.make_async_copy(
                pieces[j].at[0, at], held.at[j, plane, at], sems.at[plane, 4 * j + part]
            ).wait()


def ffn_forward_kernel(info, normed_in, cot, mem_result, *refs):
    rows, refs = [r[...][None] for r in refs[:5]], refs[5:]
    attn_gain, attn_bias, out_gain, out_bias, ffn_bias = rows
    pieces, outs = refs[:2], refs[2:]
    out, attn_low, gelu_out, slope, grad_sum, vectors = outs[:6]
    held, bias, total, sems, bias_sem = outs[6:]
    planes = held.shape[1]
    bias_at = pl.ds(held.shape[2], 16)
    bias_copies = [
        pltpu.make_async_copy(pieces[0].at[plane, bias_at], bias.at[plane], bias_sem.at[plane])
        for plane in range(planes)
    ]
    for copy in bias_copies:
        copy.start()
    start_ffn(info, pieces, held, sems)
    attn = normed_in[...] * attn_gain + attn_bias
    attn_low[...] = attn.astype(BF)
    total[...] = attn + ffn_bias
    for copy in bias_copies:
        copy.wait()

    def forward(plane, carry):
        wait_ffn(pieces, held, sems, plane)
        parts = bias[plane].astype(F32)
        hidden = dot(attn_low[...], held[0, plane])
        hidden = hidden + (parts[0:1] + parts[1:2] + parts[2:3])
        square = hidden * hidden
        curve = jnp.tanh(GELU_A * hidden * (1.0 + GELU_B * square))
        half = 0.5 + 0.5 * curve
        gelu_out[plane] = (hidden * half).astype(BF)
        slope[plane] = (
            half
            + 0.5 * hidden * (1.0 - curve * curve) * (GELU_A + 3.0 * GELU_A * GELU_B * square)
        ).astype(BF)
        total[...] += dot(gelu_out[plane], held[1, plane])
        return carry

    lax.fori_loop(0, planes, forward, 0)
    out_normed, out_inv = norm_stats(total[...])
    rows = normed_in.shape[0]
    out[:rows] = (out_normed * out_gain + out_bias).astype(BF)
    out[rows:] = mem_result[...]
    upstream = cot[...].astype(F32)
    grad = norm_pull(upstream, out_normed, out_inv, out_gain)
    vectors[0:1] = jnp.sum(grad.astype(BF).astype(F32), axis=0, keepdims=True)
    vectors[1:2] = jnp.sum(upstream * out_normed, axis=0, keepdims=True)
    vectors[2:3] = jnp.sum(upstream, axis=0, keepdims=True)
    grad_sum[...] = grad


def ffn_backward_kernel(info, grad_sum, normed_in, inv_in, slope, attn_gain, *refs):
    pieces, outs = refs[:2], refs[2:]
    hid_grad, ffn_grad, mix_grad, mix_sum, vectors, hid_vec = outs[:6]
    held, total, sems = outs[6:]
    planes = held.shape[1]
    start_ffn(info, pieces, held, sems)
    grad = grad_sum[...]
    ffn_grad[...] = grad.astype(BF)
    total[...] = grad

    def backward(plane, carry):
        wait_ffn(pieces, held, sems, plane)
        pulled = dot_nt(ffn_grad[...], held[1, plane]) * slope[plane].astype(F32)
        low = pulled.astype(BF)
        hid_grad[plane] = low
        hid_vec[plane] = jnp.sum(low.astype(F32), axis=0, keepdims=True)
        total[...] += dot_nt(low, held[0, plane])
        return carry

    lax.fori_loop(0, planes, backward, 0)
    upstream = total[...]
    normed = normed_in[...]
    vectors[0:1] = jnp.sum(upstream * normed, axis=0, keepdims=True)
    vectors[1:2] = jnp.sum(upstream, axis=0, keepdims=True)
    grad = norm_pull(upstream, normed, inv_in[...], attn_gain[...][None])
    mix_sum[...] = grad
    mix_grad[...] = grad.astype(BF)


def unpack_backward_kernel(info, q_in, k_in, v_in, ctx, lse, mix_grad, mix_sum, *refs):
    pieces, outs = refs[:8], refs[8:]
    uq, uk, uv, keep, send, tok_part, held, sems = outs
    width = q_in.shape[1]
    heads = width // HD
    start_weights(info, pieces, held, sems, (1, 0))
    masks = half_masks()
    ctx_grad = dot_nt(mix_grad[...], weight(held, sems, pieces, 1, 1))
    ctx_low = ctx_grad.astype(BF)
    for pair in range(heads // 2):
        cols = slice(pair * TILE, (pair + 1) * TILE)
        product = ctx_grad[:, cols] * ctx[:, cols].astype(F32)
        first = product.astype(BF)
        second = (product - first.astype(F32)).astype(BF)
        deltas = []
        for side in range(2):
            picker = jnp.broadcast_to(masks[side], (16, TILE))
            deltas.append((dot_nt(picker, first) + dot_nt(picker, second))[0:1])
        lses = [lse[2 * pair : 2 * pair + 1], lse[2 * pair + 1 : 2 * pair + 2]]
        dq, dk, dv = head_backward(
            q_in[:, cols], k_in[:, cols], v_in[:, cols], ctx_low[:, cols], lses, deltas, masks
        )
        uq[:, cols] = (dq.T * (HD**-0.5)).astype(BF)
        uk[:, cols] = dk.astype(BF)
        uv[:, cols] = dv.astype(BF)
    mix_part = dot(uk[...], weight(held, sems, pieces, 0, 0))
    mix_part = mix_part + dot(uv[...], weight(held, sems, pieces, 0, 1))
    put_halves(info, keep, send, mix_part.astype(BF))
    tok_part[...] = mix_sum[...] + dot(uq[...], weight(held, sems, pieces, 1, 0))


def memory_back_kernel(info, c0, c1, c2, c3, sel, grad_sum, ctx, lse, *refs):
    pieces, outs = refs[:8], refs[8:]
    mix_grad, packed, held, sems = outs
    width = ctx.shape[1]
    heads = width // HD
    start_out_matrix(info, pieces, held, sems)
    total = grad_sum[...]
    for c in (c0, c1, c2, c3):
        total = total + c[...].astype(F32)
    mix_grad[...] = total.astype(BF)
    pulled = dot_nt(mix_grad[...], out_matrix(pieces, held, sems))
    packed[:, :width] = pulled.astype(BF)
    delta = jnp.zeros(lse.shape, F32)
    for pair in range(heads // 2):
        cols = slice(pair * TILE, (pair + 1) * TILE)
        product = pulled[:, cols] * ctx[:, cols].astype(F32)
        first = product.astype(BF)
        second = (product - first.astype(F32)).astype(BF)
        delta = delta + dot(first, sel[2 + pair]) + dot(second, sel[2 + pair])
    scalars = as_parts(lse[...], heads) + as_parts(delta, heads, PARTS * heads)
    packed[:, width:] = scalars.astype(BF)


def pack_backward_kernel(info, back, sel, q_in, k_in, v_in, tok_part, *refs):
    pieces, outs = refs[:8], refs[8:]
    pq, pk, pv, tok_grad, keep, send, held, sems = outs
    width = q_in.shape[1]
    heads = width // HD
    start_weights(info, pieces, held, sems)
    masks = half_masks()
    lse = dot(back[:, width:], sel[0]).T
    delta = dot(back[:, width:], sel[1]).T
    for pair in range(heads // 2):
        cols = slice(pair * TILE, (pair + 1) * TILE)
        lses = [lse[2 * pair : 2 * pair + 1], lse[2 * pair + 1 : 2 * pair + 2]]
        deltas = [delta[2 * pair : 2 * pair + 1], delta[2 * pair + 1 : 2 * pair + 2]]
        dq, dk, dv = head_backward(
            q_in[:, cols], k_in[:, cols], v_in[:, cols], back[:, cols], lses, deltas, masks
        )
        pq[:, cols] = (dq.T * (HD**-0.5)).astype(BF)
        pk[:, cols] = dk.astype(BF)
        pv[:, cols] = dv.astype(BF)
    total = dot(pk[...], weight(held, sems, pieces, 0, 0))
    total = total + dot(pv[...], weight(held, sems, pieces, 0, 1))
    tok_grad[...] = (total + tok_part[...]).astype(BF)
    put_halves(info, keep, send, dot(pq[...], weight(held, sems, pieces, 1, 0)).astype(BF))
    weight(held, sems, pieces, 1, 1)


def selectors(width):
    heads = width // HD
    lane = np.arange(TILE)
    inside = lane < PARTS * heads
    first = inside[:, None] & inside[None, :] & (lane[:, None] % heads == lane[None, :] % heads)
    shifted = lane - PARTS * heads
    second = (shifted >= 0) & (shifted < PARTS * heads)
    second = second[:, None] & inside[None, :] & (shifted[:, None] % heads == lane[None, :] % heads)
    rows = [first, second]
    target = (shifted >= 0) & (shifted < PARTS * heads)
    for pair in range(heads // 2):
        head = 2 * pair + (lane >= HD)
        rows.append(target[None, :] & (head[:, None] == (shifted % heads)[None, :]))
    return jnp.asarray(np.stack(rows).astype(np.float32), BF)


def pair_units(info):
    role, quad = info[ROLE], info[WALK]
    bit = jnp.where(role == 0, lax.rem(quad, 2), quad // 2)
    step, scale = jnp.where(role == 0, 2, 1), jnp.where(role == 0, 1, 2)
    keep = [bit * scale + at * step for at in range(2)]
    send = [(1 - bit) * scale + at * step for at in range(2)]
    return keep, send


def split_pairs(info, value, keep, send, rows):
    for units, out in zip(pair_units(info), (keep, send)):
        for at, unit in enumerate(units):
            out[at, 0] = value[pl.ds(pl.multiple_of(unit * rows, rows), rows)]


def ffn_weight_grad(info, role, operands, added, after=()):
    attn_low, hid_grad, gelu_out, ffn_grad = operands
    planes, rows, cols = hid_grad.shape
    width = attn_low.shape[1]
    quarter = width // 4

    def kernel(info, which, attn_ref, hid_ref, gelu_ref, grad_ref, *refs):
        plane = pl.program_id(0)
        refs = refs[:1] * (added is not None) + refs[(added is not None) + len(after) :]

        def put(value):
            if added is None:
                refs[0][0] = value.astype(BF)
            else:
                recv, held = refs[0], refs[5]
                held[...] = (value + recv[0].astype(F32)).astype(BF)
                for side, (keep, send) in enumerate((refs[1:3], refs[3:5])):

                    @pl.when(plane // (planes // 2) == side)
                    def _(keep=keep, send=send):
                        split_pairs(info, held, keep, send, quarter)

        @pl.when(which[0] == 0)
        def _():
            put(dot_tn(attn_ref[...], hid_ref[plane]))

        @pl.when(which[0] == 1)
        def _():
            put(dot_tn(gelu_ref[plane], grad_ref[...]))

    vm, sm = pl.BlockSpec(memory_space=pltpu.VMEM), pl.BlockSpec(memory_space=pltpu.SMEM)
    block = pl.BlockSpec((1, width, cols), lambda i: (i, 0, 0))
    half = planes // 2
    pairs = [
        pl.BlockSpec((2, 1, quarter, cols), lambda i: (0, jnp.minimum(i, half - 1), 0, 0)),
        pl.BlockSpec((2, 1, quarter, cols), lambda i: (0, jnp.maximum(i - half, 0), 0, 0)),
    ]
    pair_shape = jax.ShapeDtypeStruct((2, half, quarter, cols), BF)
    args, specs = [info, role, attn_low, hid_grad, gelu_out, ffn_grad], [sm, sm] + [vm] * 4
    if added is not None:
        args.append(added)
        specs.append(block)
    return pl.pallas_call(
        kernel,
        grid=(planes,),
        out_shape=(
            jax.ShapeDtypeStruct((planes, width, cols), BF)
            if added is None
            else [pair_shape] * 4
        ),
        in_specs=specs + [pl.BlockSpec(memory_space=pl.ANY)] * len(after),
        out_specs=block if added is None else [pairs[0], pairs[0], pairs[1], pairs[1]],
        scratch_shapes=[] if added is None else [pltpu.VMEM((width, cols), BF)],
        compiler_params=pltpu.CompilerParams(vmem_limit_bytes=60 * MIB),
        cost_estimate=SMALL,
        name="ffn_weight_grad",
    )(*args, *after)


def attention_weight_grad(info, role, operands, planes, added, after=()):
    width = operands[0].shape[1]
    quarter = width // 4
    size = quarter // planes

    def kernel(info, which, kv, dk, dv, q_rows, dq, left, right, *refs):
        def put(mat, value, by_plane=False):
            if added is None:
                out, value = refs[0].at[mat], value.astype(BF)
            else:
                out = refs[3].at[mat]
            if by_plane:
                for plane in range(planes):
                    for quad in range(4):
                        at, to = (plane * 4 + quad) * size, (quad * planes + plane) * size
                        piece = value[at : at + size]
                        if added is not None:
                            piece = piece + refs[0][mat, to : to + size].astype(F32)
                        out[to : to + size] = piece.astype(BF)
            else:
                if added is not None:
                    value = value + refs[0][mat].astype(F32)
                out[...] = value.astype(BF)

        @pl.when(which[0] == 0)
        def _():
            put(0, dot_tn(kv[...], dk[...]))
            put(1, dot_tn(kv[...], dv[...]))

        @pl.when(which[0] == 1)
        def _():
            put(0, dot_tn(q_rows[...], dq[...]))
            put(1, dot_tn(left[...], right[...]), True)

        if added is not None:
            for mat in range(2):
                keep, send = refs[1].at[:, mat : mat + 1], refs[2].at[:, mat : mat + 1]
                split_pairs(info, refs[3].at[mat], keep, send, quarter)

    rows = operands[0].shape[0] + operands[3].shape[0]
    operands = [info, role] + list(operands)
    outs = [((2, width, width), BF)]
    scratch = []
    if added is not None:
        operands.append(added)
        outs = [((2, 2, quarter, width), BF)] * 2
        scratch = [pltpu.VMEM((2, width, width), BF)]
    result = call(
        kernel,
        "attention_weight_grad",
        operands,
        outs,
        scratch=scratch,
        flops=2 * rows * width * width,
        smem=2,
        after=after,
    )
    return result[0] if added is None else result


def add_pairs(info, kept, got, after=()):
    _, mats, rows, cols = kept.shape

    def kernel(info, kept_ref, got_ref, *refs):
        keep, send = refs[len(after) :]
        quad = info[WALK]
        at = jnp.where(info[ROLE] == 0, quad // 2, lax.rem(quad, 2))
        for index, out in ((at, keep), (1 - at, send)):
            out[0] = (kept_ref[index, 0].astype(F32) + got_ref[index, 0].astype(F32)).astype(BF)

    pairs = pl.BlockSpec((2, 1, rows, cols), lambda i: (0, i, 0, 0))
    one = pl.BlockSpec((1, rows, cols), lambda i: (i, 0, 0))
    return pl.pallas_call(
        kernel,
        grid=(mats,),
        out_shape=[jax.ShapeDtypeStruct((mats, rows, cols), BF)] * 2,
        in_specs=[pl.BlockSpec(memory_space=pltpu.SMEM), pairs, pairs]
        + [pl.BlockSpec(memory_space=pl.ANY)] * len(after),
        out_specs=[one, one],
        compiler_params=pltpu.CompilerParams(vmem_limit_bytes=16 * MIB),
        cost_estimate=SMALL,
        name="add_pairs",
    )(info, kept, got, *after)


def put_planes(info, held, keep, send):
    kind = lax.rem(info[PLANE], 2)
    for at in range(held.shape[0] // 2):
        keep[at] = held[2 * at + kind].astype(keep.dtype)
        send[at] = held[2 * at + 1 - kind].astype(send.dtype)


def ffn_blocks_kernel(info, kept_low, got_low, kept_high, got_high, keep, send):
    kind = lax.rem(info[PLANE], 2)
    for at, (kept, got) in enumerate(((kept_low, got_low), (kept_high, got_high))):
        for plane, out in ((kind, keep), (1 - kind, send)):
            out[at] = (kept[plane].astype(F32) + got[plane].astype(F32)).astype(out.dtype)


def attention_blocks_kernel(info, kept, got, keep, send, total, held):
    planes, _, rows, cols = held.shape
    size = rows // planes
    total[...] = kept[...].astype(F32) + got[...].astype(F32)
    for plane in range(planes):
        held[plane, 0] = total[0, :, plane * cols : (plane + 1) * cols]

    @pl.when(info[ROLE] == 0)
    def _():
        for plane in range(planes):
            held[plane, 1] = total[1, :, plane * cols : (plane + 1) * cols]

    @pl.when(info[ROLE] == 1)
    def _():
        for plane in range(planes):
            for at in range(planes):
                held[plane, 1, at * size : (at + 1) * size] = total[
                    1, plane * size : (plane + 1) * size, at * cols : (at + 1) * cols
                ]

    put_planes(info, held, keep, send)


def middle_kernel(info, kept, got, keep, send):
    mine = info[PLANE] // 2
    keep[...] = kept[mine] + got[mine].astype(F32)
    send[...] = (kept[1 - mine] + got[1 - mine].astype(F32)).astype(BF)


def ffn_total_kernel(info, own, other, keep, send, total):
    total[...] = own[...] + other[...].astype(F32)
    half = keep.shape[0]
    for index, out in ((info[ROLE], keep), (1 - info[ROLE], send)):
        out[...] = total[pl.ds(pl.multiple_of(index * half, half), half)]


def attention_total_kernel(info, own, other, keep, send, total, planes):
    total[...] = own[...] + other[...].astype(F32)
    half = keep.shape[1]
    for index, out in ((info[ROLE], keep), (1 - info[ROLE], send)):
        at = pl.ds(pl.multiple_of(index * half, half), half)
        out[0] = total[0, at]

        @pl.when(info[ROLE] == 0)
        def _(out=out, at=at):
            out[1] = total[1, at]

        @pl.when(info[ROLE] == 1)
        def _(out=out, index=index):
            size = half // planes
            for chunk in range(planes):
                start = pl.multiple_of(2 * chunk * size + index * size, size)
                out[1, chunk * size : (chunk + 1) * size] = total[1, pl.ds(start, size)]


def attention_final_kernel(info, kept, got, key_g, value_g, query_g, out_g, planes):
    def put(zero, one):
        key_g[...] = zero[0]
        value_g[...] = zero[1]
        query_g[...] = one[0]
        size = out_g.shape[0]
        chunks = [one[1, at * size : (at + 1) * size] for at in range(planes)]
        out_g[...] = jnp.concatenate(chunks, axis=1)

    @pl.when(info[ROLE] == 0)
    def _():
        put(kept, got)

    @pl.when(info[ROLE] == 1)
    def _():
        put(got, kept)


def ffn_final_kernel(info, kept, got, in_g, out_g):
    @pl.when(info[ROLE] == 0)
    def _():
        in_g[...] = kept[...]
        out_g[...] = got[...]

    @pl.when(info[ROLE] == 1)
    def _():
        in_g[...] = got[...]
        out_g[...] = kept[...]


def empty_row(width):
    heads = width // HD
    row = np.zeros((1, width + TILE), np.float32)
    row[:, width : width + heads] = NEG_FILL
    return jnp.asarray(row)


def blend_two_kernel(info, keep, got, sel, value):
    width = value.shape[1] - TILE
    tiles, lse = blend_values((keep, got), sel, width)
    for pair, tile in enumerate(tiles):
        value[:, pair * TILE : (pair + 1) * TILE] = tile
    value[:, width:] = as_parts(lse, width // HD).astype(BF)


def first_pieces(places, lengths, memory, weights, unit, block_len):
    sm, vm = pl.BlockSpec(memory_space=pltpu.SMEM), pl.BlockSpec(memory_space=pltpu.VMEM)
    rows, width = weights[0].shape
    return pl.pallas_call(
        functools.partial(first_pieces_kernel, unit=unit, block_len=block_len),
        out_shape=[
            jax.ShapeDtypeStruct((INFO,), jnp.int32),
            jax.ShapeDtypeStruct((4, rows // 4, width), BF),
            jax.ShapeDtypeStruct(memory.shape[1:], BF),
        ],
        in_specs=[sm, sm] + [pl.BlockSpec(memory_space=pl.ANY)] * 9,
        out_specs=[sm, vm, vm],
        scratch_shapes=[pltpu.SemaphoreType.DMA((5,))],
        compiler_params=pltpu.CompilerParams(vmem_limit_bytes=60 * MIB),
        cost_estimate=SMALL,
        name="first_pieces",
    )(places, lengths, memory, *weights)


def make_local(axis_seq, axis_head):
    unit = axis_seq // SLOTS
    fast = axis_seq == 8

    def swap(value, step):
        return lax.ppermute(value, "seq", [(i, i ^ step) for i in range(axis_seq)])

    def cross(value, order):
        steps = (2, 4) if order == 0 else (4, 2)
        return lax.ppermute(value, "seq", [(i, i ^ steps[i % 2]) for i in range(axis_seq)])

    def over(value, step):
        return lax.ppermute(value, "head", [(i, i ^ step) for i in range(axis_head)])

    def from_planes(value):
        got = [value]
        step = 1
        while step < axis_head:
            got += [over(value, step) if part is value else over(part, step) for part in got]
            step *= 2
        return got

    def direct_planes(value):
        return [value] + [over(value, step) for step in range(1, axis_head)]

    def local(
        tokens,
        memory,
        seq_lengths,
        pack_query,
        pack_key,
        pack_value,
        pack_out,
        unpack_query,
        unpack_key,
        unpack_value,
        unpack_out,
        ffn_in,
        ffn_in_bias,
        ffn_out,
        ffn_out_bias,
        mem_gain,
        mem_bias,
        attn_gain,
        attn_bias,
        out_gain,
        out_bias,
        cot_tokens,
        cot_memory,
    ):
        seq_index = lax.axis_index("seq")
        head_index = lax.axis_index("head")
        _, block_len, width = tokens.shape
        hidden_width = ffn_in.shape[1]
        my_lane, role = seq_index % unit, seq_index % 2
        quarter, head_cols = width // 4, width // axis_head
        info, pieces, mem = first_pieces(
            jnp.stack([seq_index, head_index]),
            seq_lengths,
            memory,
            [pack_key.T, pack_value.T, pack_query.T, pack_out]
            + [unpack_key.T, unpack_value.T, unpack_query.T, unpack_out],
            unit,
            block_len,
        )
        last = []

        def run(kernel, name, operands, outs, also=(), **more):
            after = list(last) + list(also)
            result = call(kernel, name, [info] + operands, outs, after=after, **more)
            last[:] = [result[0]]
            return result

        def run_grid(function, *operands):
            result = function(info, *operands, after=list(last))
            last[:] = [result[0] if isinstance(result, (list, tuple)) else result]
            return result

        def mine(value):
            return lax.dynamic_index_in_dim(value, head_index, 0, keepdims=False)

        def gather_unit(value):
            step = 1
            while step < unit:
                other = swap(value, step)
                low = (my_lane // step) % 2 == 0
                value = jnp.concatenate(
                    [jnp.where(low, value, other), jnp.where(low, other, value)], axis=0
                )
                step *= 2
            return value

        def scatter_unit(value, add, step):
            while step >= 1:
                half = value.shape[0] // 2
                low = (my_lane // step) % 2 == 0
                keep = jnp.where(low, value[:half], value[half:])
                send = jnp.where(low, value[half:], value[:half])
                value = add([keep, swap(send, step)])
                step //= 2
            return value

        def fetch_start(value):
            return [value] + [swap(value, j * unit) for j in range(1, SLOTS)]

        def fetch_finish(parts, also=()):
            return run(pick_kernel, "pick_slot", parts, [(parts[0].shape, BF)], also=also)[0]

        def sum_rows(values):
            total = values[0].astype(F32)
            for value in values[1:]:
                total = total + value.astype(F32)
            return total.astype(BF)

        packed_width = width + TILE
        row_count = memory.shape[1]
        slot_count = unit * row_count
        half_rows = slot_count // 2
        sel = selectors(width)
        deep = [((row_count, packed_width), BF)] * SLOTS
        flat = [((row_count, width), BF)] * SLOTS

        def blend_two(values):
            return run(blend_two_kernel, "blend", values + [sel], [(values[0].shape, BF)])[0]

        def to_slots(keep, got, kernel, extra, outs, add, empty, also=()):
            if unit > 2:
                keep = scatter_unit(add([keep, got]), add, unit // 4)
                got = jnp.broadcast_to(empty, keep.shape).astype(BF)
            scratch = [pltpu.VMEM(keep.shape, BF)] if extra else []
            parts = run(kernel, "to_slots", [keep, got] + extra, outs, scratch=scratch, also=also)
            return [parts[0]] + [swap(parts[j], j * unit) for j in range(1, SLOTS)]

        def spread(piece, first, second, third):
            parts = [piece, first, second, third]
            return parts + [swap(part, 1) for part in parts]

        def all_planes(pieces):
            return run(
                stack_kernel, "all_planes", pieces, [((axis_head,) + pieces[0].shape, BF)]
            )[0]

        held_out = pltpu.VMEM((axis_head, 4, head_cols // 4, width), BF)
        held_pair = pltpu.VMEM((2, 2) + held_out.shape, BF)
        pair_sems = pltpu.SemaphoreType.DMA((2, 2, 4 * axis_head))
        out_sems = pltpu.SemaphoreType.DMA((4 * axis_head,))
        ffn_sems = pltpu.SemaphoreType.DMA((axis_head, 8))
        tok_low, slot_low = ((block_len, width), BF), ((slot_count, width), BF)
        row_low, half_low = ((row_count, width), BF), ((half_rows, width), BF)
        tok_f32 = ((block_len, width), F32)

        mem_parts = fetch_start(mem)
        planes = from_planes(pieces)
        piece_ffn, tok, cot_tok, cot_mem = run(
            other_pieces_kernel,
            "other_pieces",
            [ffn_in_bias, ffn_in, ffn_out, tokens, cot_tokens, cot_memory],
            [((width + 16, hidden_width), BF), tok_low, tok_low, row_low],
            anys=5,
            scratch=[pltpu.SemaphoreType.DMA((6,))],
        )
        mem_picked = fetch_finish(mem_parts)
        shape = (2, axis_head) + pieces.shape[1:]
        rows_pack, rows_un = run(planes_kernel, "weight_planes", planes, [(shape, BF)] * 2)

        pack_first, pack_second = cross(rows_pack, 0), cross(rows_pack, 1)
        pack_third = cross(pack_first, 1)
        w_pack = spread(rows_pack, pack_first, pack_second, pack_third)
        rows_un = tie(rows_un, pack_third)
        un_first, un_second = cross(rows_un, 0), cross(rows_un, 1)
        ffn_rows = lax.all_gather(tie(piece_ffn, rows_pack), "head", axis=0)
        mem_slot = gather_unit(mem_picked)
        k_pack, v_pack, q_pack, keep, send = run(
            pack_forward_kernel,
            "pack_forward",
            [tok, mem_slot] + w_pack,
            [tok_low, tok_low, slot_low] + [((half_rows, packed_width), BF)] * 2,
            anys=8,
            scratch=[pltpu.VMEM((slot_count, packed_width), BF), held_pair, pair_sems],
        )
        got = swap(send, unit // 2)
        un_first = tie(un_first, keep)
        w_un = spread(rows_un, un_first, un_second, cross(un_first, 1))
        parts = to_slots(keep, got, blend_kernel, [sel], deep, blend_two, empty_row(width), [un_second])
        mem_result, mix_low, pack_ctx, pack_lse, grad_memsum, mem_vectors = run(
            memory_kernel,
            "memory_rows",
            parts + [sel, mem, cot_mem, mem_gain, mem_bias] + w_pack,
            [row_low, row_low, row_low]
            + [((row_count, TILE), F32), ((row_count, width), F32), ((8, width), F32)],
            anys=8,
            scratch=[held_out, out_sems],
            also=[w_un[3]],
        )
        mix_parts = fetch_start(mix_low)
        mix_picked = fetch_finish(mix_parts, w_un)
        ffn_rows = tie(ffn_rows, mix_picked)
        ffn_parts = [ffn_rows, swap(ffn_rows, 1)]
        mix_slot = gather_unit(mix_picked)
        k_un, v_un, q_un, tok_ctx, tok_lse, attn_normed, attn_inv = run(
            unpack_forward_kernel,
            "unpack_forward",
            [tok, mix_slot] + w_un,
            [slot_low, slot_low, tok_low, tok_low]
            + [((16, block_len), F32), tok_f32, ((block_len, 1), F32)],
            anys=8,
            scratch=[held_pair, pair_sems],
        )
        by_plane = (axis_head, block_len, hidden_width)
        held_ffn = pltpu.VMEM((2, axis_head, width, hidden_width), BF)
        out_result, attn_low, gelu_out, slope, grad_sum, out_vectors = run(
            ffn_forward_kernel,
            "ffn_forward",
            [attn_normed, cot_tok, mem_result]
            + [attn_gain, attn_bias, out_gain, out_bias, ffn_out_bias]
            + ffn_parts,
            [((block_len + row_count, width), BF)]
            + [tok_low, (by_plane, BF), (by_plane, BF), tok_f32, ((8, width), F32)],
            anys=2,
            scratch=[
                held_ffn,
                pltpu.VMEM((axis_head, 16, hidden_width), BF),
                pltpu.VMEM((block_len, width), F32),
                ffn_sems,
                pltpu.SemaphoreType.DMA((axis_head,)),
            ],
        )
        out_rows = lax.all_gather(out_result, "head", axis=0)
        out_tokens, out_memory = out_rows[:, :block_len], out_rows[:, block_len:]
        hid_grad, ffn_grad, mix_grad, mix_sum, attn_vectors, hid_vec = run(
            ffn_backward_kernel,
            "ffn_backward",
            [grad_sum, attn_normed, attn_inv, slope, attn_gain] + ffn_parts,
            [(by_plane, BF), tok_low, tok_low, tok_f32, ((8, width), F32)]
            + [((axis_head, 1, hidden_width), F32)],
            anys=2,
            scratch=[held_ffn, pltpu.VMEM((block_len, width), F32), ffn_sems],
        )

        role_info, other_info = role[None], 1 - role[None]
        ffn_operands = (attn_low, hid_grad, gelu_out, ffn_grad)

        def vectors_step(value, other):
            return run(total_kernel, "vectors", [value, other], [(value.shape, F32)])[0]

        if fast:
            ffn_sent = run_grid(ffn_weight_grad, other_info, ffn_operands, None)
            ffn_got = swap(ffn_sent, 1)
        small = run(
            vectors_kernel,
            "vectors",
            [mem_vectors, out_vectors, attn_vectors, hid_vec],
            [((16, width), F32)],
        )[0]
        small_got = swap(small, 1)
        uq_grad, uk_part, uv_part, keep, send, tok_part = run(
            unpack_backward_kernel,
            "unpack_backward",
            [q_un, k_un, v_un, tok_ctx, tok_lse, mix_grad, mix_sum] + w_un,
            [tok_low, slot_low, slot_low, half_low, half_low, tok_f32],
            anys=8,
            scratch=[held_pair, pair_sems],
        )
        un_operands = (mix_slot, uk_part, uv_part, tok, uq_grad, tok_ctx, mix_grad)
        got = swap(send, unit // 2)
        small = vectors_step(small, small_got)
        parts = to_slots(keep, got, sum_kernel, [], flat, sum_rows, jnp.zeros((), BF))
        small_got = swap(small, 2)
        if fast:
            ffn_low, low_sent, ffn_high, high_sent = run_grid(
                ffn_weight_grad, role_info, ffn_operands, ffn_got
            )
        mem_mix_grad, packed = run(
            memory_back_kernel,
            "memory_rows_backward",
            parts + [sel, grad_memsum, pack_ctx, pack_lse] + w_pack,
            [row_low, ((row_count, packed_width), BF)],
            anys=8,
            scratch=[held_out, out_sems],
        )
        back_parts = fetch_start(packed)
        small = vectors_step(small, small_got)
        step = 4
        while step < axis_seq:
            small_got = swap(small, step)
            if fast:
                un_sent = run_grid(attention_weight_grad, other_info, un_operands, axis_head, None)
                un_kept, un_sent = run_grid(
                    attention_weight_grad, role_info, un_operands, axis_head, swap(un_sent, 1)
                )
            small = vectors_step(small, small_got)
            step *= 2
        back_picked = fetch_finish(back_parts)
        if fast:
            un_got = cross(tie(un_sent, back_picked), 0)
            low_got = cross(tie(low_sent, back_picked), 0)
        back = gather_unit(back_picked)
        pq_part, pk_grad, pv_grad, grad_tokens, keep, send = run(
            pack_backward_kernel,
            "pack_backward",
            [back, sel, q_pack, k_pack, v_pack, tok_part] + w_pack,
            [slot_low, tok_low, tok_low, tok_low, half_low, half_low],
            anys=8,
            scratch=[held_pair, pair_sems],
            also=[out_rows],
        )
        grad_tokens = lax.all_gather(grad_tokens, "head", axis=0)
        pack_operands = (tok, pk_grad, pv_grad, mem_slot, pq_part, pack_ctx, mem_mix_grad)
        got = swap(send, unit // 2)
        if fast:
            un_kept, un_sent = run_grid(add_pairs, un_kept, un_got)
            un_got = cross(un_sent, 1)
            ffn_low, low_sent = run_grid(add_pairs, ffn_low, low_got)
            high_got = cross(tie(high_sent, ffn_low), 0)
        if fast:
            pack_sent = run_grid(attention_weight_grad, other_info, pack_operands, axis_head, None)
            pack_got = swap(pack_sent, 1)
        parts = to_slots(keep, got, sum_kernel, [], flat, sum_rows, jnp.zeros((), BF))

        rows = (quarter, hidden_width)
        half = (quarter // 2, hidden_width)
        pair_rows = (2, quarter, head_cols)
        pair_half = (2, quarter // 2, head_cols)

        def pairs_of(shape):
            return [((2,) + shape, F32), ((2,) + shape, BF)]

        def middle(kept, got, shape):
            keep, send = run(
                middle_kernel, "plane_middle", [kept, got], [(shape, F32), (shape, BF)]
            )
            return keep, over(send, 2)

        def ffn_blocks(kept, got):
            operands = [kept[0], got[0], kept[1], got[1]]
            keep, send = run(ffn_blocks_kernel, "plane_blocks", operands, pairs_of(rows))
            return keep, over(send, 1)

        def ffn_total(kept, got):
            scratch = [pltpu.VMEM(rows, F32)]
            keep, send = run(
                ffn_total_kernel, "plane_total", [kept, got], [(half, F32)] * 2, scratch=scratch
            )
            return [keep, swap(send, 1)]

        def ffn_final(halves):
            return run(ffn_final_kernel, "weight_rows", halves, [(half, F32)] * 2)

        def attention_blocks(kept, got):
            keep, send = run(
                attention_blocks_kernel,
                "plane_blocks",
                [kept, got],
                pairs_of(pair_rows),
                scratch=[
                    pltpu.VMEM((2, quarter, width), F32),
                    pltpu.VMEM((axis_head,) + pair_rows, F32),
                ],
            )
            return keep, over(send, 1)

        def attention_total(kept, got):
            keep, send = run(
                functools.partial(attention_total_kernel, planes=axis_head),
                "plane_total",
                [kept, got],
                [(pair_half, F32)] * 2,
                scratch=[pltpu.VMEM(pair_rows, F32)],
            )
            return [keep, swap(send, 1)]

        def attention_final(halves):
            return run(
                functools.partial(attention_final_kernel, planes=axis_head),
                "weight_rows",
                halves,
                [(pair_half[1:], F32)] * 3 + [((quarter // 2 // axis_head, width), F32)],
            )

        def scatter(value, axis, dim):
            return lax.psum_scatter(value, axis, scatter_dimension=dim, tiled=True)

        def by_columns(grad):
            grad = scatter(grad, "seq", 0).reshape(-1, axis_head, head_cols)
            return scatter(grad.transpose(1, 0, 2), "head", 0)[0].astype(F32)

        def by_rows(grad):
            grad = scatter(grad.reshape(axis_head, -1, width), "seq", 1)
            return scatter(grad, "head", 0)[0].astype(F32)

        def product(left, right):
            return dot_tn(left, right).astype(BF)

        def attention_simple(operands):
            kv, dk, dv, q_rows, dq, left, right = operands
            first = [by_columns(product(a, b)) for a, b in ((kv, dk), (kv, dv), (q_rows, dq))]
            return first + [by_rows(product(left, right))]

        if fast:
            pack_kept, pack_sent = run_grid(
                attention_weight_grad, role_info, pack_operands, axis_head, pack_got
            )
            pack_got = cross(pack_sent, 0)
            ffn_high, high_sent = run_grid(add_pairs, ffn_high, high_got)
            low_got, high_got = cross(tie(low_sent, ffn_high), 1), cross(high_sent, 1)
            un_blocks = attention_blocks(un_kept, un_got)
        total = run(memory_total_kernel, "memory_total", [grad_memsum] + parts, [row_low])[0]
        grad_planes = from_planes(total)
        small_planes = direct_planes(tie(small, total))
        if fast:
            un_blocks = middle(*un_blocks, pair_rows)
            pack_kept, pack_sent = run_grid(add_pairs, pack_kept, pack_got)
            pack_got = cross(pack_sent, 1)
            blocks = ffn_blocks([ffn_low, ffn_high], [low_got, high_got])
            un_halves = attention_total(*un_blocks)
            pack_blocks = attention_blocks(pack_kept, pack_got)
            blocks = middle(*blocks, rows)
            un_grads = attention_final(un_halves)
            pack_blocks = middle(*pack_blocks, pair_rows)
            halves = ffn_total(*blocks)
            grad_memory = all_planes(grad_planes)
            pack_halves = attention_total(*pack_blocks)
            fi_grad, fo_grad = ffn_final(halves)
            pack_grads = attention_final(pack_halves)
        else:
            grad_memory = all_planes(grad_planes)
            un_grads = attention_simple(un_operands)
            pack_grads = attention_simple(pack_operands)
            fi_grad = jnp.stack([product(attn_low, hid_grad[p]) for p in range(axis_head)])
            fi_grad = scatter(scatter(fi_grad, "seq", 1), "head", 0)[0].astype(F32)
            fo_grad = jnp.stack([product(gelu_out[p], ffn_grad) for p in range(axis_head)])
            fo_grad = scatter(scatter(fo_grad, "seq", 1), "head", 0)[0].astype(F32)

        small = run(
            plane_vectors_kernel,
            "vectors",
            small_planes,
            [(small.shape, F32)],
            scratch=[pltpu.VMEM((axis_head,) + small.shape, F32)],
        )[0]
        share = width // axis_seq
        vectors = lax.dynamic_slice_in_dim(small[:7], seq_index * share, share, 1)
        fib = mine(small[7 : 7 + axis_head].reshape(axis_head, -1))
        fib = lax.dynamic_slice_in_dim(fib, seq_index * share, share, 0)
        return (
            out_tokens,
            out_memory,
            grad_tokens,
            grad_memory,
            pack_grads[2],
            pack_grads[0],
            pack_grads[1],
            pack_grads[3],
            un_grads[2],
            un_grads[0],
            un_grads[1],
            un_grads[3],
            fi_grad,
            fib,
            fo_grad,
            vectors[0],
            vectors[1],
            vectors[2],
            vectors[3],
            vectors[4],
            vectors[5],
            vectors[6],
        )

    return local


def solution(mesh):
    rows = P(None, "seq", None)
    by_col, by_row, both = P(None, "head"), P("head", None), P("seq", "head")
    wide_rows = P(("head", "seq"), None)
    in_specs = (
        (rows, rows, P())
        + (by_col, by_col, by_col, by_row)
        + (by_col, by_col, by_col, by_row)
        + (by_col, P("head"), by_row)
        + (P(),) * 7
        + (rows, rows)
    )
    out_specs = (
        (rows,) * 4
        + (both, both, both, wide_rows)
        + (both, both, both, wide_rows)
        + (both, P(("head", "seq")), wide_rows)
        + (P("seq"),) * 7
    )
    local = make_local(mesh.shape["seq"], mesh.shape["head"])
    return jax.shard_map(local, mesh=mesh, in_specs=in_specs, out_specs=out_specs, check_vma=False)
```

```python
import functools
import math

import jax
import jax.numpy as jnp
import numpy as np
from jax import lax
from jax.experimental import pallas as pl
from jax.experimental.pallas import tpu as pltpu
from jax.sharding import PartitionSpec as P

HD = 64
SLOTS = 4
EPSILON = 1e-05
NEG_FILL = -1e30
BF = jnp.bfloat16
F32 = jnp.float32


def dot(left, right):
    return jnp.dot(left, right, preferred_element_type=F32)


def dot_nt(left, right):
    return lax.dot_general(left, right, (((1,), (1,)), ((), ())), preferred_element_type=F32)


def dot_tn(left, right):
    return lax.dot_general(left, right, (((0,), (0,)), ((), ())), preferred_element_type=F32)


TILE = 2 * HD
PARTS = 3
MIB = 1024 * 1024
SMALL = pl.CostEstimate(flops=1, bytes_accessed=1, transcendentals=0)


ROLE, WALK, OTHER_WALK, PLANE, SLOT, UNIT, HALF, BIT, OTHER_BIT, INFO = 0, 1, 5, 9, 10, 11, 12, 13, 14, 16


def call(kernel, name, operands, outs, anys=0, scratch=(), flops=0, vmem=None, out_any=0, after=(), smem=1):
    def body(*refs):
        kernel(*refs[: len(operands)], *refs[len(operands) + len(after) :])

    if vmem is None:
        vmem = 60 if anys or name == "attention_weight_grad" else 16
    vm, anywhere = pl.BlockSpec(memory_space=pltpu.VMEM), pl.BlockSpec(memory_space=pl.ANY)
    specs = [pl.BlockSpec(memory_space=pltpu.SMEM)] * smem
    specs += [vm] * (len(operands) - smem - anys) + [anywhere] * (anys + len(after))
    return pl.pallas_call(
        body,
        out_shape=[jax.ShapeDtypeStruct(s, d) for s, d in outs],
        in_specs=specs,
        out_specs=[vm] * (len(outs) - out_any) + [anywhere] * out_any,
        scratch_shapes=list(scratch),
        compiler_params=pltpu.CompilerParams(vmem_limit_bytes=vmem * MIB),
        cost_estimate=SMALL,
        name=name,
    )(*operands, *after)


def info_kernel(places, lengths, info, unit, block_len):
    seq, head = places[0], places[1]
    role, quad = lax.rem(seq, 2), lax.rem(seq // 2, 4)
    first, second = 1 + role, 2 - role
    info[ROLE] = role
    for at, step in enumerate((0, first, second, 3)):
        info[WALK + at] = quad ^ step
    for at, step in enumerate((0, second, first, 3)):
        info[OTHER_WALK + at] = quad ^ step
    info[PLANE] = head
    end = 0
    slot = 0
    for at in range(SLOTS):
        end = end + lengths[head, at]
        slot = slot + (end <= seq * block_len).astype(jnp.int32)
    info[SLOT] = slot
    info[UNIT] = seq // unit
    info[HALF] = lax.rem(seq, unit) // (unit // 2)
    info[BIT] = jnp.where(role == 0, lax.rem(quad, 2), quad // 2)
    info[OTHER_BIT] = jnp.where(role == 0, quad // 2, lax.rem(quad, 2))
    info[INFO - 1] = 0


def planes_kernel(info, first, second, third, fourth, *outs):
    for at, ref in enumerate((first, second, third, fourth)):
        for mat in range(4):
            out = outs[mat // 2]
            out[mat % 2, info[PLANE] ^ at] = ref[mat]


def first_pieces_kernel(places, lengths, memory, *refs, unit, block_len):
    weights, (info, piece, mem, sems) = refs[:8], refs[8:]
    info_kernel(places, lengths, info, unit, block_len)
    copy_mem = pltpu.make_async_copy(memory.at[places[1]], mem, sems.at[4])
    copy_mem.start()
    rows = piece.shape[1]
    at = pl.ds(pl.multiple_of(info[WALK] * rows, rows), rows)
    for role, chosen in enumerate(((0, 1, 4, 5), (2, 3, 6, 7))):

        @pl.when(info[ROLE] == role)
        def _(chosen=chosen):
            copies = [
                pltpu.make_async_copy(weights[which].at[at], piece.at[mat], sems.at[mat])
                for mat, which in enumerate(chosen)
            ]
            for copy in copies:
                copy.start()
            for copy in copies:
                copy.wait()

    copy_mem.wait()


def other_pieces_kernel(info, bias, *refs):
    ffn_in, ffn_out, tokens, cot_tok, cot_mem = refs[:5]
    ffn, tok, cot_t, cot_m, sems = refs[5:]
    plane = info[PLANE]
    copies = []
    for at, (source, to) in enumerate(((tokens, tok), (cot_tok, cot_t), (cot_mem, cot_m))):
        copies.append(pltpu.make_async_copy(source.at[plane], to, sems.at[2 + at]))
    for copy in copies:
        copy.start()
    rows = ffn.shape[0] - 16
    for role, source in enumerate((ffn_in, ffn_out)):

        @pl.when(info[ROLE] == role)
        def _(source=source):
            copy = pltpu.make_async_copy(source, ffn.at[pl.ds(0, rows)], sems.at[5])
            copy.start()
            copy.wait()

    value = bias[...][None]
    parts = []
    for part in range(PARTS):
        low = value.astype(BF).astype(F32)
        parts.append(low)
        value = value - low
    parts.append(jnp.zeros((16 - PARTS, bias.shape[0]), F32))
    ffn[rows:] = jnp.concatenate(parts, axis=0).astype(BF)
    for copy in copies:
        copy.wait()


def vectors_kernel(info, mem_vectors, out_vectors, hid_vec, out):
    out[...] = jnp.zeros(out.shape, F32)
    out[0:1] = out_vectors[0:1]
    out[1:3] = mem_vectors[0:2]
    out[3:5] = out_vectors[3:5]
    out[5:7] = out_vectors[1:3]
    for plane in range(hid_vec.shape[0]):
        out[7 + plane : 8 + plane] = hid_vec[plane]


def total_kernel(info, *refs):
    total = refs[0][...]
    for ref in refs[1:-1]:
        total = total + ref[...]
    refs[-1][...] = total


def plane_vectors_kernel(info, first, second, third, fourth, out, held):
    planes = held.shape[0]
    for at, ref in enumerate((first, second, third, fourth)):
        held[info[PLANE] ^ at] = ref[...]
    total = held[0]
    for plane in range(1, planes):
        total = total + held[plane]
    out[...] = total


def memory_total_kernel(info, base, first, second, third, fourth, out):
    total = base[...]
    for ref in (first, second, third, fourth):
        total = total + ref[...].astype(F32)
    out[...] = total.astype(BF)


def pick_kernel(info, first, second, third, fourth, out, sem):
    for at, ref in enumerate((first, second, third, fourth)):

        @pl.when(info[SLOT] == (info[UNIT] ^ at))
        def _(ref=ref):
            copy = pltpu.make_async_copy(ref, out, sem)
            copy.start()
            copy.wait()


def tie(value, *after):
    anywhere = pl.BlockSpec(memory_space=pl.ANY)
    return pl.pallas_call(
        lambda *refs: None,
        out_shape=jax.ShapeDtypeStruct(value.shape, value.dtype),
        in_specs=[anywhere] * (1 + len(after)),
        out_specs=anywhere,
        input_output_aliases={0: 0},
        compiler_params=pltpu.CompilerParams(vmem_limit_bytes=16 * MIB),
        cost_estimate=SMALL,
        name="tie",
    )(value, *after)


def stack_kernel(info, first, second, third, fourth, out):
    for at, ref in enumerate((first, second, third, fourth)):
        out[info[PLANE] ^ at] = ref[...]


def put_halves(info, keep, send, value):
    size = keep.shape[0]

    @pl.when(info[HALF] == 0)
    def _():
        keep[...] = value[:size]
        send[...] = value[size:]

    @pl.when(info[HALF] == 1)
    def _():
        keep[...] = value[size:]
        send[...] = value[:size]


def put_slots(info, outs, value, empty):
    for at, out in enumerate(outs):
        here = info[SLOT] == (info[UNIT] ^ at)

        @pl.when(here)
        def _(out=out):
            out[...] = value

        @pl.when(jnp.logical_not(here))
        def _(out=out):
            out[...] = empty


def blend_values(given, sel, width):
    lses = [dot(c[:, width:], sel[0]) for c in given]
    top = lses[0]
    for lse in lses[1:]:
        top = jnp.maximum(top, lse)
    shares = [jnp.exp(lse - top) for lse in lses]
    total = shares[0]
    for share in shares[1:]:
        total = total + share
    inv = 1.0 / total
    low = lax.broadcasted_iota(jnp.int32, (1, TILE), 1) < HD
    tiles = []
    for pair in range(width // TILE):
        cols = slice(pair * TILE, (pair + 1) * TILE)
        ctx = None
        for share, c in zip(shares, given):
            share = share * inv
            weight = jnp.where(
                low, share[:, 2 * pair : 2 * pair + 1], share[:, 2 * pair + 1 : 2 * pair + 2]
            )
            term = weight * c[:, cols].astype(F32)
            ctx = term if ctx is None else ctx + term
        tiles.append(ctx.astype(BF))
    return tiles, top + jnp.log(total)


def blend_kernel(info, keep, got, sel, *outs):
    outs, value = outs[:SLOTS], outs[SLOTS]
    width = value.shape[1] - TILE
    heads = width // HD
    tiles, lse = blend_values((keep, got), sel, width)
    for pair, tile in enumerate(tiles):
        value[:, pair * TILE : (pair + 1) * TILE] = tile
    value[:, width:] = as_parts(lse, heads).astype(BF)
    col = lax.broadcasted_iota(jnp.int32, value.shape, 1)
    fill = jnp.where((col >= width) & (col < width + heads), NEG_FILL, 0.0)
    put_slots(info, outs, value[...], fill.astype(BF))


def sum_kernel(info, keep, got, *outs):
    total = (keep[...].astype(F32) + got[...].astype(F32)).astype(BF)
    put_slots(info, outs, total, jnp.zeros(total.shape, BF))


def start_weights(info, pieces, held, sems, mats=(0, 1)):
    planes = held.shape[2]
    for mat in mats:
        for j in range(4):
            mine = (info[ROLE], info[WALK + j], pieces[j])
            theirs = (1 - info[ROLE], info[OTHER_WALK + j], pieces[4 + j])
            for role, unit, piece in (mine, theirs):
                for plane in range(planes):
                    pltpu.make_async_copy(
                        piece.at[mat, plane],
                        held.at[role, mat, plane, unit],
                        sems.at[role, mat, j * planes + plane],
                    ).start()


def weight(held, sems, pieces, role, mat):
    planes = held.shape[2]
    for j in range(4):
        for plane in range(planes):
            pltpu.make_async_copy(
                pieces[j].at[mat, plane],
                held.at[role, mat, plane, j],
                sems.at[role, mat, j * planes + plane],
            ).wait()
    return matrix(held, role, mat)


def matrix(held, *index):
    block = held[index]
    return block.reshape(-1, block.shape[-1])


def half_masks():
    lane = lax.broadcasted_iota(jnp.int32, (1, TILE), 1)
    low = (lane < HD).astype(F32).astype(BF)
    return low, (lane >= HD).astype(F32).astype(BF)


def put_scalars(rows):
    count = len(rows)
    stack = jnp.concatenate(rows * PARTS, axis=0)
    extra = TILE - stack.shape[0]
    stack = jnp.concatenate([stack, jnp.zeros((extra, stack.shape[1]), F32)], axis=0)
    return stack.T


def as_parts(wide, heads, offset=0):
    first = wide.astype(BF).astype(F32)
    rest = wide - first
    second = rest.astype(BF).astype(F32)
    third = rest - second
    lane = lax.broadcasted_iota(jnp.int32, wide.shape, 1) - offset
    return jnp.where(
        lane < 0,
        0.0,
        jnp.where(
            lane < heads,
            first,
            jnp.where(lane < 2 * heads, second, jnp.where(lane < 3 * heads, third, 0.0)),
        ),
    )


def norm_stats(summed):
    centre = summed - jnp.mean(summed, axis=-1, keepdims=True)
    inv = lax.rsqrt(jnp.mean(centre * centre, axis=-1, keepdims=True) + EPSILON)
    return centre * inv, inv


def norm_pull(upstream, normed, inv, gain):
    scaled = upstream * gain
    return inv * (
        scaled
        - jnp.mean(scaled, axis=-1, keepdims=True)
        - normed * jnp.mean(scaled * normed, axis=-1, keepdims=True)
    )


def head_forward(q_tile, k_tile, v_tile, masks):
    parts, rows = [], []
    for side in range(2):
        scores = dot_nt(k_tile * masks[side], q_tile)
        top = jnp.max(scores, axis=0, keepdims=True)
        weights = jnp.exp(scores - top)
        den = jnp.sum(weights, axis=0, keepdims=True)
        num = dot_tn(v_tile, weights.astype(BF))[side * HD : (side + 1) * HD]
        parts.append(num * (1.0 / den))
        rows.append(top + jnp.log(den))
    return jnp.concatenate(parts, axis=0), rows


def head_backward(q_tile, k_tile, v_tile, g_tile, lses, deltas, masks):
    dq, dk, dv = [], None, None
    for side in range(2):
        q_side, g_side = q_tile * masks[side], g_tile * masks[side]
        weights = jnp.exp(dot_nt(k_tile, q_side) - lses[side])
        dscores = (weights * (dot_nt(v_tile, g_side) - deltas[side])).astype(BF)
        weights = weights.astype(BF)
        dq.append(dot_tn(k_tile, dscores)[side * HD : (side + 1) * HD])
        dk_side, dv_side = dot(dscores, q_side), dot(weights, g_side)
        dk = dk_side if dk is None else dk + dk_side
        dv = dv_side if dv is None else dv + dv_side
    return jnp.concatenate(dq, axis=0), dk, dv


def pack_forward_kernel(
    info, tok, mem, *refs
):
    pieces, (k_out, v_out, q_out, keep, send, packed, held, sems) = refs[:8], refs[8:]
    width = tok.shape[1]
    heads = width // HD
    start_weights(info, pieces, held, sems)
    k_out[...] = dot_nt(tok[...], weight(held, sems, pieces, 0, 0)).astype(BF)
    v_out[...] = dot_nt(tok[...], weight(held, sems, pieces, 0, 1)).astype(BF)
    q_out[...] = dot_nt(mem[...], weight(held, sems, pieces, 1, 0)).astype(BF) * BF(HD**-0.5)
    masks = half_masks()
    rows = []
    for pair in range(heads // 2):
        cols = slice(pair * TILE, (pair + 1) * TILE)
        ctx, pair_rows = head_forward(q_out[:, cols], k_out[:, cols], v_out[:, cols], masks)
        packed[:, cols] = ctx.T.astype(BF)
        rows += pair_rows
    packed[:, width:] = as_parts(put_scalars(rows), heads).astype(BF)
    put_halves(info, keep, send, packed)
    weight(held, sems, pieces, 1, 1)


def start_out_matrix(info, pieces, held, sems):
    planes = held.shape[0]
    for j in range(4):
        for role, piece, unit in ((1, pieces[j], WALK + j), (0, pieces[4 + j], OTHER_WALK + j)):

            @pl.when(info[ROLE] == role)
            def _(piece=piece, unit=unit, j=j):
                for plane in range(planes):
                    pltpu.make_async_copy(
                        piece.at[1, plane], held.at[plane, info[unit]], sems.at[j * planes + plane]
                    ).start()


def out_matrix(pieces, held, sems):
    planes = held.shape[0]
    for j in range(4):
        for plane in range(planes):
            pltpu.make_async_copy(
                pieces[j].at[1, plane], held.at[plane, j], sems.at[j * planes + plane]
            ).wait()
    return matrix(held, Ellipsis)


def memory_kernel(info, c0, c1, c2, c3, sel, mem, cot, gain, bias, *refs):
    pieces, outs = refs[:8], refs[8:]
    result, mix_low, ctx_out, lse_out, grad_sum, vectors, held, sems = outs
    width = mem.shape[1]
    heads = width // HD
    start_out_matrix(info, pieces, held, sems)
    tiles, lse = blend_values((c0, c1, c2, c3), sel, width)
    lse_out[...] = lse
    for pair, tile in enumerate(tiles):
        ctx_out[:, pair * TILE : (pair + 1) * TILE] = tile
    mix = dot(ctx_out[...], out_matrix(pieces, held, sems))
    mix_low[...] = mix.astype(BF)
    normed, inv_std = norm_stats(mix + mem[...].astype(F32))
    gain_row = gain[...][None]
    result[...] = (normed * gain_row + bias[...][None]).astype(BF)
    upstream = cot[...].astype(F32)
    grad_sum[...] = norm_pull(upstream, normed, inv_std, gain_row)
    vectors[0:1] = jnp.sum(upstream * normed, axis=0, keepdims=True)
    vectors[1:2] = jnp.sum(upstream, axis=0, keepdims=True)


def unpack_forward_kernel(info, tok, mix, *refs):
    pieces, outs = refs[:8], refs[8:]
    k_out, v_out, q_out, ctx_out, lse_out, normed_out, inv_out, held, sems = outs
    width = tok.shape[1]
    heads = width // HD
    start_weights(info, pieces, held, sems)
    k_out[...] = dot_nt(mix[...], weight(held, sems, pieces, 0, 0)).astype(BF)
    v_out[...] = dot_nt(mix[...], weight(held, sems, pieces, 0, 1)).astype(BF)
    q_out[...] = dot_nt(tok[...], weight(held, sems, pieces, 1, 0)).astype(BF) * BF(HD**-0.5)
    masks = half_masks()
    for pair in range(heads // 2):
        cols = slice(pair * TILE, (pair + 1) * TILE)
        ctx, rows = head_forward(q_out[:, cols], k_out[:, cols], v_out[:, cols], masks)
        ctx_out[:, cols] = ctx.T.astype(BF)
        lse_out[2 * pair : 2 * pair + 1] = rows[0]
        lse_out[2 * pair + 1 : 2 * pair + 2] = rows[1]
    summed = dot(ctx_out[...], weight(held, sems, pieces, 1, 1)) + tok[...].astype(F32)
    normed, inv = norm_stats(summed)
    normed_out[...] = normed
    inv_out[...] = inv


GELU_A = math.sqrt(2.0 / math.pi)
GELU_B = 0.044715
CHUNK = 256


def start_ffn(info, pieces, held, sems):
    planes, rows = held.shape[1], held.shape[2]
    quarter = rows // 4
    for plane in range(planes):
        for j, role in enumerate((info[ROLE], 1 - info[ROLE])):
            for part in range(4):
                at = pl.ds(part * quarter, quarter)
                pltpu.make_async_copy(
                    pieces[j].at[plane, at], held.at[role, plane, at], sems.at[plane, 4 * j + part]
                ).start()


def wait_ffn(pieces, held, sems, plane):
    rows = held.shape[2]
    quarter = rows // 4
    for j in range(2):
        for part in range(4):
            at = pl.ds(part * quarter, quarter)
            pltpu.make_async_copy(
                pieces[j].at[0, at], held.at[j, plane, at], sems.at[plane, 4 * j + part]
            ).wait()


def ffn_kernel(info, normed_in, inv_in, cot, mem_result, *refs):
    rows, refs = [r[...][None] for r in refs[:5]], refs[5:]
    attn_gain, attn_bias, out_gain, out_bias, ffn_bias = rows
    pieces, outs = refs[:2], refs[2:]
    out, attn_low, ffn_grad, mix_grad, mix_sum, vectors, hid_vec, gelu_out, hid_out = outs[:9]
    held, bias, total, gelu_low, slope, sems, bias_sem, out_sems = outs[9:]
    planes, width = held.shape[1], held.shape[2]
    bias_at = pl.ds(width, 16)
    bias_copies = [
        pltpu.make_async_copy(pieces[0].at[plane, bias_at], bias.at[plane], bias_sem.at[plane])
        for plane in range(planes)
    ]
    for copy in bias_copies:
        copy.start()
    start_ffn(info, pieces, held, sems)
    attn = normed_in[...] * attn_gain + attn_bias
    attn_low[...] = attn.astype(BF)
    total[...] = attn + ffn_bias
    for copy in bias_copies:
        copy.wait()
    out_copies = []
    for plane in range(planes):
        wait_ffn(pieces, held, sems, plane)
        parts = bias[plane].astype(F32)
        shift = parts[0:1] + parts[1:2] + parts[2:3]
        for start in range(0, held.shape[3], CHUNK):
            cols = slice(start, start + CHUNK)
            hidden = dot(attn_low[...], held[0, plane, :, cols]) + shift[:, cols]
            square = hidden * hidden
            half = 1.0 / (1.0 + jnp.exp(hidden * (-2.0 * GELU_A - 2.0 * GELU_A * GELU_B * square)))
            gelu = hidden * half
            gelu_low[plane, :, cols] = gelu.astype(BF)
            inner = 2.0 * GELU_A + 6.0 * GELU_A * GELU_B * square
            slope[plane, :, cols] = (half + gelu * (1.0 - half) * inner).astype(BF)
        total[...] += dot(gelu_low[plane], held[1, plane])
        copy = pltpu.make_async_copy(gelu_low.at[plane], gelu_out.at[plane], out_sems.at[plane, 0])
        copy.start()
        out_copies.append(copy)
    out_normed, out_inv = norm_stats(total[...])
    count = normed_in.shape[0]
    out[:count] = (out_normed * out_gain + out_bias).astype(BF)
    out[count:] = mem_result[...]
    upstream = cot[...].astype(F32)
    grad = norm_pull(upstream, out_normed, out_inv, out_gain)
    ffn_grad[...] = grad.astype(BF)
    vectors[0:1] = jnp.sum(grad.astype(BF).astype(F32), axis=0, keepdims=True)
    vectors[1:2] = jnp.sum(upstream * out_normed, axis=0, keepdims=True)
    vectors[2:3] = jnp.sum(upstream, axis=0, keepdims=True)
    total[...] = grad
    for plane in range(planes):
        for start in range(0, held.shape[3], CHUNK):
            cols = slice(start, start + CHUNK)
            pulled = dot_nt(ffn_grad[...], held[1, plane, cols]) * slope[plane, :, cols].astype(F32)
            low = pulled.astype(BF)
            slope[plane, :, cols] = low
            hid_vec[plane, :, cols] = jnp.sum(low.astype(F32), axis=0, keepdims=True)
        total[...] += dot_nt(slope[plane], held[0, plane])
        copy = pltpu.make_async_copy(slope.at[plane], hid_out.at[plane], out_sems.at[plane, 1])
        copy.start()
        out_copies.append(copy)
    upstream = total[...]
    normed = normed_in[...]
    vectors[3:4] = jnp.sum(upstream * normed, axis=0, keepdims=True)
    vectors[4:5] = jnp.sum(upstream, axis=0, keepdims=True)
    grad = norm_pull(upstream, normed, inv_in[...], attn_gain)
    mix_sum[...] = grad
    mix_grad[...] = grad.astype(BF)
    for copy in out_copies:
        copy.wait()


def unpack_backward_kernel(info, q_in, k_in, v_in, ctx, lse, mix_grad, mix_sum, *refs):
    pieces, outs = refs[:8], refs[8:]
    uq, uk, uv, keep, send, tok_part, held, sems = outs
    width = q_in.shape[1]
    heads = width // HD
    start_weights(info, pieces, held, sems, (1, 0))
    masks = half_masks()
    ctx_grad = dot_nt(mix_grad[...], weight(held, sems, pieces, 1, 1))
    ctx_low = ctx_grad.astype(BF)
    for pair in range(heads // 2):
        cols = slice(pair * TILE, (pair + 1) * TILE)
        product = ctx_grad[:, cols] * ctx[:, cols].astype(F32)
        first = product.astype(BF)
        second = (product - first.astype(F32)).astype(BF)
        deltas = []
        for side in range(2):
            picker = jnp.broadcast_to(masks[side], (16, TILE))
            deltas.append((dot_nt(picker, first) + dot_nt(picker, second))[0:1])
        lses = [lse[2 * pair : 2 * pair + 1], lse[2 * pair + 1 : 2 * pair + 2]]
        dq, dk, dv = head_backward(
            q_in[:, cols], k_in[:, cols], v_in[:, cols], ctx_low[:, cols], lses, deltas, masks
        )
        uq[:, cols] = (dq.T * (HD**-0.5)).astype(BF)
        uk[:, cols] = dk.astype(BF)
        uv[:, cols] = dv.astype(BF)
    mix_part = dot(uk[...], weight(held, sems, pieces, 0, 0))
    mix_part = mix_part + dot(uv[...], weight(held, sems, pieces, 0, 1))
    put_halves(info, keep, send, mix_part.astype(BF))
    tok_part[...] = mix_sum[...] + dot(uq[...], weight(held, sems, pieces, 1, 0))


def memory_back_kernel(info, c0, c1, c2, c3, sel, grad_sum, ctx, lse, *refs):
    pieces, outs = refs[:8], refs[8:]
    mix_grad, packed, held, sems = outs
    width = ctx.shape[1]
    heads = width // HD
    start_out_matrix(info, pieces, held, sems)
    total = grad_sum[...]
    for c in (c0, c1, c2, c3):
        total = total + c[...].astype(F32)
    mix_grad[...] = total.astype(BF)
    pulled = dot_nt(mix_grad[...], out_matrix(pieces, held, sems))
    packed[:, :width] = pulled.astype(BF)
    delta = jnp.zeros(lse.shape, F32)
    for pair in range(heads // 2):
        cols = slice(pair * TILE, (pair + 1) * TILE)
        product = pulled[:, cols] * ctx[:, cols].astype(F32)
        first = product.astype(BF)
        second = (product - first.astype(F32)).astype(BF)
        delta = delta + dot(first, sel[2 + pair]) + dot(second, sel[2 + pair])
    scalars = as_parts(lse[...], heads) + as_parts(delta, heads, PARTS * heads)
    packed[:, width:] = scalars.astype(BF)


def pack_backward_kernel(info, back, sel, q_in, k_in, v_in, tok_part, *refs):
    pieces, outs = refs[:8], refs[8:]
    pq, pk, pv, tok_grad, keep, send, held, sems = outs
    width = q_in.shape[1]
    heads = width // HD
    start_weights(info, pieces, held, sems)
    masks = half_masks()
    lse = dot(back[:, width:], sel[0]).T
    delta = dot(back[:, width:], sel[1]).T
    for pair in range(heads // 2):
        cols = slice(pair * TILE, (pair + 1) * TILE)
        lses = [lse[2 * pair : 2 * pair + 1], lse[2 * pair + 1 : 2 * pair + 2]]
        deltas = [delta[2 * pair : 2 * pair + 1], delta[2 * pair + 1 : 2 * pair + 2]]
        dq, dk, dv = head_backward(
            q_in[:, cols], k_in[:, cols], v_in[:, cols], back[:, cols], lses, deltas, masks
        )
        pq[:, cols] = (dq.T * (HD**-0.5)).astype(BF)
        pk[:, cols] = dk.astype(BF)
        pv[:, cols] = dv.astype(BF)
    total = dot(pk[...], weight(held, sems, pieces, 0, 0))
    total = total + dot(pv[...], weight(held, sems, pieces, 0, 1))
    tok_grad[...] = (total + tok_part[...]).astype(BF)
    put_halves(info, keep, send, dot(pq[...], weight(held, sems, pieces, 1, 0)).astype(BF))
    weight(held, sems, pieces, 1, 1)


def selectors(width):
    heads = width // HD
    lane = np.arange(TILE)
    inside = lane < PARTS * heads
    first = inside[:, None] & inside[None, :] & (lane[:, None] % heads == lane[None, :] % heads)
    shifted = lane - PARTS * heads
    second = (shifted >= 0) & (shifted < PARTS * heads)
    second = second[:, None] & inside[None, :] & (shifted[:, None] % heads == lane[None, :] % heads)
    rows = [first, second]
    target = (shifted >= 0) & (shifted < PARTS * heads)
    for pair in range(heads // 2):
        head = 2 * pair + (lane >= HD)
        rows.append(target[None, :] & (head[:, None] == (shifted % heads)[None, :]))
    return jnp.asarray(np.stack(rows).astype(np.float32), BF)


def pair_units(info):
    role, quad = info[ROLE], info[WALK]
    bit = jnp.where(role == 0, lax.rem(quad, 2), quad // 2)
    step, scale = jnp.where(role == 0, 2, 1), jnp.where(role == 0, 1, 2)
    keep = [bit * scale + at * step for at in range(2)]
    send = [(1 - bit) * scale + at * step for at in range(2)]
    return keep, send


def split_pairs(info, value, keep, send, rows):
    for units, out in zip(pair_units(info), (keep, send)):
        for at, unit in enumerate(units):
            out[at, 0] = value[pl.ds(pl.multiple_of(unit * rows, rows), rows)]


def ffn_weight_grad(info, role, operands, added, after=()):
    attn_low, hid_grad, gelu_out, ffn_grad = operands
    planes, rows, cols = hid_grad.shape
    width = attn_low.shape[1]
    quarter, half = width // 4, planes // 2

    def kernel(which, info, attn_ref, hid_ref, gelu_ref, grad_ref, *refs):
        plane = pl.program_id(0)
        refs = refs[len(after) :] if added is None else refs[:2] + refs[2 + len(after) :]

        def put(value):
            for side in range(2):

                @pl.when(plane // half == side)
                def _(side=side):
                    if added is None:
                        refs[side][0] = value.astype(BF)
                    else:
                        recv, held = refs[side], refs[6]
                        held[...] = (value + recv[0].astype(F32)).astype(BF)
                        keep, send = refs[2 + 2 * side : 4 + 2 * side]
                        split_pairs(info, held, keep, send, quarter)

        @pl.when(which[0] == 0)
        def _():
            put(dot_tn(attn_ref[...], hid_ref[0]))

        @pl.when(which[0] == 1)
        def _():
            put(dot_tn(gelu_ref[0], grad_ref[...]))

    vm, sm = pl.BlockSpec(memory_space=pltpu.VMEM), pl.BlockSpec(memory_space=pltpu.SMEM)
    blocks = [
        pl.BlockSpec((1, width, cols), lambda i, w: (jnp.minimum(i, half - 1), 0, 0)),
        pl.BlockSpec((1, width, cols), lambda i, w: (jnp.maximum(i - half, 0), 0, 0)),
    ]
    pairs = [
        pl.BlockSpec((2, 1, quarter, cols), lambda i, w: (0, jnp.minimum(i, half - 1), 0, 0)),
        pl.BlockSpec((2, 1, quarter, cols), lambda i, w: (0, jnp.maximum(i - half, 0), 0, 0)),
    ]
    pair_shape = jax.ShapeDtypeStruct((2, half, quarter, cols), BF)
    hid_block = pl.BlockSpec((1, rows, cols), lambda i, w: (i * (1 - w[0]), 0, 0))
    gelu_block = pl.BlockSpec((1, rows, cols), lambda i, w: (i * w[0], 0, 0))
    args = [role, info, attn_low, hid_grad, gelu_out, ffn_grad]
    specs = [sm, vm, hid_block, gelu_block, vm]
    if added is not None:
        args += added
        specs += blocks
    return pl.pallas_call(
        kernel,
        out_shape=(
            [jax.ShapeDtypeStruct((half, width, cols), BF)] * 2
            if added is None
            else [pair_shape] * 4
        ),
        grid_spec=pltpu.PrefetchScalarGridSpec(
            num_scalar_prefetch=1,
            grid=(planes,),
            in_specs=specs + [pl.BlockSpec(memory_space=pl.ANY)] * len(after),
            out_specs=blocks if added is None else [pairs[0], pairs[0], pairs[1], pairs[1]],
            scratch_shapes=[] if added is None else [pltpu.VMEM((width, cols), BF)],
        ),
        compiler_params=pltpu.CompilerParams(vmem_limit_bytes=60 * MIB),
        cost_estimate=SMALL,
        name="ffn_weight_grad",
    )(*args, *after)


def attention_weight_grad(info, role, operands, planes, added, after=()):
    width = operands[0].shape[1]
    quarter = width // 4
    size = quarter // planes

    def kernel(info, which, kv, dk, dv, q_rows, dq, left, right, *refs):
        def put(mat, value, by_plane=False):
            if added is None:
                out, value = refs[0].at[mat], value.astype(BF)
            else:
                out = refs[3].at[mat]
            if by_plane:
                for plane in range(planes):
                    for quad in range(4):
                        at, to = (plane * 4 + quad) * size, (quad * planes + plane) * size
                        piece = value[at : at + size]
                        if added is not None:
                            piece = piece + refs[0][mat, to : to + size].astype(F32)
                        out[to : to + size] = piece.astype(BF)
            else:
                if added is not None:
                    value = value + refs[0][mat].astype(F32)
                out[...] = value.astype(BF)

        @pl.when(which[0] == 0)
        def _():
            put(0, dot_tn(kv[...], dk[...]))
            put(1, dot_tn(kv[...], dv[...]))

        @pl.when(which[0] == 1)
        def _():
            put(0, dot_tn(q_rows[...], dq[...]))
            put(1, dot_tn(left[...], right[...]), True)

        if added is not None:
            for mat in range(2):
                keep, send = refs[1].at[:, mat : mat + 1], refs[2].at[:, mat : mat + 1]
                split_pairs(info, refs[3].at[mat], keep, send, quarter)

    rows = operands[0].shape[0] + operands[3].shape[0]
    operands = [info, role] + list(operands)
    outs = [((2, width, width), BF)]
    scratch = []
    if added is not None:
        operands.append(added)
        outs = [((2, 2, quarter, width), BF)] * 2
        scratch = [pltpu.VMEM((2, width, width), BF)]
    result = call(
        kernel,
        "attention_weight_grad",
        operands,
        outs,
        scratch=scratch,
        flops=2 * rows * width * width,
        smem=2,
        after=after,
    )
    return result[0] if added is None else result


def add_pairs(info, kept, got, after=()):
    _, mats, rows, cols = kept.shape

    def kernel(info, kept_ref, got_ref, *refs):
        keep, send = refs[len(after) :]
        quad = info[WALK]
        at = jnp.where(info[ROLE] == 0, quad // 2, lax.rem(quad, 2))
        for index, out in ((at, keep), (1 - at, send)):
            out[0] = (kept_ref[index, 0].astype(F32) + got_ref[index, 0].astype(F32)).astype(BF)

    pairs = pl.BlockSpec((2, 1, rows, cols), lambda i: (0, i, 0, 0))
    one = pl.BlockSpec((1, rows, cols), lambda i: (i, 0, 0))
    return pl.pallas_call(
        kernel,
        grid=(mats,),
        out_shape=[jax.ShapeDtypeStruct((mats, rows, cols), BF)] * 2,
        in_specs=[pl.BlockSpec(memory_space=pltpu.SMEM), pairs, pairs]
        + [pl.BlockSpec(memory_space=pl.ANY)] * len(after),
        out_specs=[one, one],
        compiler_params=pltpu.CompilerParams(vmem_limit_bytes=16 * MIB),
        cost_estimate=SMALL,
        name="add_pairs",
    )(info, kept, got, *after)


def put_planes(info, held, keep, send):
    kind = lax.rem(info[PLANE], 2)
    for at in range(held.shape[0] // 2):
        keep[at] = held[2 * at + kind].astype(keep.dtype)
        send[at] = held[2 * at + 1 - kind].astype(send.dtype)


def ffn_blocks_kernel(info, kept_low, got_low, kept_high, got_high, keep, send):
    kind = lax.rem(info[PLANE], 2)
    for at, (kept, got) in enumerate(((kept_low, got_low), (kept_high, got_high))):
        for plane, out in ((kind, keep), (1 - kind, send)):
            out[at] = (kept[plane].astype(F32) + got[plane].astype(F32)).astype(out.dtype)


def attention_blocks_kernel(info, kept, got, keep, send, total, held):
    planes, _, rows, cols = held.shape
    size = rows // planes
    total[...] = kept[...].astype(F32) + got[...].astype(F32)
    for plane in range(planes):
        held[plane, 0] = total[0, :, plane * cols : (plane + 1) * cols]

    @pl.when(info[ROLE] == 0)
    def _():
        for plane in range(planes):
            held[plane, 1] = total[1, :, plane * cols : (plane + 1) * cols]

    @pl.when(info[ROLE] == 1)
    def _():
        for plane in range(planes):
            for at in range(planes):
                held[plane, 1, at * size : (at + 1) * size] = total[
                    1, plane * size : (plane + 1) * size, at * cols : (at + 1) * cols
                ]

    put_planes(info, held, keep, send)


def middle_kernel(info, kept, got, keep, send):
    mine = info[PLANE] // 2
    keep[...] = kept[mine] + got[mine].astype(F32)
    send[...] = (kept[1 - mine] + got[1 - mine].astype(F32)).astype(BF)


def ffn_total_kernel(info, own, other, keep, send, total):
    total[...] = own[...] + other[...].astype(F32)
    half = keep.shape[0]
    for index, out in ((info[ROLE], keep), (1 - info[ROLE], send)):
        out[...] = total[pl.ds(pl.multiple_of(index * half, half), half)]


def attention_total_kernel(info, own, other, keep, send, total, planes):
    total[...] = own[...] + other[...].astype(F32)
    half = keep.shape[1]
    for index, out in ((info[ROLE], keep), (1 - info[ROLE], send)):
        at = pl.ds(pl.multiple_of(index * half, half), half)
        out[0] = total[0, at]

        @pl.when(info[ROLE] == 0)
        def _(out=out, at=at):
            out[1] = total[1, at]

        @pl.when(info[ROLE] == 1)
        def _(out=out, index=index):
            size = half // planes
            for chunk in range(planes):
                start = pl.multiple_of(2 * chunk * size + index * size, size)
                out[1, chunk * size : (chunk + 1) * size] = total[1, pl.ds(start, size)]


def attention_final_kernel(info, kept, got, key_g, value_g, query_g, out_g, planes):
    def put(zero, one):
        key_g[...] = zero[0]
        value_g[...] = zero[1]
        query_g[...] = one[0]
        size = out_g.shape[0]
        chunks = [one[1, at * size : (at + 1) * size] for at in range(planes)]
        out_g[...] = jnp.concatenate(chunks, axis=1)

    @pl.when(info[ROLE] == 0)
    def _():
        put(kept, got)

    @pl.when(info[ROLE] == 1)
    def _():
        put(got, kept)


def ffn_final_kernel(info, kept, got, in_g, out_g):
    @pl.when(info[ROLE] == 0)
    def _():
        in_g[...] = kept[...]
        out_g[...] = got[...]

    @pl.when(info[ROLE] == 1)
    def _():
        in_g[...] = got[...]
        out_g[...] = kept[...]


def empty_row(width):
    heads = width // HD
    row = np.zeros((1, width + TILE), np.float32)
    row[:, width : width + heads] = NEG_FILL
    return jnp.asarray(row)


def blend_two_kernel(info, keep, got, sel, value):
    width = value.shape[1] - TILE
    tiles, lse = blend_values((keep, got), sel, width)
    for pair, tile in enumerate(tiles):
        value[:, pair * TILE : (pair + 1) * TILE] = tile
    value[:, width:] = as_parts(lse, width // HD).astype(BF)


def first_pieces(places, lengths, memory, weights, unit, block_len):
    sm, vm = pl.BlockSpec(memory_space=pltpu.SMEM), pl.BlockSpec(memory_space=pltpu.VMEM)
    rows, width = weights[0].shape
    return pl.pallas_call(
        functools.partial(first_pieces_kernel, unit=unit, block_len=block_len),
        out_shape=[
            jax.ShapeDtypeStruct((INFO,), jnp.int32),
            jax.ShapeDtypeStruct((4, rows // 4, width), BF),
            jax.ShapeDtypeStruct(memory.shape[1:], BF),
        ],
        in_specs=[sm, sm] + [pl.BlockSpec(memory_space=pl.ANY)] * 9,
        out_specs=[sm, vm, vm],
        scratch_shapes=[pltpu.SemaphoreType.DMA((5,))],
        compiler_params=pltpu.CompilerParams(vmem_limit_bytes=60 * MIB),
        cost_estimate=SMALL,
        name="first_pieces",
    )(places, lengths, memory, *weights)


def make_local(axis_seq, axis_head):
    unit = axis_seq // SLOTS
    fast = axis_seq == 8

    def swap(value, step):
        return lax.ppermute(value, "seq", [(i, i ^ step) for i in range(axis_seq)])

    def cross(value, order):
        steps = (2, 4) if order == 0 else (4, 2)
        return lax.ppermute(value, "seq", [(i, i ^ steps[i % 2]) for i in range(axis_seq)])

    def over(value, step):
        return lax.ppermute(value, "head", [(i, i ^ step) for i in range(axis_head)])

    def from_planes(value):
        got = [value]
        step = 1
        while step < axis_head:
            got += [over(value, step) if part is value else over(part, step) for part in got]
            step *= 2
        return got

    def direct_planes(value):
        return [value] + [over(value, step) for step in range(1, axis_head)]

    def local(
        tokens,
        memory,
        seq_lengths,
        pack_query,
        pack_key,
        pack_value,
        pack_out,
        unpack_query,
        unpack_key,
        unpack_value,
        unpack_out,
        ffn_in,
        ffn_in_bias,
        ffn_out,
        ffn_out_bias,
        mem_gain,
        mem_bias,
        attn_gain,
        attn_bias,
        out_gain,
        out_bias,
        cot_tokens,
        cot_memory,
    ):
        seq_index = lax.axis_index("seq")
        head_index = lax.axis_index("head")
        _, block_len, width = tokens.shape
        hidden_width = ffn_in.shape[1]
        my_lane, role = seq_index % unit, seq_index % 2
        quarter, head_cols = width // 4, width // axis_head
        info, pieces, mem = first_pieces(
            jnp.stack([seq_index, head_index]),
            seq_lengths,
            memory,
            [pack_key.T, pack_value.T, pack_query.T, pack_out]
            + [unpack_key.T, unpack_value.T, unpack_query.T, unpack_out],
            unit,
            block_len,
        )
        last = []

        def run(kernel, name, operands, outs, also=(), **more):
            after = list(last) + list(also)
            result = call(kernel, name, [info] + operands, outs, after=after, **more)
            last[:] = [result[0]]
            return result

        def run_grid(function, *operands):
            result = function(info, *operands, after=list(last))
            last[:] = [result[0] if isinstance(result, (list, tuple)) else result]
            return result

        def mine(value):
            return lax.dynamic_index_in_dim(value, head_index, 0, keepdims=False)

        def gather_unit(value):
            step = 1
            while step < unit:
                other = swap(value, step)
                low = (my_lane // step) % 2 == 0
                value = jnp.concatenate(
                    [jnp.where(low, value, other), jnp.where(low, other, value)], axis=0
                )
                step *= 2
            return value

        def scatter_unit(value, add, step):
            while step >= 1:
                half = value.shape[0] // 2
                low = (my_lane // step) % 2 == 0
                keep = jnp.where(low, value[:half], value[half:])
                send = jnp.where(low, value[half:], value[:half])
                value = add([keep, swap(send, step)])
                step //= 2
            return value

        def fetch_start(value):
            return [value] + [swap(value, j * unit) for j in range(1, SLOTS)]

        def fetch_finish(parts, also=()):
            shapes = [(parts[0].shape, BF)]
            sem = [pltpu.SemaphoreType.DMA]
            return run(pick_kernel, "pick_slot", parts, shapes, anys=SLOTS, scratch=sem, also=also)[0]

        def sum_rows(values):
            total = values[0].astype(F32)
            for value in values[1:]:
                total = total + value.astype(F32)
            return total.astype(BF)

        packed_width = width + TILE
        row_count = memory.shape[1]
        slot_count = unit * row_count
        half_rows = slot_count // 2
        sel = selectors(width)
        deep = [((row_count, packed_width), BF)] * SLOTS
        flat = [((row_count, width), BF)] * SLOTS

        def blend_two(values):
            return run(blend_two_kernel, "blend", values + [sel], [(values[0].shape, BF)])[0]

        def to_slots(keep, got, kernel, extra, outs, add, empty, also=()):
            if unit > 2:
                keep = scatter_unit(add([keep, got]), add, unit // 4)
                got = jnp.broadcast_to(empty, keep.shape).astype(BF)
            scratch = [pltpu.VMEM(keep.shape, BF)] if extra else []
            parts = run(kernel, "to_slots", [keep, got] + extra, outs, scratch=scratch, also=also)
            return [parts[0]] + [swap(parts[j], j * unit) for j in range(1, SLOTS)]

        def spread(piece, first, second, third):
            parts = [piece, first, second, third]
            return parts + [swap(part, 1) for part in parts]

        def all_planes(pieces):
            return run(
                stack_kernel, "all_planes", pieces, [((axis_head,) + pieces[0].shape, BF)]
            )[0]

        held_out = pltpu.VMEM((axis_head, 4, head_cols // 4, width), BF)
        held_pair = pltpu.VMEM((2, 2) + held_out.shape, BF)
        pair_sems = pltpu.SemaphoreType.DMA((2, 2, 4 * axis_head))
        out_sems = pltpu.SemaphoreType.DMA((4 * axis_head,))
        ffn_sems = pltpu.SemaphoreType.DMA((axis_head, 8))
        tok_low, slot_low = ((block_len, width), BF), ((slot_count, width), BF)
        row_low, half_low = ((row_count, width), BF), ((half_rows, width), BF)
        tok_f32 = ((block_len, width), F32)

        mem_parts = fetch_start(mem)
        planes = from_planes(pieces)
        piece_ffn, tok, cot_tok, cot_mem = run(
            other_pieces_kernel,
            "other_pieces",
            [ffn_in_bias, ffn_in, ffn_out, tokens, cot_tokens, cot_memory],
            [((width + 16, hidden_width), BF), tok_low, tok_low, row_low],
            anys=5,
            scratch=[pltpu.SemaphoreType.DMA((6,))],
        )
        mem_picked = fetch_finish(mem_parts)
        shape = (2, axis_head) + pieces.shape[1:]
        rows_pack, rows_un = run(planes_kernel, "weight_planes", planes, [(shape, BF)] * 2)

        pack_first, pack_second = cross(rows_pack, 0), cross(rows_pack, 1)
        pack_third = cross(pack_first, 1)
        w_pack = spread(rows_pack, pack_first, pack_second, pack_third)
        rows_un = tie(rows_un, pack_third)
        un_first, un_second = cross(rows_un, 0), cross(rows_un, 1)
        ffn_rows = lax.all_gather(tie(piece_ffn, rows_pack), "head", axis=0)
        mem_slot = gather_unit(mem_picked)
        k_pack, v_pack, q_pack, keep, send = run(
            pack_forward_kernel,
            "pack_forward",
            [tok, mem_slot] + w_pack,
            [tok_low, tok_low, slot_low] + [((half_rows, packed_width), BF)] * 2,
            anys=8,
            scratch=[pltpu.VMEM((slot_count, packed_width), BF), held_pair, pair_sems],
        )
        got = swap(send, unit // 2)
        un_first = tie(un_first, keep)
        w_un = spread(rows_un, un_first, un_second, cross(un_first, 1))
        parts = to_slots(keep, got, blend_kernel, [sel], deep, blend_two, empty_row(width), [un_second])
        mem_result, mix_low, pack_ctx, pack_lse, grad_memsum, mem_vectors = run(
            memory_kernel,
            "memory_rows",
            parts + [sel, mem, cot_mem, mem_gain, mem_bias] + w_pack,
            [row_low, row_low, row_low]
            + [((row_count, TILE), F32), ((row_count, width), F32), ((8, width), F32)],
            anys=8,
            scratch=[held_out, out_sems],
            also=[w_un[3]],
        )
        mix_parts = fetch_start(mix_low)
        mix_picked = fetch_finish(mix_parts, w_un)
        mix_slot = gather_unit(mix_picked)
        ffn_rows = tie(ffn_rows, mix_slot)
        ffn_parts = [ffn_rows, swap(ffn_rows, 1)]
        k_un, v_un, q_un, tok_ctx, tok_lse, attn_normed, attn_inv = run(
            unpack_forward_kernel,
            "unpack_forward",
            [tok, mix_slot] + w_un,
            [slot_low, slot_low, tok_low, tok_low]
            + [((16, block_len), F32), tok_f32, ((block_len, 1), F32)],
            anys=8,
            scratch=[held_pair, pair_sems],
        )
        by_plane = (axis_head, block_len, hidden_width)
        held_ffn = pltpu.VMEM((2, axis_head, width, hidden_width), BF)
        plane_sems = pltpu.SemaphoreType.DMA((axis_head,))
        (
            out_result,
            attn_low,
            ffn_grad,
            mix_grad,
            mix_sum,
            out_vectors,
            hid_vec,
            gelu_out,
            hid_grad,
        ) = run(
            ffn_kernel,
            "ffn",
            [attn_normed, attn_inv, cot_tok, mem_result]
            + [attn_gain, attn_bias, out_gain, out_bias, ffn_out_bias]
            + ffn_parts,
            [((block_len + row_count, width), BF), tok_low, tok_low, tok_low, tok_f32]
            + [((8, width), F32), ((axis_head, 1, hidden_width), F32)]
            + [(by_plane, BF), (by_plane, BF)],
            anys=2,
            out_any=2,
            scratch=[
                held_ffn,
                pltpu.VMEM((axis_head, 16, hidden_width), BF),
                pltpu.VMEM((block_len, width), F32),
                pltpu.VMEM(by_plane, BF),
                pltpu.VMEM(by_plane, BF),
                ffn_sems,
                plane_sems,
                pltpu.SemaphoreType.DMA((axis_head, 2)),
            ],
        )
        out_rows = lax.all_gather(out_result, "head", axis=0)
        out_tokens, out_memory = out_rows[:, :block_len], out_rows[:, block_len:]

        role_info, other_info = role[None], 1 - role[None]
        ffn_operands = (attn_low, hid_grad, gelu_out, ffn_grad)

        def vectors_step(value, other):
            return run(total_kernel, "vectors", [value, other], [(value.shape, F32)])[0]

        small = run(
            vectors_kernel,
            "vectors",
            [mem_vectors, out_vectors, hid_vec],
            [((16, width), F32)],
        )[0]
        small_got = swap(small, 1)
        uq_grad, uk_part, uv_part, keep, send, tok_part = run(
            unpack_backward_kernel,
            "unpack_backward",
            [q_un, k_un, v_un, tok_ctx, tok_lse, mix_grad, mix_sum] + w_un,
            [tok_low, slot_low, slot_low, half_low, half_low, tok_f32],
            anys=8,
            scratch=[held_pair, pair_sems],
        )
        un_operands = (mix_slot, uk_part, uv_part, tok, uq_grad, tok_ctx, mix_grad)
        got = swap(send, unit // 2)
        small = vectors_step(small, small_got)
        small_got = swap(small, 2)
        if fast:
            ffn_sent = run_grid(ffn_weight_grad, other_info, ffn_operands, None)
            ffn_got = [swap(sent, 1) for sent in ffn_sent]
        parts = to_slots(keep, got, sum_kernel, [], flat, sum_rows, jnp.zeros((), BF))
        if fast:
            ffn_low, low_sent, ffn_high, high_sent = run_grid(
                ffn_weight_grad, role_info, ffn_operands, ffn_got
            )
        small = vectors_step(small, small_got)
        mem_mix_grad, packed = run(
            memory_back_kernel,
            "memory_rows_backward",
            parts + [sel, grad_memsum, pack_ctx, pack_lse] + w_pack,
            [row_low, ((row_count, packed_width), BF)],
            anys=8,
            scratch=[held_out, out_sems],
        )
        back_parts = fetch_start(packed)
        if fast:
            un_sent = run_grid(attention_weight_grad, other_info, un_operands, axis_head, None)
        back_picked = fetch_finish(back_parts, [out_rows])
        if fast:
            low_got = cross(tie(low_sent, back_picked), 0)
            un_got = swap(tie(un_sent, back_picked), 1)
        back = gather_unit(back_picked)
        pq_part, pk_grad, pv_grad, grad_tokens, keep, send = run(
            pack_backward_kernel,
            "pack_backward",
            [back, sel, q_pack, k_pack, v_pack, tok_part] + w_pack,
            [slot_low, tok_low, tok_low, tok_low, half_low, half_low],
            anys=8,
            scratch=[held_pair, pair_sems],
        )
        grad_tokens = lax.all_gather(grad_tokens, "head", axis=0)
        pack_operands = (tok, pk_grad, pv_grad, mem_slot, pq_part, pack_ctx, mem_mix_grad)
        got = swap(send, unit // 2)
        if fast:
            ffn_low, low_sent = run_grid(add_pairs, ffn_low, low_got)
            high_got = cross(tie(high_sent, ffn_low), 0)
            un_kept, un_sent = run_grid(
                attention_weight_grad, role_info, un_operands, axis_head, un_got
            )
            pack_sent = run_grid(attention_weight_grad, other_info, pack_operands, axis_head, None)
        step = 4
        while step < axis_seq:
            small = vectors_step(small, swap(small, step))
            step *= 2
        parts = to_slots(keep, got, sum_kernel, [], flat, sum_rows, jnp.zeros((), BF))

        rows = (quarter, hidden_width)
        half = (quarter // 2, hidden_width)
        pair_rows = (2, quarter, head_cols)
        pair_half = (2, quarter // 2, head_cols)

        def pairs_of(shape):
            return [((2,) + shape, F32), ((2,) + shape, BF)]

        def middle(kept, got, shape):
            keep, send = run(
                middle_kernel, "plane_middle", [kept, got], [(shape, F32), (shape, BF)]
            )
            return keep, over(send, 2)

        def ffn_blocks(kept, got):
            operands = [kept[0], got[0], kept[1], got[1]]
            keep, send = run(ffn_blocks_kernel, "plane_blocks", operands, pairs_of(rows))
            return keep, over(send, 1)

        def ffn_total(kept, got):
            scratch = [pltpu.VMEM(rows, F32)]
            keep, send = run(
                ffn_total_kernel, "plane_total", [kept, got], [(half, F32)] * 2, scratch=scratch
            )
            return [keep, swap(send, 1)]

        def ffn_final(halves):
            return run(ffn_final_kernel, "weight_rows", halves, [(half, F32)] * 2)

        def attention_blocks(kept, got):
            keep, send = run(
                attention_blocks_kernel,
                "plane_blocks",
                [kept, got],
                pairs_of(pair_rows),
                scratch=[
                    pltpu.VMEM((2, quarter, width), F32),
                    pltpu.VMEM((axis_head,) + pair_rows, F32),
                ],
            )
            return keep, over(send, 1)

        def attention_total(kept, got):
            keep, send = run(
                functools.partial(attention_total_kernel, planes=axis_head),
                "plane_total",
                [kept, got],
                [(pair_half, F32)] * 2,
                scratch=[pltpu.VMEM(pair_rows, F32)],
            )
            return [keep, swap(send, 1)]

        def attention_final(halves):
            return run(
                functools.partial(attention_final_kernel, planes=axis_head),
                "weight_rows",
                halves,
                [(pair_half[1:], F32)] * 3 + [((quarter // 2 // axis_head, width), F32)],
            )

        def scatter(value, axis, dim):
            return lax.psum_scatter(value, axis, scatter_dimension=dim, tiled=True)

        def by_columns(grad):
            grad = scatter(grad, "seq", 0).reshape(-1, axis_head, head_cols)
            return scatter(grad.transpose(1, 0, 2), "head", 0)[0].astype(F32)

        def by_rows(grad):
            grad = scatter(grad.reshape(axis_head, -1, width), "seq", 1)
            return scatter(grad, "head", 0)[0].astype(F32)

        def product(left, right):
            return dot_tn(left, right).astype(BF)

        def attention_simple(operands):
            kv, dk, dv, q_rows, dq, left, right = operands
            first = [by_columns(product(a, b)) for a, b in ((kv, dk), (kv, dv), (q_rows, dq))]
            return first + [by_rows(product(left, right))]

        if fast:
            ffn_high, high_sent = run_grid(add_pairs, ffn_high, high_got)
            low_got, high_got = cross(tie(low_sent, ffn_high), 1), cross(high_sent, 1)
            pack_got = swap(tie(pack_sent, ffn_high), 1)
            pack_kept, pack_sent = run_grid(
                attention_weight_grad, role_info, pack_operands, axis_head, pack_got
            )
        total = run(memory_total_kernel, "memory_total", [grad_memsum] + parts, [row_low])[0]
        grad_planes = from_planes(total)
        if fast:
            un_got = cross(tie(un_sent, total), 0)
            blocks = ffn_blocks([ffn_low, ffn_high], [low_got, high_got])
            pack_got = cross(tie(pack_sent, blocks[0]), 0)
            un_kept, un_sent = run_grid(add_pairs, un_kept, un_got)
            un_got = cross(un_sent, 1)
            pack_kept, pack_sent = run_grid(add_pairs, pack_kept, pack_got)
            pack_got = cross(pack_sent, 1)
            blocks = middle(*blocks, rows)
            un_blocks = attention_blocks(un_kept, un_got)
            pack_blocks = attention_blocks(pack_kept, pack_got)
            halves = ffn_total(*blocks)
            grad_memory = all_planes(grad_planes)
            un_blocks = middle(*un_blocks, pair_rows)
            pack_blocks = middle(*pack_blocks, pair_rows)
            small_planes = direct_planes(tie(small, pack_blocks[0]))
            fi_grad, fo_grad = ffn_final(halves)
            un_halves = attention_total(*un_blocks)
            pack_halves = attention_total(*pack_blocks)
            un_grads = attention_final(un_halves)
            pack_grads = attention_final(pack_halves)
        else:
            grad_memory = all_planes(grad_planes)
            small_planes = direct_planes(small)
            un_grads = attention_simple(un_operands)
            pack_grads = attention_simple(pack_operands)
            fi_grad = jnp.stack([product(attn_low, hid_grad[p]) for p in range(axis_head)])
            fi_grad = scatter(scatter(fi_grad, "seq", 1), "head", 0)[0].astype(F32)
            fo_grad = jnp.stack([product(gelu_out[p], ffn_grad) for p in range(axis_head)])
            fo_grad = scatter(scatter(fo_grad, "seq", 1), "head", 0)[0].astype(F32)

        small = run(
            plane_vectors_kernel,
            "vectors",
            small_planes,
            [(small.shape, F32)],
            scratch=[pltpu.VMEM((axis_head,) + small.shape, F32)],
        )[0]
        share = width // axis_seq
        vectors = lax.dynamic_slice_in_dim(small[:7], seq_index * share, share, 1)
        fib = mine(small[7 : 7 + axis_head].reshape(axis_head, -1))
        fib = lax.dynamic_slice_in_dim(fib, seq_index * share, share, 0)
        return (
            out_tokens,
            out_memory,
            grad_tokens,
            grad_memory,
            pack_grads[2],
            pack_grads[0],
            pack_grads[1],
            pack_grads[3],
            un_grads[2],
            un_grads[0],
            un_grads[1],
            un_grads[3],
            fi_grad,
            fib,
            fo_grad,
            vectors[0],
            vectors[1],
            vectors[2],
            vectors[3],
            vectors[4],
            vectors[5],
            vectors[6],
        )

    return local


def solution(mesh):
    rows = P(None, "seq", None)
    by_col, by_row, both = P(None, "head"), P("head", None), P("seq", "head")
    wide_rows = P(("head", "seq"), None)
    in_specs = (
        (rows, rows, P())
        + (by_col, by_col, by_col, by_row)
        + (by_col, by_col, by_col, by_row)
        + (by_col, P("head"), by_row)
        + (P(),) * 7
        + (rows, rows)
    )
    out_specs = (
        (rows,) * 4
        + (both, both, both, wide_rows)
        + (both, both, both, wide_rows)
        + (both, P(("head", "seq")), wide_rows)
        + (P("seq"),) * 7
    )
    local = make_local(mesh.shape["seq"], mesh.shape["head"])
    return jax.shard_map(local, mesh=mesh, in_specs=in_specs, out_specs=out_specs, check_vma=False)
```

```python
import functools
import math

import jax
import jax.numpy as jnp
import numpy as np
from jax import lax
from jax.experimental import pallas as pl
from jax.experimental.pallas import tpu as pltpu
from jax.sharding import PartitionSpec as P

HD = 64
SLOTS = 4
EPSILON = 1e-05
NEG_FILL = -1e30
BF = jnp.bfloat16
F32 = jnp.float32


def dot(left, right):
    return jnp.dot(left, right, preferred_element_type=F32)


def dot_nt(left, right):
    return lax.dot_general(left, right, (((1,), (1,)), ((), ())), preferred_element_type=F32)


def dot_tn(left, right):
    return lax.dot_general(left, right, (((0,), (0,)), ((), ())), preferred_element_type=F32)


TILE = 2 * HD
PARTS = 3
MIB = 1024 * 1024
SMALL = pl.CostEstimate(flops=1, bytes_accessed=1, transcendentals=0)


ROLE, WALK, OTHER_WALK, PLANE, SLOT, UNIT, HALF, BIT, OTHER_BIT, INFO = 0, 1, 5, 9, 10, 11, 12, 13, 14, 16


def call(kernel, name, operands, outs, anys=0, scratch=(), flops=0, vmem=None, out_any=0, after=(), smem=1):
    def body(*refs):
        kernel(*refs[: len(operands)], *refs[len(operands) + len(after) :])

    if vmem is None:
        vmem = 60 if anys or name == "attention_weight_grad" else 16
    vm, anywhere = pl.BlockSpec(memory_space=pltpu.VMEM), pl.BlockSpec(memory_space=pl.ANY)
    specs = [pl.BlockSpec(memory_space=pltpu.SMEM)] * smem
    specs += [vm] * (len(operands) - smem - anys) + [anywhere] * (anys + len(after))
    return pl.pallas_call(
        body,
        out_shape=[jax.ShapeDtypeStruct(s, d) for s, d in outs],
        in_specs=specs,
        out_specs=[vm] * (len(outs) - out_any) + [anywhere] * out_any,
        scratch_shapes=list(scratch),
        compiler_params=pltpu.CompilerParams(vmem_limit_bytes=vmem * MIB),
        cost_estimate=SMALL,
        name=name,
    )(*operands, *after)


def info_kernel(places, lengths, info, unit, block_len):
    seq, head = places[0], places[1]
    role, quad = lax.rem(seq, 2), lax.rem(seq // 2, 4)
    first, second = 1 + role, 2 - role
    info[ROLE] = role
    for at, step in enumerate((0, first, second, 3)):
        info[WALK + at] = quad ^ step
    for at, step in enumerate((0, second, first, 3)):
        info[OTHER_WALK + at] = quad ^ step
    info[PLANE] = head
    end = 0
    slot = 0
    for at in range(SLOTS):
        end = end + lengths[head, at]
        slot = slot + (end <= seq * block_len).astype(jnp.int32)
    info[SLOT] = slot
    info[UNIT] = seq // unit
    info[HALF] = lax.rem(seq, unit) // (unit // 2)
    info[BIT] = jnp.where(role == 0, lax.rem(quad, 2), quad // 2)
    info[OTHER_BIT] = jnp.where(role == 0, quad // 2, lax.rem(quad, 2))
    info[INFO - 1] = 0


def planes_kernel(info, first, second, third, fourth, *outs):
    for at, ref in enumerate((first, second, third, fourth)):
        for mat in range(4):
            out = outs[mat // 2]
            out[mat % 2, info[PLANE] ^ at] = ref[mat]


def first_pieces_kernel(places, lengths, memory, *refs, unit, block_len):
    weights, (info, piece, mem, sems) = refs[:8], refs[8:]
    info_kernel(places, lengths, info, unit, block_len)
    copy_mem = pltpu.make_async_copy(memory.at[places[1]], mem, sems.at[4])
    copy_mem.start()
    rows = piece.shape[1]
    at = pl.ds(pl.multiple_of(info[WALK] * rows, rows), rows)
    for role, chosen in enumerate(((0, 1, 4, 5), (2, 3, 6, 7))):

        @pl.when(info[ROLE] == role)
        def _(chosen=chosen):
            copies = [
                pltpu.make_async_copy(weights[which].at[at], piece.at[mat], sems.at[mat])
                for mat, which in enumerate(chosen)
            ]
            for copy in copies:
                copy.start()
            for copy in copies:
                copy.wait()

    copy_mem.wait()


def other_pieces_kernel(info, bias, *refs):
    ffn_in, ffn_out, tokens, cot_tok, cot_mem = refs[:5]
    ffn, tok, cot_t, cot_m, sems = refs[5:]
    plane = info[PLANE]
    copies = []
    for at, (source, to) in enumerate(((tokens, tok), (cot_tok, cot_t), (cot_mem, cot_m))):
        copies.append(pltpu.make_async_copy(source.at[plane], to, sems.at[2 + at]))
    for copy in copies:
        copy.start()
    rows = ffn.shape[0] - 16
    for role, source in enumerate((ffn_in, ffn_out)):

        @pl.when(info[ROLE] == role)
        def _(source=source):
            copy = pltpu.make_async_copy(source, ffn.at[pl.ds(0, rows)], sems.at[5])
            copy.start()
            copy.wait()

    value = bias[...][None]
    parts = []
    for part in range(PARTS):
        low = value.astype(BF).astype(F32)
        parts.append(low)
        value = value - low
    parts.append(jnp.zeros((16 - PARTS, bias.shape[0]), F32))
    ffn[rows:] = jnp.concatenate(parts, axis=0).astype(BF)
    for copy in copies:
        copy.wait()


def vectors_kernel(info, mem_vectors, out_vectors, hid_vec, out):
    out[...] = jnp.zeros(out.shape, F32)
    out[0:1] = out_vectors[0:1]
    out[1:3] = mem_vectors[0:2]
    out[3:5] = out_vectors[3:5]
    out[5:7] = out_vectors[1:3]
    for plane in range(hid_vec.shape[0]):
        out[7 + plane : 8 + plane] = hid_vec[plane]


def total_kernel(info, *refs):
    total = refs[0][...]
    for ref in refs[1:-1]:
        total = total + ref[...]
    refs[-1][...] = total


def plane_vectors_kernel(info, first, second, third, fourth, out, held):
    planes = held.shape[0]
    for at, ref in enumerate((first, second, third, fourth)):
        held[info[PLANE] ^ at] = ref[...]
    total = held[0]
    for plane in range(1, planes):
        total = total + held[plane]
    out[...] = total


def memory_total_kernel(info, base, first, second, third, fourth, out):
    total = base[...]
    for ref in (first, second, third, fourth):
        total = total + ref[...].astype(F32)
    out[...] = total.astype(BF)


def pick_kernel(info, first, second, third, fourth, out, sem):
    for at, ref in enumerate((first, second, third, fourth)):

        @pl.when(info[SLOT] == (info[UNIT] ^ at))
        def _(ref=ref):
            copy = pltpu.make_async_copy(ref, out, sem)
            copy.start()
            copy.wait()


def tie(value, *after):
    anywhere = pl.BlockSpec(memory_space=pl.ANY)
    return pl.pallas_call(
        lambda *refs: None,
        out_shape=jax.ShapeDtypeStruct(value.shape, value.dtype),
        in_specs=[anywhere] * (1 + len(after)),
        out_specs=anywhere,
        input_output_aliases={0: 0},
        compiler_params=pltpu.CompilerParams(vmem_limit_bytes=16 * MIB),
        cost_estimate=SMALL,
        name="tie",
    )(value, *after)


def stack_kernel(info, first, second, third, fourth, out):
    for at, ref in enumerate((first, second, third, fourth)):
        out[info[PLANE] ^ at] = ref[...]


def put_halves(info, keep, send, value):
    size = keep.shape[0]

    @pl.when(info[HALF] == 0)
    def _():
        keep[...] = value[:size]
        send[...] = value[size:]

    @pl.when(info[HALF] == 1)
    def _():
        keep[...] = value[size:]
        send[...] = value[:size]


def put_slots(info, outs, value, empty):
    for at, out in enumerate(outs):
        here = info[SLOT] == (info[UNIT] ^ at)

        @pl.when(here)
        def _(out=out):
            out[...] = value

        @pl.when(jnp.logical_not(here))
        def _(out=out):
            out[...] = empty


def blend_values(given, sel, width):
    lses = [dot(c[:, width:], sel[0]) for c in given]
    top = lses[0]
    for lse in lses[1:]:
        top = jnp.maximum(top, lse)
    shares = [jnp.exp(lse - top) for lse in lses]
    total = shares[0]
    for share in shares[1:]:
        total = total + share
    inv = 1.0 / total
    low = lax.broadcasted_iota(jnp.int32, (1, TILE), 1) < HD
    tiles = []
    for pair in range(width // TILE):
        cols = slice(pair * TILE, (pair + 1) * TILE)
        ctx = None
        for share, c in zip(shares, given):
            share = share * inv
            weight = jnp.where(
                low, share[:, 2 * pair : 2 * pair + 1], share[:, 2 * pair + 1 : 2 * pair + 2]
            )
            term = weight * c[:, cols].astype(F32)
            ctx = term if ctx is None else ctx + term
        tiles.append(ctx.astype(BF))
    return tiles, top + jnp.log(total)


def blend_kernel(info, keep, got, sel, *outs):
    outs, value = outs[:SLOTS], outs[SLOTS]
    width = value.shape[1] - TILE
    heads = width // HD
    tiles, lse = blend_values((keep, got), sel, width)
    for pair, tile in enumerate(tiles):
        value[:, pair * TILE : (pair + 1) * TILE] = tile
    value[:, width:] = as_parts(lse, heads).astype(BF)
    col = lax.broadcasted_iota(jnp.int32, value.shape, 1)
    fill = jnp.where((col >= width) & (col < width + heads), NEG_FILL, 0.0)
    put_slots(info, outs, value[...], fill.astype(BF))


def sum_kernel(info, keep, got, *outs):
    total = (keep[...].astype(F32) + got[...].astype(F32)).astype(BF)
    put_slots(info, outs, total, jnp.zeros(total.shape, BF))


def start_weights(info, pieces, held, sems, mats=(0, 1)):
    planes = held.shape[2]
    for mat in mats:
        for j in range(4):
            mine = (info[ROLE], info[WALK + j], pieces[j])
            theirs = (1 - info[ROLE], info[OTHER_WALK + j], pieces[4 + j])
            for role, unit, piece in (mine, theirs):
                for plane in range(planes):
                    pltpu.make_async_copy(
                        piece.at[mat, plane],
                        held.at[role, mat, plane, unit],
                        sems.at[role, mat, j * planes + plane],
                    ).start()


def weight(held, sems, pieces, role, mat):
    planes = held.shape[2]
    for j in range(4):
        for plane in range(planes):
            pltpu.make_async_copy(
                pieces[j].at[mat, plane],
                held.at[role, mat, plane, j],
                sems.at[role, mat, j * planes + plane],
            ).wait()
    return matrix(held, role, mat)


def matrix(held, *index):
    block = held[index]
    return block.reshape(-1, block.shape[-1])


def half_masks():
    lane = lax.broadcasted_iota(jnp.int32, (1, TILE), 1)
    low = (lane < HD).astype(F32).astype(BF)
    return low, (lane >= HD).astype(F32).astype(BF)


def put_scalars(rows):
    count = len(rows)
    stack = jnp.concatenate(rows * PARTS, axis=0)
    extra = TILE - stack.shape[0]
    stack = jnp.concatenate([stack, jnp.zeros((extra, stack.shape[1]), F32)], axis=0)
    return stack.T


def as_parts(wide, heads, offset=0):
    first = wide.astype(BF).astype(F32)
    rest = wide - first
    second = rest.astype(BF).astype(F32)
    third = rest - second
    lane = lax.broadcasted_iota(jnp.int32, wide.shape, 1) - offset
    return jnp.where(
        lane < 0,
        0.0,
        jnp.where(
            lane < heads,
            first,
            jnp.where(lane < 2 * heads, second, jnp.where(lane < 3 * heads, third, 0.0)),
        ),
    )


def norm_stats(summed):
    centre = summed - jnp.mean(summed, axis=-1, keepdims=True)
    inv = lax.rsqrt(jnp.mean(centre * centre, axis=-1, keepdims=True) + EPSILON)
    return centre * inv, inv


def norm_pull(upstream, normed, inv, gain):
    scaled = upstream * gain
    return inv * (
        scaled
        - jnp.mean(scaled, axis=-1, keepdims=True)
        - normed * jnp.mean(scaled * normed, axis=-1, keepdims=True)
    )


def head_forward(q_tile, k_tile, v_tile, masks):
    parts, rows = [], []
    for side in range(2):
        scores = dot_nt(k_tile * masks[side], q_tile)
        top = jnp.max(scores, axis=0, keepdims=True)
        weights = jnp.exp(scores - top)
        den = jnp.sum(weights, axis=0, keepdims=True)
        num = dot_tn(v_tile, weights.astype(BF))[side * HD : (side + 1) * HD]
        parts.append(num * (1.0 / den))
        rows.append(top + jnp.log(den))
    return jnp.concatenate(parts, axis=0), rows


def head_backward(q_tile, k_tile, v_tile, g_tile, lses, deltas, masks):
    dq, dk, dv = [], None, None
    for side in range(2):
        q_side, g_side = q_tile * masks[side], g_tile * masks[side]
        weights = jnp.exp(dot_nt(k_tile, q_side) - lses[side])
        dscores = (weights * (dot_nt(v_tile, g_side) - deltas[side])).astype(BF)
        weights = weights.astype(BF)
        dq.append(dot_tn(k_tile, dscores)[side * HD : (side + 1) * HD])
        dk_side, dv_side = dot(dscores, q_side), dot(weights, g_side)
        dk = dk_side if dk is None else dk + dk_side
        dv = dv_side if dv is None else dv + dv_side
    return jnp.concatenate(dq, axis=0), dk, dv


def pack_forward_kernel(
    info, tok, mem, *refs
):
    pieces, (k_out, v_out, q_out, keep, send, packed, held, sems) = refs[:8], refs[8:]
    width = tok.shape[1]
    heads = width // HD
    start_weights(info, pieces, held, sems)
    k_out[...] = dot_nt(tok[...], weight(held, sems, pieces, 0, 0)).astype(BF)
    v_out[...] = dot_nt(tok[...], weight(held, sems, pieces, 0, 1)).astype(BF)
    q_out[...] = dot_nt(mem[...], weight(held, sems, pieces, 1, 0)).astype(BF) * BF(HD**-0.5)
    masks = half_masks()
    rows = []
    for pair in range(heads // 2):
        cols = slice(pair * TILE, (pair + 1) * TILE)
        ctx, pair_rows = head_forward(q_out[:, cols], k_out[:, cols], v_out[:, cols], masks)
        packed[:, cols] = ctx.T.astype(BF)
        rows += pair_rows
    packed[:, width:] = as_parts(put_scalars(rows), heads).astype(BF)
    put_halves(info, keep, send, packed)
    weight(held, sems, pieces, 1, 1)


def start_out_matrix(info, pieces, held, sems):
    planes = held.shape[0]
    for j in range(4):
        for role, piece, unit in ((1, pieces[j], WALK + j), (0, pieces[4 + j], OTHER_WALK + j)):

            @pl.when(info[ROLE] == role)
            def _(piece=piece, unit=unit, j=j):
                for plane in range(planes):
                    pltpu.make_async_copy(
                        piece.at[1, plane], held.at[plane, info[unit]], sems.at[j * planes + plane]
                    ).start()


def out_matrix(pieces, held, sems):
    planes = held.shape[0]
    for j in range(4):
        for plane in range(planes):
            pltpu.make_async_copy(
                pieces[j].at[1, plane], held.at[plane, j], sems.at[j * planes + plane]
            ).wait()
    return matrix(held, Ellipsis)


def memory_kernel(info, c0, c1, c2, c3, sel, mem, cot, gain, bias, *refs):
    pieces, outs = refs[:8], refs[8:]
    result, mix_low, ctx_out, lse_out, grad_sum, vectors, held, sems = outs
    width = mem.shape[1]
    heads = width // HD
    start_out_matrix(info, pieces, held, sems)
    tiles, lse = blend_values((c0, c1, c2, c3), sel, width)
    lse_out[...] = lse
    for pair, tile in enumerate(tiles):
        ctx_out[:, pair * TILE : (pair + 1) * TILE] = tile
    mix = dot(ctx_out[...], out_matrix(pieces, held, sems))
    mix_low[...] = mix.astype(BF)
    normed, inv_std = norm_stats(mix + mem[...].astype(F32))
    gain_row = gain[...][None]
    result[...] = (normed * gain_row + bias[...][None]).astype(BF)
    upstream = cot[...].astype(F32)
    grad_sum[...] = norm_pull(upstream, normed, inv_std, gain_row)
    vectors[0:1] = jnp.sum(upstream * normed, axis=0, keepdims=True)
    vectors[1:2] = jnp.sum(upstream, axis=0, keepdims=True)


def unpack_forward_kernel(info, tok, mix, *refs):
    pieces, outs = refs[:8], refs[8:]
    k_out, v_out, q_out, ctx_out, lse_out, normed_out, inv_out, held, sems = outs
    width = tok.shape[1]
    heads = width // HD
    start_weights(info, pieces, held, sems)
    k_out[...] = dot_nt(mix[...], weight(held, sems, pieces, 0, 0)).astype(BF)
    v_out[...] = dot_nt(mix[...], weight(held, sems, pieces, 0, 1)).astype(BF)
    q_out[...] = dot_nt(tok[...], weight(held, sems, pieces, 1, 0)).astype(BF) * BF(HD**-0.5)
    masks = half_masks()
    for pair in range(heads // 2):
        cols = slice(pair * TILE, (pair + 1) * TILE)
        ctx, rows = head_forward(q_out[:, cols], k_out[:, cols], v_out[:, cols], masks)
        ctx_out[:, cols] = ctx.T.astype(BF)
        lse_out[2 * pair : 2 * pair + 1] = rows[0]
        lse_out[2 * pair + 1 : 2 * pair + 2] = rows[1]
    summed = dot(ctx_out[...], weight(held, sems, pieces, 1, 1)) + tok[...].astype(F32)
    normed, inv = norm_stats(summed)
    normed_out[...] = normed
    inv_out[...] = inv


GELU_A = math.sqrt(2.0 / math.pi)
GELU_B = 0.044715
CHUNK = 256


def start_ffn(info, pieces, held, sems):
    planes, rows = held.shape[1], held.shape[2]
    quarter = rows // 4
    for plane in range(planes):
        for j, role in enumerate((info[ROLE], 1 - info[ROLE])):
            for part in range(4):
                at = pl.ds(part * quarter, quarter)
                pltpu.make_async_copy(
                    pieces[j].at[plane, at], held.at[role, plane, at], sems.at[plane, 4 * j + part]
                ).start()


def wait_ffn(pieces, held, sems, plane):
    rows = held.shape[2]
    quarter = rows // 4
    for j in range(2):
        for part in range(4):
            at = pl.ds(part * quarter, quarter)
            pltpu.make_async_copy(
                pieces[j].at[0, at], held.at[j, plane, at], sems.at[plane, 4 * j + part]
            ).wait()


def ffn_kernel(info, normed_in, inv_in, cot, mem_result, *refs):
    rows, refs = [r[...][None] for r in refs[:5]], refs[5:]
    attn_gain, attn_bias, out_gain, out_bias, ffn_bias = rows
    pieces, outs = refs[:2], refs[2:]
    out, attn_low, ffn_grad, mix_grad, mix_sum, vectors, hid_vec, gelu_out, hid_out = outs[:9]
    held, bias, total, gelu_low, slope, sems, bias_sem, out_sems = outs[9:]
    planes, width = held.shape[1], held.shape[2]
    bias_at = pl.ds(width, 16)
    bias_copies = [
        pltpu.make_async_copy(pieces[0].at[plane, bias_at], bias.at[plane], bias_sem.at[plane])
        for plane in range(planes)
    ]
    for copy in bias_copies:
        copy.start()
    start_ffn(info, pieces, held, sems)
    attn = normed_in[...] * attn_gain + attn_bias
    attn_low[...] = attn.astype(BF)
    total[...] = attn + ffn_bias
    for copy in bias_copies:
        copy.wait()
    out_copies = []
    for plane in range(planes):
        wait_ffn(pieces, held, sems, plane)
        parts = bias[plane].astype(F32)
        shift = parts[0:1] + parts[1:2] + parts[2:3]
        for start in range(0, held.shape[3], CHUNK):
            cols = slice(start, start + CHUNK)
            hidden = dot(attn_low[...], held[0, plane, :, cols]) + shift[:, cols]
            square = hidden * hidden
            half = 1.0 / (1.0 + jnp.exp(hidden * (-2.0 * GELU_A - 2.0 * GELU_A * GELU_B * square)))
            gelu = hidden * half
            gelu_low[plane, :, cols] = gelu.astype(BF)
            inner = 2.0 * GELU_A + 6.0 * GELU_A * GELU_B * square
            slope[plane, :, cols] = (half + gelu * (1.0 - half) * inner).astype(BF)
        total[...] += dot(gelu_low[plane], held[1, plane])
        copy = pltpu.make_async_copy(gelu_low.at[plane], gelu_out.at[plane], out_sems.at[plane, 0])
        copy.start()
        out_copies.append(copy)
    out_normed, out_inv = norm_stats(total[...])
    count = normed_in.shape[0]
    out[:count] = (out_normed * out_gain + out_bias).astype(BF)
    out[count:] = mem_result[...]
    upstream = cot[...].astype(F32)
    grad = norm_pull(upstream, out_normed, out_inv, out_gain)
    ffn_grad[...] = grad.astype(BF)
    vectors[0:1] = jnp.sum(grad.astype(BF).astype(F32), axis=0, keepdims=True)
    vectors[1:2] = jnp.sum(upstream * out_normed, axis=0, keepdims=True)
    vectors[2:3] = jnp.sum(upstream, axis=0, keepdims=True)
    total[...] = grad
    for plane in range(planes):
        for start in range(0, held.shape[3], CHUNK):
            cols = slice(start, start + CHUNK)
            pulled = dot_nt(ffn_grad[...], held[1, plane, cols]) * slope[plane, :, cols].astype(F32)
            low = pulled.astype(BF)
            slope[plane, :, cols] = low
            hid_vec[plane, :, cols] = jnp.sum(low.astype(F32), axis=0, keepdims=True)
        total[...] += dot_nt(slope[plane], held[0, plane])
        copy = pltpu.make_async_copy(slope.at[plane], hid_out.at[plane], out_sems.at[plane, 1])
        copy.start()
        out_copies.append(copy)
    upstream = total[...]
    normed = normed_in[...]
    vectors[3:4] = jnp.sum(upstream * normed, axis=0, keepdims=True)
    vectors[4:5] = jnp.sum(upstream, axis=0, keepdims=True)
    grad = norm_pull(upstream, normed, inv_in[...], attn_gain)
    mix_sum[...] = grad
    mix_grad[...] = grad.astype(BF)
    for copy in out_copies:
        copy.wait()


def unpack_backward_kernel(info, q_in, k_in, v_in, ctx, lse, mix_grad, mix_sum, *refs):
    pieces, outs = refs[:8], refs[8:]
    uq, uk, uv, keep, send, tok_part, held, sems = outs
    width = q_in.shape[1]
    heads = width // HD
    start_weights(info, pieces, held, sems, (1, 0))
    masks = half_masks()
    ctx_grad = dot_nt(mix_grad[...], weight(held, sems, pieces, 1, 1))
    ctx_low = ctx_grad.astype(BF)
    for pair in range(heads // 2):
        cols = slice(pair * TILE, (pair + 1) * TILE)
        product = ctx_grad[:, cols] * ctx[:, cols].astype(F32)
        first = product.astype(BF)
        second = (product - first.astype(F32)).astype(BF)
        deltas = []
        for side in range(2):
            picker = jnp.broadcast_to(masks[side], (16, TILE))
            deltas.append((dot_nt(picker, first) + dot_nt(picker, second))[0:1])
        lses = [lse[2 * pair : 2 * pair + 1], lse[2 * pair + 1 : 2 * pair + 2]]
        dq, dk, dv = head_backward(
            q_in[:, cols], k_in[:, cols], v_in[:, cols], ctx_low[:, cols], lses, deltas, masks
        )
        uq[:, cols] = (dq.T * (HD**-0.5)).astype(BF)
        uk[:, cols] = dk.astype(BF)
        uv[:, cols] = dv.astype(BF)
    mix_part = dot(uk[...], weight(held, sems, pieces, 0, 0))
    mix_part = mix_part + dot(uv[...], weight(held, sems, pieces, 0, 1))
    put_halves(info, keep, send, mix_part.astype(BF))
    tok_part[...] = mix_sum[...] + dot(uq[...], weight(held, sems, pieces, 1, 0))


def memory_back_kernel(info, c0, c1, c2, c3, sel, grad_sum, ctx, lse, *refs):
    pieces, outs = refs[:8], refs[8:]
    mix_grad, packed, held, sems = outs
    width = ctx.shape[1]
    heads = width // HD
    start_out_matrix(info, pieces, held, sems)
    total = grad_sum[...]
    for c in (c0, c1, c2, c3):
        total = total + c[...].astype(F32)
    mix_grad[...] = total.astype(BF)
    pulled = dot_nt(mix_grad[...], out_matrix(pieces, held, sems))
    packed[:, :width] = pulled.astype(BF)
    delta = jnp.zeros(lse.shape, F32)
    for pair in range(heads // 2):
        cols = slice(pair * TILE, (pair + 1) * TILE)
        product = pulled[:, cols] * ctx[:, cols].astype(F32)
        first = product.astype(BF)
        second = (product - first.astype(F32)).astype(BF)
        delta = delta + dot(first, sel[2 + pair]) + dot(second, sel[2 + pair])
    scalars = as_parts(lse[...], heads) + as_parts(delta, heads, PARTS * heads)
    packed[:, width:] = scalars.astype(BF)


def pack_backward_kernel(info, back, sel, q_in, k_in, v_in, tok_part, *refs):
    pieces, outs = refs[:8], refs[8:]
    pq, pk, pv, tok_grad, keep, send, held, sems = outs
    width = q_in.shape[1]
    heads = width // HD
    start_weights(info, pieces, held, sems)
    masks = half_masks()
    lse = dot(back[:, width:], sel[0]).T
    delta = dot(back[:, width:], sel[1]).T
    for pair in range(heads // 2):
        cols = slice(pair * TILE, (pair + 1) * TILE)
        lses = [lse[2 * pair : 2 * pair + 1], lse[2 * pair + 1 : 2 * pair + 2]]
        deltas = [delta[2 * pair : 2 * pair + 1], delta[2 * pair + 1 : 2 * pair + 2]]
        dq, dk, dv = head_backward(
            q_in[:, cols], k_in[:, cols], v_in[:, cols], back[:, cols], lses, deltas, masks
        )
        pq[:, cols] = (dq.T * (HD**-0.5)).astype(BF)
        pk[:, cols] = dk.astype(BF)
        pv[:, cols] = dv.astype(BF)
    total = dot(pk[...], weight(held, sems, pieces, 0, 0))
    total = total + dot(pv[...], weight(held, sems, pieces, 0, 1))
    tok_grad[...] = (total + tok_part[...]).astype(BF)
    put_halves(info, keep, send, dot(pq[...], weight(held, sems, pieces, 1, 0)).astype(BF))
    weight(held, sems, pieces, 1, 1)


def selectors(width):
    heads = width // HD
    lane = np.arange(TILE)
    inside = lane < PARTS * heads
    first = inside[:, None] & inside[None, :] & (lane[:, None] % heads == lane[None, :] % heads)
    shifted = lane - PARTS * heads
    second = (shifted >= 0) & (shifted < PARTS * heads)
    second = second[:, None] & inside[None, :] & (shifted[:, None] % heads == lane[None, :] % heads)
    rows = [first, second]
    target = (shifted >= 0) & (shifted < PARTS * heads)
    for pair in range(heads // 2):
        head = 2 * pair + (lane >= HD)
        rows.append(target[None, :] & (head[:, None] == (shifted % heads)[None, :]))
    return jnp.asarray(np.stack(rows).astype(np.float32), BF)


def pair_units(info):
    role, quad = info[ROLE], info[WALK]
    bit = jnp.where(role == 0, lax.rem(quad, 2), quad // 2)
    step, scale = jnp.where(role == 0, 2, 1), jnp.where(role == 0, 1, 2)
    keep = [bit * scale + at * step for at in range(2)]
    send = [(1 - bit) * scale + at * step for at in range(2)]
    return keep, send


def split_pairs(info, value, keep, send, rows):
    for units, out in zip(pair_units(info), (keep, send)):
        for at, unit in enumerate(units):
            out[at, 0] = value[pl.ds(pl.multiple_of(unit * rows, rows), rows)]


def ffn_weight_grad(info, role, operands, added, after=()):
    attn_low, hid_grad, gelu_out, ffn_grad = operands
    planes, rows, cols = hid_grad.shape
    width = attn_low.shape[1]
    quarter, half = width // 4, planes // 2

    def kernel(which, info, attn_ref, hid_ref, gelu_ref, grad_ref, *refs):
        plane = pl.program_id(0)
        refs = refs[len(after) :] if added is None else refs[:2] + refs[2 + len(after) :]

        def put(value):
            for side in range(2):

                @pl.when(plane // half == side)
                def _(side=side):
                    if added is None:
                        refs[side][0] = value.astype(BF)
                    else:
                        recv, held = refs[side], refs[6]
                        held[...] = (value + recv[0].astype(F32)).astype(BF)
                        keep, send = refs[2 + 2 * side : 4 + 2 * side]
                        split_pairs(info, held, keep, send, quarter)

        @pl.when(which[0] == 0)
        def _():
            put(dot_tn(attn_ref[...], hid_ref[0]))

        @pl.when(which[0] == 1)
        def _():
            put(dot_tn(gelu_ref[0], grad_ref[...]))

    vm, sm = pl.BlockSpec(memory_space=pltpu.VMEM), pl.BlockSpec(memory_space=pltpu.SMEM)
    blocks = [
        pl.BlockSpec((1, width, cols), lambda i, w: (jnp.minimum(i, half - 1), 0, 0)),
        pl.BlockSpec((1, width, cols), lambda i, w: (jnp.maximum(i - half, 0), 0, 0)),
    ]
    pairs = [
        pl.BlockSpec((2, 1, quarter, cols), lambda i, w: (0, jnp.minimum(i, half - 1), 0, 0)),
        pl.BlockSpec((2, 1, quarter, cols), lambda i, w: (0, jnp.maximum(i - half, 0), 0, 0)),
    ]
    pair_shape = jax.ShapeDtypeStruct((2, half, quarter, cols), BF)
    hid_block = pl.BlockSpec((1, rows, cols), lambda i, w: (i * (1 - w[0]), 0, 0))
    gelu_block = pl.BlockSpec((1, rows, cols), lambda i, w: (i * w[0], 0, 0))
    args = [role, info, attn_low, hid_grad, gelu_out, ffn_grad]
    specs = [sm, vm, hid_block, gelu_block, vm]
    if added is not None:
        args += added
        specs += blocks
    return pl.pallas_call(
        kernel,
        out_shape=(
            [jax.ShapeDtypeStruct((half, width, cols), BF)] * 2
            if added is None
            else [pair_shape] * 4
        ),
        grid_spec=pltpu.PrefetchScalarGridSpec(
            num_scalar_prefetch=1,
            grid=(planes,),
            in_specs=specs + [pl.BlockSpec(memory_space=pl.ANY)] * len(after),
            out_specs=blocks if added is None else [pairs[0], pairs[0], pairs[1], pairs[1]],
            scratch_shapes=[] if added is None else [pltpu.VMEM((width, cols), BF)],
        ),
        compiler_params=pltpu.CompilerParams(vmem_limit_bytes=60 * MIB),
        cost_estimate=SMALL,
        name="ffn_weight_grad",
    )(*args, *after)


def attention_weight_grad(info, role, operands, planes, added, after=()):
    width = operands[0].shape[1]
    quarter = width // 4
    size = quarter // planes

    def kernel(info, which, kv, dk, dv, q_rows, dq, left, right, *refs):
        def put(mat, value, by_plane=False):
            if added is None:
                out, value = refs[0].at[mat], value.astype(BF)
            else:
                out = refs[3].at[mat]
            if by_plane:
                for plane in range(planes):
                    for quad in range(4):
                        at, to = (plane * 4 + quad) * size, (quad * planes + plane) * size
                        piece = value[at : at + size]
                        if added is not None:
                            piece = piece + refs[0][mat, to : to + size].astype(F32)
                        out[to : to + size] = piece.astype(BF)
            else:
                if added is not None:
                    value = value + refs[0][mat].astype(F32)
                out[...] = value.astype(BF)

        @pl.when(which[0] == 0)
        def _():
            put(0, dot_tn(kv[...], dk[...]))
            put(1, dot_tn(kv[...], dv[...]))

        @pl.when(which[0] == 1)
        def _():
            put(0, dot_tn(q_rows[...], dq[...]))
            put(1, dot_tn(left[...], right[...]), True)

        if added is not None:
            for mat in range(2):
                keep, send = refs[1].at[:, mat : mat + 1], refs[2].at[:, mat : mat + 1]
                split_pairs(info, refs[3].at[mat], keep, send, quarter)

    rows = operands[0].shape[0] + operands[3].shape[0]
    operands = [info, role] + list(operands)
    outs = [((2, width, width), BF)]
    scratch = []
    if added is not None:
        operands.append(added)
        outs = [((2, 2, quarter, width), BF)] * 2
        scratch = [pltpu.VMEM((2, width, width), BF)]
    result = call(
        kernel,
        "attention_weight_grad",
        operands,
        outs,
        scratch=scratch,
        flops=2 * rows * width * width,
        smem=2,
        after=after,
    )
    return result[0] if added is None else result


def add_pairs(info, kept, got, after=()):
    _, mats, rows, cols = kept.shape

    def kernel(info, kept_ref, got_ref, *refs):
        keep, send = refs[len(after) :]
        quad = info[WALK]
        at = jnp.where(info[ROLE] == 0, quad // 2, lax.rem(quad, 2))
        for index, out in ((at, keep), (1 - at, send)):
            out[0] = (kept_ref[index, 0].astype(F32) + got_ref[index, 0].astype(F32)).astype(BF)

    pairs = pl.BlockSpec((2, 1, rows, cols), lambda i: (0, i, 0, 0))
    one = pl.BlockSpec((1, rows, cols), lambda i: (i, 0, 0))
    return pl.pallas_call(
        kernel,
        grid=(mats,),
        out_shape=[jax.ShapeDtypeStruct((mats, rows, cols), BF)] * 2,
        in_specs=[pl.BlockSpec(memory_space=pltpu.SMEM), pairs, pairs]
        + [pl.BlockSpec(memory_space=pl.ANY)] * len(after),
        out_specs=[one, one],
        compiler_params=pltpu.CompilerParams(vmem_limit_bytes=16 * MIB),
        cost_estimate=SMALL,
        name="add_pairs",
    )(info, kept, got, *after)


def put_planes(info, held, keep, send):
    kind = lax.rem(info[PLANE], 2)
    for at in range(held.shape[0] // 2):
        keep[at] = held[2 * at + kind].astype(keep.dtype)
        send[at] = held[2 * at + 1 - kind].astype(send.dtype)


def ffn_blocks_kernel(info, kept_low, got_low, kept_high, got_high, keep, send):
    kind = lax.rem(info[PLANE], 2)
    for at, (kept, got) in enumerate(((kept_low, got_low), (kept_high, got_high))):
        for plane, out in ((kind, keep), (1 - kind, send)):
            out[at] = (kept[plane].astype(F32) + got[plane].astype(F32)).astype(out.dtype)


def attention_blocks_kernel(info, kept, got, keep, send, total, held):
    planes, _, rows, cols = held.shape
    size = rows // planes
    total[...] = kept[...].astype(F32) + got[...].astype(F32)
    for plane in range(planes):
        held[plane, 0] = total[0, :, plane * cols : (plane + 1) * cols]

    @pl.when(info[ROLE] == 0)
    def _():
        for plane in range(planes):
            held[plane, 1] = total[1, :, plane * cols : (plane + 1) * cols]

    @pl.when(info[ROLE] == 1)
    def _():
        for plane in range(planes):
            for at in range(planes):
                held[plane, 1, at * size : (at + 1) * size] = total[
                    1, plane * size : (plane + 1) * size, at * cols : (at + 1) * cols
                ]

    put_planes(info, held, keep, send)


def middle_kernel(info, kept, got, keep, send):
    mine = info[PLANE] // 2
    keep[...] = kept[mine] + got[mine].astype(F32)
    send[...] = (kept[1 - mine] + got[1 - mine].astype(F32)).astype(BF)


def ffn_total_kernel(info, own, other, keep, send, total):
    total[...] = own[...] + other[...].astype(F32)
    half = keep.shape[0]
    for index, out in ((info[ROLE], keep), (1 - info[ROLE], send)):
        out[...] = total[pl.ds(pl.multiple_of(index * half, half), half)]


def attention_total_kernel(info, own, other, keep, send, total, planes):
    total[...] = own[...] + other[...].astype(F32)
    half = keep.shape[1]
    for index, out in ((info[ROLE], keep), (1 - info[ROLE], send)):
        at = pl.ds(pl.multiple_of(index * half, half), half)
        out[0] = total[0, at]

        @pl.when(info[ROLE] == 0)
        def _(out=out, at=at):
            out[1] = total[1, at]

        @pl.when(info[ROLE] == 1)
        def _(out=out, index=index):
            size = half // planes
            for chunk in range(planes):
                start = pl.multiple_of(2 * chunk * size + index * size, size)
                out[1, chunk * size : (chunk + 1) * size] = total[1, pl.ds(start, size)]


def attention_final_kernel(info, kept, got, key_g, value_g, query_g, out_g, planes):
    def put(zero, one):
        key_g[...] = zero[0]
        value_g[...] = zero[1]
        query_g[...] = one[0]
        size = out_g.shape[0]
        chunks = [one[1, at * size : (at + 1) * size] for at in range(planes)]
        out_g[...] = jnp.concatenate(chunks, axis=1)

    @pl.when(info[ROLE] == 0)
    def _():
        put(kept, got)

    @pl.when(info[ROLE] == 1)
    def _():
        put(got, kept)


def ffn_final_kernel(info, kept, got, in_g, out_g):
    @pl.when(info[ROLE] == 0)
    def _():
        in_g[...] = kept[...]
        out_g[...] = got[...]

    @pl.when(info[ROLE] == 1)
    def _():
        in_g[...] = got[...]
        out_g[...] = kept[...]


def empty_row(width):
    heads = width // HD
    row = np.zeros((1, width + TILE), np.float32)
    row[:, width : width + heads] = NEG_FILL
    return jnp.asarray(row)


def blend_two_kernel(info, keep, got, sel, value):
    width = value.shape[1] - TILE
    tiles, lse = blend_values((keep, got), sel, width)
    for pair, tile in enumerate(tiles):
        value[:, pair * TILE : (pair + 1) * TILE] = tile
    value[:, width:] = as_parts(lse, width // HD).astype(BF)


def first_pieces(places, lengths, memory, weights, unit, block_len):
    sm, vm = pl.BlockSpec(memory_space=pltpu.SMEM), pl.BlockSpec(memory_space=pltpu.VMEM)
    rows, width = weights[0].shape
    return pl.pallas_call(
        functools.partial(first_pieces_kernel, unit=unit, block_len=block_len),
        out_shape=[
            jax.ShapeDtypeStruct((INFO,), jnp.int32),
            jax.ShapeDtypeStruct((4, rows // 4, width), BF),
            jax.ShapeDtypeStruct(memory.shape[1:], BF),
        ],
        in_specs=[sm, sm] + [pl.BlockSpec(memory_space=pl.ANY)] * 9,
        out_specs=[sm, vm, vm],
        scratch_shapes=[pltpu.SemaphoreType.DMA((5,))],
        compiler_params=pltpu.CompilerParams(vmem_limit_bytes=60 * MIB),
        cost_estimate=SMALL,
        name="first_pieces",
    )(places, lengths, memory, *weights)


def make_local(axis_seq, axis_head):
    unit = axis_seq // SLOTS
    fast = axis_seq == 8

    def swap(value, step):
        return lax.ppermute(value, "seq", [(i, i ^ step) for i in range(axis_seq)])

    def cross(value, order):
        steps = (2, 4) if order == 0 else (4, 2)
        return lax.ppermute(value, "seq", [(i, i ^ steps[i % 2]) for i in range(axis_seq)])

    def over(value, step):
        return lax.ppermute(value, "head", [(i, i ^ step) for i in range(axis_head)])

    def from_planes(value):
        got = [value]
        step = 1
        while step < axis_head:
            got += [over(value, step) if part is value else over(part, step) for part in got]
            step *= 2
        return got

    def direct_planes(value):
        return [value] + [over(value, step) for step in range(1, axis_head)]

    def local(
        tokens,
        memory,
        seq_lengths,
        pack_query,
        pack_key,
        pack_value,
        pack_out,
        unpack_query,
        unpack_key,
        unpack_value,
        unpack_out,
        ffn_in,
        ffn_in_bias,
        ffn_out,
        ffn_out_bias,
        mem_gain,
        mem_bias,
        attn_gain,
        attn_bias,
        out_gain,
        out_bias,
        cot_tokens,
        cot_memory,
    ):
        seq_index = lax.axis_index("seq")
        head_index = lax.axis_index("head")
        _, block_len, width = tokens.shape
        hidden_width = ffn_in.shape[1]
        my_lane, role = seq_index % unit, seq_index % 2
        quarter, head_cols = width // 4, width // axis_head
        info, pieces, mem = first_pieces(
            jnp.stack([seq_index, head_index]),
            seq_lengths,
            memory,
            [pack_key.T, pack_value.T, pack_query.T, pack_out]
            + [unpack_key.T, unpack_value.T, unpack_query.T, unpack_out],
            unit,
            block_len,
        )
        last = []

        def run(kernel, name, operands, outs, also=(), **more):
            after = list(last) + list(also)
            result = call(kernel, name, [info] + operands, outs, after=after, **more)
            last[:] = [result[0]]
            return result

        def run_grid(function, *operands):
            result = function(info, *operands, after=list(last))
            last[:] = [result[0] if isinstance(result, (list, tuple)) else result]
            return result

        def mine(value):
            return lax.dynamic_index_in_dim(value, head_index, 0, keepdims=False)

        def gather_unit(value):
            step = 1
            while step < unit:
                other = swap(value, step)
                low = (my_lane // step) % 2 == 0
                value = jnp.concatenate(
                    [jnp.where(low, value, other), jnp.where(low, other, value)], axis=0
                )
                step *= 2
            return value

        def scatter_unit(value, add, step):
            while step >= 1:
                half = value.shape[0] // 2
                low = (my_lane // step) % 2 == 0
                keep = jnp.where(low, value[:half], value[half:])
                send = jnp.where(low, value[half:], value[:half])
                value = add([keep, swap(send, step)])
                step //= 2
            return value

        def fetch_start(value):
            return [value] + [swap(value, j * unit) for j in range(1, SLOTS)]

        def fetch_finish(parts, also=()):
            shapes = [(parts[0].shape, BF)]
            sem = [pltpu.SemaphoreType.DMA]
            return run(pick_kernel, "pick_slot", parts, shapes, anys=SLOTS, scratch=sem, also=also)[0]

        def sum_rows(values):
            total = values[0].astype(F32)
            for value in values[1:]:
                total = total + value.astype(F32)
            return total.astype(BF)

        packed_width = width + TILE
        row_count = memory.shape[1]
        slot_count = unit * row_count
        half_rows = slot_count // 2
        sel = selectors(width)
        deep = [((row_count, packed_width), BF)] * SLOTS
        flat = [((row_count, width), BF)] * SLOTS

        def blend_two(values):
            return run(blend_two_kernel, "blend", values + [sel], [(values[0].shape, BF)])[0]

        def to_slots(keep, got, kernel, extra, outs, add, empty, also=()):
            if unit > 2:
                keep = scatter_unit(add([keep, got]), add, unit // 4)
                got = jnp.broadcast_to(empty, keep.shape).astype(BF)
            scratch = [pltpu.VMEM(keep.shape, BF)] if extra else []
            parts = run(kernel, "to_slots", [keep, got] + extra, outs, scratch=scratch, also=also)
            return [parts[0]] + [swap(parts[j], j * unit) for j in range(1, SLOTS)]

        def spread(piece, first, second, third):
            parts = [piece, first, second, third]
            return parts + [swap(part, 1) for part in parts]

        def all_planes(pieces):
            return run(
                stack_kernel, "all_planes", pieces, [((axis_head,) + pieces[0].shape, BF)]
            )[0]

        held_out = pltpu.VMEM((axis_head, 4, head_cols // 4, width), BF)
        held_pair = pltpu.VMEM((2, 2) + held_out.shape, BF)
        pair_sems = pltpu.SemaphoreType.DMA((2, 2, 4 * axis_head))
        out_sems = pltpu.SemaphoreType.DMA((4 * axis_head,))
        ffn_sems = pltpu.SemaphoreType.DMA((axis_head, 8))
        tok_low, slot_low = ((block_len, width), BF), ((slot_count, width), BF)
        row_low, half_low = ((row_count, width), BF), ((half_rows, width), BF)
        tok_f32 = ((block_len, width), F32)

        mem_parts = fetch_start(mem)
        planes = from_planes(pieces)
        piece_ffn, tok, cot_tok, cot_mem = run(
            other_pieces_kernel,
            "other_pieces",
            [ffn_in_bias, ffn_in, ffn_out, tokens, cot_tokens, cot_memory],
            [((width + 16, hidden_width), BF), tok_low, tok_low, row_low],
            anys=5,
            scratch=[pltpu.SemaphoreType.DMA((6,))],
        )
        mem_picked = fetch_finish(mem_parts)
        shape = (2, axis_head) + pieces.shape[1:]
        rows_pack, rows_un = run(planes_kernel, "weight_planes", planes, [(shape, BF)] * 2)

        pack_first, pack_second = cross(rows_pack, 0), cross(rows_pack, 1)
        pack_third = cross(pack_first, 1)
        w_pack = spread(rows_pack, pack_first, pack_second, pack_third)
        rows_un = tie(rows_un, pack_third)
        un_first, un_second = cross(rows_un, 0), cross(rows_un, 1)
        ffn_rows = lax.all_gather(tie(piece_ffn, rows_pack), "head", axis=0)
        mem_slot = gather_unit(mem_picked)
        k_pack, v_pack, q_pack, keep, send = run(
            pack_forward_kernel,
            "pack_forward",
            [tok, mem_slot] + w_pack,
            [tok_low, tok_low, slot_low] + [((half_rows, packed_width), BF)] * 2,
            anys=8,
            scratch=[pltpu.VMEM((slot_count, packed_width), BF), held_pair, pair_sems],
        )
        got = swap(send, unit // 2)
        un_first = tie(un_first, keep)
        w_un = spread(rows_un, un_first, un_second, cross(un_first, 1))
        parts = to_slots(keep, got, blend_kernel, [sel], deep, blend_two, empty_row(width), [un_second])
        mem_result, mix_low, pack_ctx, pack_lse, grad_memsum, mem_vectors = run(
            memory_kernel,
            "memory_rows",
            parts + [sel, mem, cot_mem, mem_gain, mem_bias] + w_pack,
            [row_low, row_low, row_low]
            + [((row_count, TILE), F32), ((row_count, width), F32), ((8, width), F32)],
            anys=8,
            scratch=[held_out, out_sems],
            also=[w_un[3]],
        )
        mix_parts = fetch_start(mix_low)
        mix_picked = fetch_finish(mix_parts, w_un)
        mix_slot = gather_unit(mix_picked)
        ffn_rows = tie(ffn_rows, mix_slot)
        ffn_parts = [ffn_rows, swap(ffn_rows, 1)]
        k_un, v_un, q_un, tok_ctx, tok_lse, attn_normed, attn_inv = run(
            unpack_forward_kernel,
            "unpack_forward",
            [tok, mix_slot] + w_un,
            [slot_low, slot_low, tok_low, tok_low]
            + [((16, block_len), F32), tok_f32, ((block_len, 1), F32)],
            anys=8,
            scratch=[held_pair, pair_sems],
        )
        by_plane = (axis_head, block_len, hidden_width)
        held_ffn = pltpu.VMEM((2, axis_head, width, hidden_width), BF)
        plane_sems = pltpu.SemaphoreType.DMA((axis_head,))
        (
            out_result,
            attn_low,
            ffn_grad,
            mix_grad,
            mix_sum,
            out_vectors,
            hid_vec,
            gelu_out,
            hid_grad,
        ) = run(
            ffn_kernel,
            "ffn",
            [attn_normed, attn_inv, cot_tok, mem_result]
            + [attn_gain, attn_bias, out_gain, out_bias, ffn_out_bias]
            + ffn_parts,
            [((block_len + row_count, width), BF), tok_low, tok_low, tok_low, tok_f32]
            + [((8, width), F32), ((axis_head, 1, hidden_width), F32)]
            + [(by_plane, BF), (by_plane, BF)],
            anys=2,
            out_any=2,
            scratch=[
                held_ffn,
                pltpu.VMEM((axis_head, 16, hidden_width), BF),
                pltpu.VMEM((block_len, width), F32),
                pltpu.VMEM(by_plane, BF),
                pltpu.VMEM(by_plane, BF),
                ffn_sems,
                plane_sems,
                pltpu.SemaphoreType.DMA((axis_head, 2)),
            ],
        )
        out_rows = lax.all_gather(out_result, "head", axis=0)
        out_tokens, out_memory = out_rows[:, :block_len], out_rows[:, block_len:]

        role_info, other_info = role[None], 1 - role[None]
        ffn_operands = (attn_low, hid_grad, gelu_out, ffn_grad)

        def vectors_step(value, other):
            return run(total_kernel, "vectors", [value, other], [(value.shape, F32)])[0]

        small = run(
            vectors_kernel,
            "vectors",
            [mem_vectors, out_vectors, hid_vec],
            [((16, width), F32)],
        )[0]
        small_got = swap(small, 1)
        uq_grad, uk_part, uv_part, keep, send, tok_part = run(
            unpack_backward_kernel,
            "unpack_backward",
            [q_un, k_un, v_un, tok_ctx, tok_lse, mix_grad, mix_sum] + w_un,
            [tok_low, slot_low, slot_low, half_low, half_low, tok_f32],
            anys=8,
            scratch=[held_pair, pair_sems],
        )
        un_operands = (mix_slot, uk_part, uv_part, tok, uq_grad, tok_ctx, mix_grad)
        got = swap(send, unit // 2)
        small = vectors_step(small, small_got)
        small_got = swap(small, 2)
        if fast:
            ffn_sent = run_grid(ffn_weight_grad, other_info, ffn_operands, None)
            ffn_got = [swap(sent, 1) for sent in ffn_sent]
        parts = to_slots(keep, got, sum_kernel, [], flat, sum_rows, jnp.zeros((), BF))
        if fast:
            ffn_low, low_sent, ffn_high, high_sent = run_grid(
                ffn_weight_grad, role_info, ffn_operands, ffn_got
            )
        small = vectors_step(small, small_got)
        mem_mix_grad, packed = run(
            memory_back_kernel,
            "memory_rows_backward",
            parts + [sel, grad_memsum, pack_ctx, pack_lse] + w_pack,
            [row_low, ((row_count, packed_width), BF)],
            anys=8,
            scratch=[held_out, out_sems],
        )
        back_parts = fetch_start(packed)
        if fast:
            un_sent = run_grid(attention_weight_grad, other_info, un_operands, axis_head, None)
        back_picked = fetch_finish(back_parts, [out_rows])
        if fast:
            low_got = cross(tie(low_sent, back_picked), 0)
            un_got = swap(tie(un_sent, back_picked), 1)
        back = gather_unit(back_picked)
        pq_part, pk_grad, pv_grad, grad_tokens, keep, send = run(
            pack_backward_kernel,
            "pack_backward",
            [back, sel, q_pack, k_pack, v_pack, tok_part] + w_pack,
            [slot_low, tok_low, tok_low, tok_low, half_low, half_low],
            anys=8,
            scratch=[held_pair, pair_sems],
        )
        grad_tokens = lax.all_gather(grad_tokens, "head", axis=0)
        pack_operands = (tok, pk_grad, pv_grad, mem_slot, pq_part, pack_ctx, mem_mix_grad)
        got = swap(send, unit // 2)
        if fast:
            ffn_low, low_sent = run_grid(add_pairs, ffn_low, low_got)
            high_got = cross(tie(high_sent, ffn_low), 0)
            un_kept, un_sent = run_grid(
                attention_weight_grad, role_info, un_operands, axis_head, un_got
            )
            pack_sent = run_grid(attention_weight_grad, other_info, pack_operands, axis_head, None)
        step = 4
        while step < axis_seq:
            small = vectors_step(small, swap(small, step))
            step *= 2
        parts = to_slots(keep, got, sum_kernel, [], flat, sum_rows, jnp.zeros((), BF))

        rows = (quarter, hidden_width)
        half = (quarter // 2, hidden_width)
        pair_rows = (2, quarter, head_cols)
        pair_half = (2, quarter // 2, head_cols)

        def pairs_of(shape):
            return [((2,) + shape, F32), ((2,) + shape, BF)]

        def middle(kept, got, shape):
            keep, send = run(
                middle_kernel, "plane_middle", [kept, got], [(shape, F32), (shape, BF)]
            )
            return keep, over(send, 2)

        def ffn_blocks(kept, got):
            operands = [kept[0], got[0], kept[1], got[1]]
            keep, send = run(ffn_blocks_kernel, "plane_blocks", operands, pairs_of(rows))
            return keep, over(send, 1)

        def ffn_total(kept, got):
            scratch = [pltpu.VMEM(rows, F32)]
            keep, send = run(
                ffn_total_kernel, "plane_total", [kept, got], [(half, F32)] * 2, scratch=scratch
            )
            return [keep, swap(send, 1)]

        def ffn_final(halves):
            return run(ffn_final_kernel, "weight_rows", halves, [(half, F32)] * 2)

        def attention_blocks(kept, got):
            keep, send = run(
                attention_blocks_kernel,
                "plane_blocks",
                [kept, got],
                pairs_of(pair_rows),
                scratch=[
                    pltpu.VMEM((2, quarter, width), F32),
                    pltpu.VMEM((axis_head,) + pair_rows, F32),
                ],
            )
            return keep, over(send, 1)

        def attention_total(kept, got):
            keep, send = run(
                functools.partial(attention_total_kernel, planes=axis_head),
                "plane_total",
                [kept, got],
                [(pair_half, F32)] * 2,
                scratch=[pltpu.VMEM(pair_rows, F32)],
            )
            return [keep, swap(send, 1)]

        def attention_final(halves):
            return run(
                functools.partial(attention_final_kernel, planes=axis_head),
                "weight_rows",
                halves,
                [(pair_half[1:], F32)] * 3 + [((quarter // 2 // axis_head, width), F32)],
            )

        def scatter(value, axis, dim):
            return lax.psum_scatter(value, axis, scatter_dimension=dim, tiled=True)

        def by_columns(grad):
            grad = scatter(grad, "seq", 0).reshape(-1, axis_head, head_cols)
            return scatter(grad.transpose(1, 0, 2), "head", 0)[0].astype(F32)

        def by_rows(grad):
            grad = scatter(grad.reshape(axis_head, -1, width), "seq", 1)
            return scatter(grad, "head", 0)[0].astype(F32)

        def product(left, right):
            return dot_tn(left, right).astype(BF)

        def attention_simple(operands):
            kv, dk, dv, q_rows, dq, left, right = operands
            first = [by_columns(product(a, b)) for a, b in ((kv, dk), (kv, dv), (q_rows, dq))]
            return first + [by_rows(product(left, right))]

        if fast:
            ffn_high, high_sent = run_grid(add_pairs, ffn_high, high_got)
            low_got, high_got = cross(tie(low_sent, ffn_high), 1), cross(high_sent, 1)
            pack_got = swap(tie(pack_sent, ffn_high), 1)
            pack_kept, pack_sent = run_grid(
                attention_weight_grad, role_info, pack_operands, axis_head, pack_got
            )
        done = [out_tokens, out_memory]
        total = run(
            memory_total_kernel, "memory_total", [grad_memsum] + parts, [row_low], also=done
        )[0]
        grad_planes = from_planes(total)
        if fast:
            un_got = cross(tie(un_sent, total), 0)
            blocks = ffn_blocks([ffn_low, ffn_high], [low_got, high_got])
            pack_got = cross(tie(pack_sent, blocks[0]), 0)
            un_kept, un_sent = run_grid(add_pairs, un_kept, un_got)
            un_got = cross(un_sent, 1)
            pack_kept, pack_sent = run_grid(add_pairs, pack_kept, pack_got)
            pack_got = cross(pack_sent, 1)
            blocks = middle(*blocks, rows)
            un_blocks = attention_blocks(un_kept, un_got)
            pack_blocks = attention_blocks(pack_kept, pack_got)
            halves = ffn_total(*blocks)
            grad_memory = all_planes(grad_planes)
            un_blocks = middle(*un_blocks, pair_rows)
            pack_blocks = middle(*pack_blocks, pair_rows)
            small_planes = direct_planes(tie(small, grad_memory))
            fi_grad, fo_grad = ffn_final(halves)
            un_halves = attention_total(*un_blocks)
            small = run(
                plane_vectors_kernel,
                "vectors",
                small_planes,
                [(small.shape, F32)],
                scratch=[pltpu.VMEM((axis_head,) + small.shape, F32)],
            )[0]
            pack_halves = attention_total(*pack_blocks)
            un_grads = attention_final(un_halves)
            pack_grads = attention_final(pack_halves)
        else:
            grad_memory = all_planes(grad_planes)
            small_planes = direct_planes(small)
            small = run(
                plane_vectors_kernel,
                "vectors",
                small_planes,
                [(small.shape, F32)],
                scratch=[pltpu.VMEM((axis_head,) + small.shape, F32)],
            )[0]
            un_grads = attention_simple(un_operands)
            pack_grads = attention_simple(pack_operands)
            fi_grad = jnp.stack([product(attn_low, hid_grad[p]) for p in range(axis_head)])
            fi_grad = scatter(scatter(fi_grad, "seq", 1), "head", 0)[0].astype(F32)
            fo_grad = jnp.stack([product(gelu_out[p], ffn_grad) for p in range(axis_head)])
            fo_grad = scatter(scatter(fo_grad, "seq", 1), "head", 0)[0].astype(F32)

        share = width // axis_seq
        vectors = lax.dynamic_slice_in_dim(small[:7], seq_index * share, share, 1)
        fib = mine(small[7 : 7 + axis_head].reshape(axis_head, -1))
        fib = lax.dynamic_slice_in_dim(fib, seq_index * share, share, 0)
        return (
            out_tokens,
            out_memory,
            grad_tokens,
            grad_memory,
            pack_grads[2],
            pack_grads[0],
            pack_grads[1],
            pack_grads[3],
            un_grads[2],
            un_grads[0],
            un_grads[1],
            un_grads[3],
            fi_grad,
            fib,
            fo_grad,
            vectors[0],
            vectors[1],
            vectors[2],
            vectors[3],
            vectors[4],
            vectors[5],
            vectors[6],
        )

    return local


def solution(mesh):
    rows = P(None, "seq", None)
    by_col, by_row, both = P(None, "head"), P("head", None), P("seq", "head")
    wide_rows = P(("head", "seq"), None)
    in_specs = (
        (rows, rows, P())
        + (by_col, by_col, by_col, by_row)
        + (by_col, by_col, by_col, by_row)
        + (by_col, P("head"), by_row)
        + (P(),) * 7
        + (rows, rows)
    )
    out_specs = (
        (rows,) * 4
        + (both, both, both, wide_rows)
        + (both, both, both, wide_rows)
        + (both, P(("head", "seq")), wide_rows)
        + (P("seq"),) * 7
    )
    local = make_local(mesh.shape["seq"], mesh.shape["head"])
    return jax.shard_map(local, mesh=mesh, in_specs=in_specs, out_specs=out_specs, check_vma=False)
```

```python
import functools
import math

import jax
import jax.numpy as jnp
import numpy as np
from jax import lax
from jax.experimental import pallas as pl
from jax.experimental.pallas import tpu as pltpu
from jax.sharding import PartitionSpec as P

HD = 64
SLOTS = 4
EPSILON = 1e-05
NEG_FILL = -1e30
BF = jnp.bfloat16
F32 = jnp.float32


def dot(left, right):
    return jnp.dot(left, right, preferred_element_type=F32)


def dot_nt(left, right):
    return lax.dot_general(left, right, (((1,), (1,)), ((), ())), preferred_element_type=F32)


def dot_tn(left, right):
    return lax.dot_general(left, right, (((0,), (0,)), ((), ())), preferred_element_type=F32)


TILE = 2 * HD
PARTS = 3
MIB = 1024 * 1024
SMALL = pl.CostEstimate(flops=1, bytes_accessed=1, transcendentals=0)


ROLE, WALK, OTHER_WALK, PLANE, SLOT, UNIT, HALF, BIT, OTHER_BIT, INFO = 0, 1, 5, 9, 10, 11, 12, 13, 14, 16


def call(kernel, name, operands, outs, anys=0, scratch=(), flops=0, vmem=None, out_any=0, after=(), smem=1):
    def body(*refs):
        kernel(*refs[: len(operands)], *refs[len(operands) + len(after) :])

    if vmem is None:
        vmem = 60 if anys or name == "attention_weight_grad" else 16
    vm, anywhere = pl.BlockSpec(memory_space=pltpu.VMEM), pl.BlockSpec(memory_space=pl.ANY)
    specs = [pl.BlockSpec(memory_space=pltpu.SMEM)] * smem
    specs += [vm] * (len(operands) - smem - anys) + [anywhere] * (anys + len(after))
    return pl.pallas_call(
        body,
        out_shape=[jax.ShapeDtypeStruct(s, d) for s, d in outs],
        in_specs=specs,
        out_specs=[vm] * (len(outs) - out_any) + [anywhere] * out_any,
        scratch_shapes=list(scratch),
        compiler_params=pltpu.CompilerParams(vmem_limit_bytes=vmem * MIB),
        cost_estimate=SMALL,
        name=name,
    )(*operands, *after)


def info_kernel(places, lengths, info, unit, block_len):
    seq, head = places[0], places[1]
    role, quad = lax.rem(seq, 2), lax.rem(seq // 2, 4)
    first, second = 1 + role, 2 - role
    info[ROLE] = role
    for at, step in enumerate((0, first, second, 3)):
        info[WALK + at] = quad ^ step
    for at, step in enumerate((0, second, first, 3)):
        info[OTHER_WALK + at] = quad ^ step
    info[PLANE] = head
    end = 0
    slot = 0
    for at in range(SLOTS):
        end = end + lengths[head, at]
        slot = slot + (end <= seq * block_len).astype(jnp.int32)
    info[SLOT] = slot
    info[UNIT] = seq // unit
    info[HALF] = lax.rem(seq, unit) // (unit // 2)
    info[BIT] = jnp.where(role == 0, lax.rem(quad, 2), quad // 2)
    info[OTHER_BIT] = jnp.where(role == 0, quad // 2, lax.rem(quad, 2))
    info[INFO - 1] = 0


def planes_kernel(info, first, second, third, fourth, *outs):
    for at, ref in enumerate((first, second, third, fourth)):
        for mat in range(4):
            out = outs[mat // 2]
            out[mat % 2, info[PLANE] ^ at] = ref[mat]


def first_pieces_kernel(places, lengths, memory, *refs, unit, block_len):
    weights, (info, piece, mem, sems) = refs[:8], refs[8:]
    info_kernel(places, lengths, info, unit, block_len)
    copy_mem = pltpu.make_async_copy(memory.at[places[1]], mem, sems.at[4])
    copy_mem.start()
    rows = piece.shape[1]
    at = pl.ds(pl.multiple_of(info[WALK] * rows, rows), rows)
    for role, chosen in enumerate(((0, 1, 4, 5), (2, 3, 6, 7))):

        @pl.when(info[ROLE] == role)
        def _(chosen=chosen):
            copies = [
                pltpu.make_async_copy(weights[which].at[at], piece.at[mat], sems.at[mat])
                for mat, which in enumerate(chosen)
            ]
            for copy in copies:
                copy.start()
            for copy in copies:
                copy.wait()

    copy_mem.wait()


def other_pieces_kernel(info, bias, *refs):
    ffn_in, ffn_out, tokens, cot_tok, cot_mem = refs[:5]
    ffn, tok, cot_t, cot_m, sems = refs[5:]
    plane = info[PLANE]
    copies = []
    for at, (source, to) in enumerate(((tokens, tok), (cot_tok, cot_t), (cot_mem, cot_m))):
        copies.append(pltpu.make_async_copy(source.at[plane], to, sems.at[2 + at]))
    for copy in copies:
        copy.start()
    rows = ffn.shape[0] - 16
    for role, source in enumerate((ffn_in, ffn_out)):

        @pl.when(info[ROLE] == role)
        def _(source=source):
            copy = pltpu.make_async_copy(source, ffn.at[pl.ds(0, rows)], sems.at[5])
            copy.start()
            copy.wait()

    value = bias[...][None]
    parts = []
    for part in range(PARTS):
        low = value.astype(BF).astype(F32)
        parts.append(low)
        value = value - low
    parts.append(jnp.zeros((16 - PARTS, bias.shape[0]), F32))
    ffn[rows:] = jnp.concatenate(parts, axis=0).astype(BF)
    for copy in copies:
        copy.wait()


def vectors_kernel(info, mem_vectors, out_vectors, hid_vec, out):
    out[...] = jnp.zeros(out.shape, F32)
    out[0:1] = out_vectors[0:1]
    out[1:3] = mem_vectors[0:2]
    out[3:5] = out_vectors[3:5]
    out[5:7] = out_vectors[1:3]
    for plane in range(hid_vec.shape[0]):
        out[7 + plane : 8 + plane] = hid_vec[plane]


def total_kernel(info, *refs):
    total = refs[0][...]
    for ref in refs[1:-1]:
        total = total + ref[...]
    refs[-1][...] = total


def plane_vectors_kernel(info, first, second, third, fourth, out, held):
    planes = held.shape[0]
    for at, ref in enumerate((first, second, third, fourth)):
        held[info[PLANE] ^ at] = ref[...]
    total = held[0]
    for plane in range(1, planes):
        total = total + held[plane]
    out[...] = total


def memory_total_kernel(info, base, first, second, third, fourth, out):
    total = base[...]
    for ref in (first, second, third, fourth):
        total = total + ref[...].astype(F32)
    out[...] = total.astype(BF)


def pick_kernel(info, first, second, third, fourth, out, sem):
    for at, ref in enumerate((first, second, third, fourth)):

        @pl.when(info[SLOT] == (info[UNIT] ^ at))
        def _(ref=ref):
            copy = pltpu.make_async_copy(ref, out, sem)
            copy.start()
            copy.wait()


def tie(value, *after):
    anywhere = pl.BlockSpec(memory_space=pl.ANY)
    return pl.pallas_call(
        lambda *refs: None,
        out_shape=jax.ShapeDtypeStruct(value.shape, value.dtype),
        in_specs=[anywhere] * (1 + len(after)),
        out_specs=anywhere,
        input_output_aliases={0: 0},
        compiler_params=pltpu.CompilerParams(vmem_limit_bytes=16 * MIB),
        cost_estimate=SMALL,
        name="tie",
    )(value, *after)


def stack_kernel(info, first, second, third, fourth, out):
    for at, ref in enumerate((first, second, third, fourth)):
        out[info[PLANE] ^ at] = ref[...]


def put_halves(info, keep, send, value):
    size = keep.shape[0]

    @pl.when(info[HALF] == 0)
    def _():
        keep[...] = value[:size]
        send[...] = value[size:]

    @pl.when(info[HALF] == 1)
    def _():
        keep[...] = value[size:]
        send[...] = value[:size]


def put_slots(info, outs, value, empty):
    for at, out in enumerate(outs):
        here = info[SLOT] == (info[UNIT] ^ at)

        @pl.when(here)
        def _(out=out):
            out[...] = value

        @pl.when(jnp.logical_not(here))
        def _(out=out):
            out[...] = empty


def blend_values(given, sel, width):
    lses = [dot(c[:, width:], sel[0]) for c in given]
    top = lses[0]
    for lse in lses[1:]:
        top = jnp.maximum(top, lse)
    shares = [jnp.exp(lse - top) for lse in lses]
    total = shares[0]
    for share in shares[1:]:
        total = total + share
    inv = 1.0 / total
    low = lax.broadcasted_iota(jnp.int32, (1, TILE), 1) < HD
    tiles = []
    for pair in range(width // TILE):
        cols = slice(pair * TILE, (pair + 1) * TILE)
        ctx = None
        for share, c in zip(shares, given):
            share = share * inv
            weight = jnp.where(
                low, share[:, 2 * pair : 2 * pair + 1], share[:, 2 * pair + 1 : 2 * pair + 2]
            )
            term = weight * c[:, cols].astype(F32)
            ctx = term if ctx is None else ctx + term
        tiles.append(ctx.astype(BF))
    return tiles, top + jnp.log(total)


def blend_kernel(info, keep, got, sel, *outs):
    outs, value = outs[:SLOTS], outs[SLOTS]
    width = value.shape[1] - TILE
    heads = width // HD
    tiles, lse = blend_values((keep, got), sel, width)
    for pair, tile in enumerate(tiles):
        value[:, pair * TILE : (pair + 1) * TILE] = tile
    value[:, width:] = as_parts(lse, heads).astype(BF)
    col = lax.broadcasted_iota(jnp.int32, value.shape, 1)
    fill = jnp.where((col >= width) & (col < width + heads), NEG_FILL, 0.0)
    put_slots(info, outs, value[...], fill.astype(BF))


def sum_kernel(info, keep, got, *outs):
    total = (keep[...].astype(F32) + got[...].astype(F32)).astype(BF)
    put_slots(info, outs, total, jnp.zeros(total.shape, BF))


def start_weights(info, pieces, held, sems, mats=(0, 1)):
    planes = held.shape[2]
    for mat in mats:
        for j in range(4):
            mine = (info[ROLE], info[WALK + j], pieces[j])
            theirs = (1 - info[ROLE], info[OTHER_WALK + j], pieces[4 + j])
            for role, unit, piece in (mine, theirs):
                for plane in range(planes):
                    pltpu.make_async_copy(
                        piece.at[mat, plane],
                        held.at[role, mat, plane, unit],
                        sems.at[role, mat, j * planes + plane],
                    ).start()


def weight(held, sems, pieces, role, mat):
    planes = held.shape[2]
    for j in range(4):
        for plane in range(planes):
            pltpu.make_async_copy(
                pieces[j].at[mat, plane],
                held.at[role, mat, plane, j],
                sems.at[role, mat, j * planes + plane],
            ).wait()
    return matrix(held, role, mat)


def matrix(held, *index):
    block = held[index]
    return block.reshape(-1, block.shape[-1])


def half_masks():
    lane = lax.broadcasted_iota(jnp.int32, (1, TILE), 1)
    low = (lane < HD).astype(F32).astype(BF)
    return low, (lane >= HD).astype(F32).astype(BF)


def put_scalars(rows):
    count = len(rows)
    stack = jnp.concatenate(rows * PARTS, axis=0)
    extra = TILE - stack.shape[0]
    stack = jnp.concatenate([stack, jnp.zeros((extra, stack.shape[1]), F32)], axis=0)
    return stack.T


def as_parts(wide, heads, offset=0):
    first = wide.astype(BF).astype(F32)
    rest = wide - first
    second = rest.astype(BF).astype(F32)
    third = rest - second
    lane = lax.broadcasted_iota(jnp.int32, wide.shape, 1) - offset
    return jnp.where(
        lane < 0,
        0.0,
        jnp.where(
            lane < heads,
            first,
            jnp.where(lane < 2 * heads, second, jnp.where(lane < 3 * heads, third, 0.0)),
        ),
    )


def norm_stats(summed):
    centre = summed - jnp.mean(summed, axis=-1, keepdims=True)
    inv = lax.rsqrt(jnp.mean(centre * centre, axis=-1, keepdims=True) + EPSILON)
    return centre * inv, inv


def norm_pull(upstream, normed, inv, gain):
    scaled = upstream * gain
    return inv * (
        scaled
        - jnp.mean(scaled, axis=-1, keepdims=True)
        - normed * jnp.mean(scaled * normed, axis=-1, keepdims=True)
    )


def head_forward(q_tile, k_tile, v_tile, masks):
    parts, rows = [], []
    for side in range(2):
        scores = dot_nt(k_tile * masks[side], q_tile)
        top = jnp.max(scores, axis=0, keepdims=True)
        weights = jnp.exp(scores - top)
        den = jnp.sum(weights, axis=0, keepdims=True)
        num = dot_tn(v_tile, weights.astype(BF))[side * HD : (side + 1) * HD]
        parts.append(num * (1.0 / den))
        rows.append(top + jnp.log(den))
    return jnp.concatenate(parts, axis=0), rows


def head_backward(q_tile, k_tile, v_tile, g_tile, lses, deltas, masks):
    dq, dk, dv = [], None, None
    for side in range(2):
        q_side, g_side = q_tile * masks[side], g_tile * masks[side]
        weights = jnp.exp(dot_nt(k_tile, q_side) - lses[side])
        dscores = (weights * (dot_nt(v_tile, g_side) - deltas[side])).astype(BF)
        weights = weights.astype(BF)
        dq.append(dot_tn(k_tile, dscores)[side * HD : (side + 1) * HD])
        dk_side, dv_side = dot(dscores, q_side), dot(weights, g_side)
        dk = dk_side if dk is None else dk + dk_side
        dv = dv_side if dv is None else dv + dv_side
    return jnp.concatenate(dq, axis=0), dk, dv


def pack_forward_kernel(
    info, tok, mem, *refs
):
    pieces, (k_out, v_out, q_out, keep, send, packed, held, sems) = refs[:8], refs[8:]
    width = tok.shape[1]
    heads = width // HD
    start_weights(info, pieces, held, sems)
    k_out[...] = dot_nt(tok[...], weight(held, sems, pieces, 0, 0)).astype(BF)
    v_out[...] = dot_nt(tok[...], weight(held, sems, pieces, 0, 1)).astype(BF)
    q_out[...] = dot_nt(mem[...], weight(held, sems, pieces, 1, 0)).astype(BF) * BF(HD**-0.5)
    masks = half_masks()
    rows = []
    for pair in range(heads // 2):
        cols = slice(pair * TILE, (pair + 1) * TILE)
        ctx, pair_rows = head_forward(q_out[:, cols], k_out[:, cols], v_out[:, cols], masks)
        packed[:, cols] = ctx.T.astype(BF)
        rows += pair_rows
    packed[:, width:] = as_parts(put_scalars(rows), heads).astype(BF)
    put_halves(info, keep, send, packed)
    weight(held, sems, pieces, 1, 1)


def start_out_matrix(info, pieces, held, sems):
    planes = held.shape[0]
    for j in range(4):
        for role, piece, unit in ((1, pieces[j], WALK + j), (0, pieces[4 + j], OTHER_WALK + j)):

            @pl.when(info[ROLE] == role)
            def _(piece=piece, unit=unit, j=j):
                for plane in range(planes):
                    pltpu.make_async_copy(
                        piece.at[1, plane], held.at[plane, info[unit]], sems.at[j * planes + plane]
                    ).start()


def out_matrix(pieces, held, sems):
    planes = held.shape[0]
    for j in range(4):
        for plane in range(planes):
            pltpu.make_async_copy(
                pieces[j].at[1, plane], held.at[plane, j], sems.at[j * planes + plane]
            ).wait()
    return matrix(held, Ellipsis)


def memory_kernel(info, c0, c1, c2, c3, sel, mem, cot, gain, bias, *refs):
    pieces, outs = refs[:8], refs[8:]
    result, mix_low, ctx_out, lse_out, grad_sum, vectors, held, sems = outs
    width = mem.shape[1]
    heads = width // HD
    start_out_matrix(info, pieces, held, sems)
    tiles, lse = blend_values((c0, c1, c2, c3), sel, width)
    lse_out[...] = lse
    for pair, tile in enumerate(tiles):
        ctx_out[:, pair * TILE : (pair + 1) * TILE] = tile
    mix = dot(ctx_out[...], out_matrix(pieces, held, sems))
    mix_low[...] = mix.astype(BF)
    normed, inv_std = norm_stats(mix + mem[...].astype(F32))
    gain_row = gain[...][None]
    result[...] = (normed * gain_row + bias[...][None]).astype(BF)
    upstream = cot[...].astype(F32)
    grad_sum[...] = norm_pull(upstream, normed, inv_std, gain_row)
    vectors[0:1] = jnp.sum(upstream * normed, axis=0, keepdims=True)
    vectors[1:2] = jnp.sum(upstream, axis=0, keepdims=True)


def unpack_forward_kernel(info, tok, mix, *refs):
    pieces, outs = refs[:8], refs[8:]
    k_out, v_out, q_out, ctx_out, lse_out, normed_out, inv_out, held, sems = outs
    width = tok.shape[1]
    heads = width // HD
    start_weights(info, pieces, held, sems)
    k_out[...] = dot_nt(mix[...], weight(held, sems, pieces, 0, 0)).astype(BF)
    v_out[...] = dot_nt(mix[...], weight(held, sems, pieces, 0, 1)).astype(BF)
    q_out[...] = dot_nt(tok[...], weight(held, sems, pieces, 1, 0)).astype(BF) * BF(HD**-0.5)
    masks = half_masks()
    for pair in range(heads // 2):
        cols = slice(pair * TILE, (pair + 1) * TILE)
        ctx, rows = head_forward(q_out[:, cols], k_out[:, cols], v_out[:, cols], masks)
        ctx_out[:, cols] = ctx.T.astype(BF)
        lse_out[2 * pair : 2 * pair + 1] = rows[0]
        lse_out[2 * pair + 1 : 2 * pair + 2] = rows[1]
    summed = dot(ctx_out[...], weight(held, sems, pieces, 1, 1)) + tok[...].astype(F32)
    normed, inv = norm_stats(summed)
    normed_out[...] = normed
    inv_out[...] = inv


GELU_A = math.sqrt(2.0 / math.pi)
GELU_B = 0.044715
CHUNK = 256


def start_ffn(info, pieces, held, sems):
    planes, rows = held.shape[1], held.shape[2]
    quarter = rows // 4
    for plane in range(planes):
        for j, role in enumerate((info[ROLE], 1 - info[ROLE])):
            for part in range(4):
                at = pl.ds(part * quarter, quarter)
                pltpu.make_async_copy(
                    pieces[j].at[plane, at], held.at[role, plane, at], sems.at[plane, 4 * j + part]
                ).start()


def wait_ffn(pieces, held, sems, plane):
    rows = held.shape[2]
    quarter = rows // 4
    for j in range(2):
        for part in range(4):
            at = pl.ds(part * quarter, quarter)
            pltpu.make_async_copy(
                pieces[j].at[0, at], held.at[j, plane, at], sems.at[plane, 4 * j + part]
            ).wait()


def ffn_kernel(info, normed_in, inv_in, cot, mem_result, *refs):
    rows, refs = [r[...][None] for r in refs[:5]], refs[5:]
    attn_gain, attn_bias, out_gain, out_bias, ffn_bias = rows
    pieces, outs = refs[:2], refs[2:]
    out, attn_low, ffn_grad, mix_grad, mix_sum, vectors, hid_vec, gelu_out, hid_out = outs[:9]
    held, bias, total, gelu_low, slope, sems, bias_sem, out_sems = outs[9:]
    planes, width = held.shape[1], held.shape[2]
    bias_at = pl.ds(width, 16)
    bias_copies = [
        pltpu.make_async_copy(pieces[0].at[plane, bias_at], bias.at[plane], bias_sem.at[plane])
        for plane in range(planes)
    ]
    for copy in bias_copies:
        copy.start()
    start_ffn(info, pieces, held, sems)
    attn = normed_in[...] * attn_gain + attn_bias
    attn_low[...] = attn.astype(BF)
    total[...] = attn + ffn_bias
    for copy in bias_copies:
        copy.wait()
    out_copies = []
    for plane in range(planes):
        wait_ffn(pieces, held, sems, plane)
        parts = bias[plane].astype(F32)
        shift = parts[0:1] + parts[1:2] + parts[2:3]
        for start in range(0, held.shape[3], CHUNK):
            cols = slice(start, start + CHUNK)
            hidden = dot(attn_low[...], held[0, plane, :, cols]) + shift[:, cols]
            square = hidden * hidden
            half = 1.0 / (1.0 + jnp.exp(hidden * (-2.0 * GELU_A - 2.0 * GELU_A * GELU_B * square)))
            gelu = hidden * half
            gelu_low[plane, :, cols] = gelu.astype(BF)
            inner = 2.0 * GELU_A + 6.0 * GELU_A * GELU_B * square
            slope[plane, :, cols] = (half + gelu * (1.0 - half) * inner).astype(BF)
        total[...] += dot(gelu_low[plane], held[1, plane])
        copy = pltpu.make_async_copy(gelu_low.at[plane], gelu_out.at[plane], out_sems.at[plane, 0])
        copy.start()
        out_copies.append(copy)
    out_normed, out_inv = norm_stats(total[...])
    count = normed_in.shape[0]
    out[:count] = (out_normed * out_gain + out_bias).astype(BF)
    out[count:] = mem_result[...]
    upstream = cot[...].astype(F32)
    grad = norm_pull(upstream, out_normed, out_inv, out_gain)
    ffn_grad[...] = grad.astype(BF)
    vectors[0:1] = jnp.sum(grad.astype(BF).astype(F32), axis=0, keepdims=True)
    vectors[1:2] = jnp.sum(upstream * out_normed, axis=0, keepdims=True)
    vectors[2:3] = jnp.sum(upstream, axis=0, keepdims=True)
    total[...] = grad
    for plane in range(planes):
        for start in range(0, held.shape[3], CHUNK):
            cols = slice(start, start + CHUNK)
            pulled = dot_nt(ffn_grad[...], held[1, plane, cols]) * slope[plane, :, cols].astype(F32)
            low = pulled.astype(BF)
            slope[plane, :, cols] = low
            hid_vec[plane, :, cols] = jnp.sum(low.astype(F32), axis=0, keepdims=True)
        total[...] += dot_nt(slope[plane], held[0, plane])
        copy = pltpu.make_async_copy(slope.at[plane], hid_out.at[plane], out_sems.at[plane, 1])
        copy.start()
        out_copies.append(copy)
    upstream = total[...]
    normed = normed_in[...]
    vectors[3:4] = jnp.sum(upstream * normed, axis=0, keepdims=True)
    vectors[4:5] = jnp.sum(upstream, axis=0, keepdims=True)
    grad = norm_pull(upstream, normed, inv_in[...], attn_gain)
    mix_sum[...] = grad
    mix_grad[...] = grad.astype(BF)
    for copy in out_copies:
        copy.wait()


def unpack_backward_kernel(info, q_in, k_in, v_in, ctx, lse, mix_grad, mix_sum, *refs):
    pieces, outs = refs[:8], refs[8:]
    uq, uk, uv, keep, send, tok_part, held, sems = outs
    width = q_in.shape[1]
    heads = width // HD
    start_weights(info, pieces, held, sems, (1, 0))
    masks = half_masks()
    ctx_grad = dot_nt(mix_grad[...], weight(held, sems, pieces, 1, 1))
    ctx_low = ctx_grad.astype(BF)
    for pair in range(heads // 2):
        cols = slice(pair * TILE, (pair + 1) * TILE)
        product = ctx_grad[:, cols] * ctx[:, cols].astype(F32)
        first = product.astype(BF)
        second = (product - first.astype(F32)).astype(BF)
        deltas = []
        for side in range(2):
            picker = jnp.broadcast_to(masks[side], (16, TILE))
            deltas.append((dot_nt(picker, first) + dot_nt(picker, second))[0:1])
        lses = [lse[2 * pair : 2 * pair + 1], lse[2 * pair + 1 : 2 * pair + 2]]
        dq, dk, dv = head_backward(
            q_in[:, cols], k_in[:, cols], v_in[:, cols], ctx_low[:, cols], lses, deltas, masks
        )
        uq[:, cols] = (dq.T * (HD**-0.5)).astype(BF)
        uk[:, cols] = dk.astype(BF)
        uv[:, cols] = dv.astype(BF)
    mix_part = dot(uk[...], weight(held, sems, pieces, 0, 0))
    mix_part = mix_part + dot(uv[...], weight(held, sems, pieces, 0, 1))
    put_halves(info, keep, send, mix_part.astype(BF))
    tok_part[...] = mix_sum[...] + dot(uq[...], weight(held, sems, pieces, 1, 0))


def memory_back_kernel(info, c0, c1, c2, c3, sel, grad_sum, ctx, lse, *refs):
    pieces, outs = refs[:8], refs[8:]
    mix_grad, packed, held, sems = outs
    width = ctx.shape[1]
    heads = width // HD
    start_out_matrix(info, pieces, held, sems)
    total = grad_sum[...]
    for c in (c0, c1, c2, c3):
        total = total + c[...].astype(F32)
    mix_grad[...] = total.astype(BF)
    pulled = dot_nt(mix_grad[...], out_matrix(pieces, held, sems))
    packed[:, :width] = pulled.astype(BF)
    delta = jnp.zeros(lse.shape, F32)
    for pair in range(heads // 2):
        cols = slice(pair * TILE, (pair + 1) * TILE)
        product = pulled[:, cols] * ctx[:, cols].astype(F32)
        first = product.astype(BF)
        second = (product - first.astype(F32)).astype(BF)
        delta = delta + dot(first, sel[2 + pair]) + dot(second, sel[2 + pair])
    scalars = as_parts(lse[...], heads) + as_parts(delta, heads, PARTS * heads)
    packed[:, width:] = scalars.astype(BF)


def pack_backward_kernel(info, back, sel, q_in, k_in, v_in, tok_part, *refs):
    pieces, outs = refs[:8], refs[8:]
    pq, pk, pv, tok_grad, keep, send, held, sems = outs
    width = q_in.shape[1]
    heads = width // HD
    start_weights(info, pieces, held, sems)
    masks = half_masks()
    lse = dot(back[:, width:], sel[0]).T
    delta = dot(back[:, width:], sel[1]).T
    for pair in range(heads // 2):
        cols = slice(pair * TILE, (pair + 1) * TILE)
        lses = [lse[2 * pair : 2 * pair + 1], lse[2 * pair + 1 : 2 * pair + 2]]
        deltas = [delta[2 * pair : 2 * pair + 1], delta[2 * pair + 1 : 2 * pair + 2]]
        dq, dk, dv = head_backward(
            q_in[:, cols], k_in[:, cols], v_in[:, cols], back[:, cols], lses, deltas, masks
        )
        pq[:, cols] = (dq.T * (HD**-0.5)).astype(BF)
        pk[:, cols] = dk.astype(BF)
        pv[:, cols] = dv.astype(BF)
    total = dot(pk[...], weight(held, sems, pieces, 0, 0))
    total = total + dot(pv[...], weight(held, sems, pieces, 0, 1))
    count = tok_part.shape[0]
    tok_grad[:count] = (total + tok_part[...]).astype(BF)
    tok_grad[count:] = jnp.zeros((tok_grad.shape[0] - count, tok_grad.shape[1]), BF)
    put_halves(info, keep, send, dot(pq[...], weight(held, sems, pieces, 1, 0)).astype(BF))
    weight(held, sems, pieces, 1, 1)


def selectors(width):
    heads = width // HD
    lane = np.arange(TILE)
    inside = lane < PARTS * heads
    first = inside[:, None] & inside[None, :] & (lane[:, None] % heads == lane[None, :] % heads)
    shifted = lane - PARTS * heads
    second = (shifted >= 0) & (shifted < PARTS * heads)
    second = second[:, None] & inside[None, :] & (shifted[:, None] % heads == lane[None, :] % heads)
    rows = [first, second]
    target = (shifted >= 0) & (shifted < PARTS * heads)
    for pair in range(heads // 2):
        head = 2 * pair + (lane >= HD)
        rows.append(target[None, :] & (head[:, None] == (shifted % heads)[None, :]))
    return jnp.asarray(np.stack(rows).astype(np.float32), BF)


def pair_units(info):
    role, quad = info[ROLE], info[WALK]
    bit = jnp.where(role == 0, lax.rem(quad, 2), quad // 2)
    step, scale = jnp.where(role == 0, 2, 1), jnp.where(role == 0, 1, 2)
    keep = [bit * scale + at * step for at in range(2)]
    send = [(1 - bit) * scale + at * step for at in range(2)]
    return keep, send


def split_pairs(info, value, keep, send, rows):
    for units, out in zip(pair_units(info), (keep, send)):
        for at, unit in enumerate(units):
            out[at, 0] = value[pl.ds(pl.multiple_of(unit * rows, rows), rows)]


def ffn_weight_grad(info, role, operands, added, after=()):
    attn_low, hid_grad, gelu_out, ffn_grad = operands
    planes, rows, cols = hid_grad.shape
    width = attn_low.shape[1]
    quarter, half = width // 4, planes // 2

    def kernel(which, info, attn_ref, hid_ref, gelu_ref, grad_ref, *refs):
        plane = pl.program_id(0)
        refs = refs[len(after) :] if added is None else refs[:2] + refs[2 + len(after) :]

        def put(value):
            for side in range(2):

                @pl.when(plane // half == side)
                def _(side=side):
                    if added is None:
                        refs[side][0] = value.astype(BF)
                    else:
                        recv, held = refs[side], refs[6]
                        held[...] = (value + recv[0].astype(F32)).astype(BF)
                        keep, send = refs[2 + 2 * side : 4 + 2 * side]
                        split_pairs(info, held, keep, send, quarter)

        @pl.when(which[0] == 0)
        def _():
            put(dot_tn(attn_ref[...], hid_ref[0]))

        @pl.when(which[0] == 1)
        def _():
            put(dot_tn(gelu_ref[0], grad_ref[...]))

    vm, sm = pl.BlockSpec(memory_space=pltpu.VMEM), pl.BlockSpec(memory_space=pltpu.SMEM)
    blocks = [
        pl.BlockSpec((1, width, cols), lambda i, w: (jnp.minimum(i, half - 1), 0, 0)),
        pl.BlockSpec((1, width, cols), lambda i, w: (jnp.maximum(i - half, 0), 0, 0)),
    ]
    pairs = [
        pl.BlockSpec((2, 1, quarter, cols), lambda i, w: (0, jnp.minimum(i, half - 1), 0, 0)),
        pl.BlockSpec((2, 1, quarter, cols), lambda i, w: (0, jnp.maximum(i - half, 0), 0, 0)),
    ]
    pair_shape = jax.ShapeDtypeStruct((2, half, quarter, cols), BF)
    hid_block = pl.BlockSpec((1, rows, cols), lambda i, w: (i * (1 - w[0]), 0, 0))
    gelu_block = pl.BlockSpec((1, rows, cols), lambda i, w: (i * w[0], 0, 0))
    args = [role, info, attn_low, hid_grad, gelu_out, ffn_grad]
    specs = [sm, vm, hid_block, gelu_block, vm]
    if added is not None:
        args += added
        specs += blocks
    return pl.pallas_call(
        kernel,
        out_shape=(
            [jax.ShapeDtypeStruct((half, width, cols), BF)] * 2
            if added is None
            else [pair_shape] * 4
        ),
        grid_spec=pltpu.PrefetchScalarGridSpec(
            num_scalar_prefetch=1,
            grid=(planes,),
            in_specs=specs + [pl.BlockSpec(memory_space=pl.ANY)] * len(after),
            out_specs=blocks if added is None else [pairs[0], pairs[0], pairs[1], pairs[1]],
            scratch_shapes=[] if added is None else [pltpu.VMEM((width, cols), BF)],
        ),
        compiler_params=pltpu.CompilerParams(vmem_limit_bytes=60 * MIB),
        cost_estimate=SMALL,
        name="ffn_weight_grad",
    )(*args, *after)


def attention_weight_grad(info, role, operands, planes, added, after=()):
    width = operands[0].shape[1]
    quarter = width // 4
    size = quarter // planes

    def kernel(info, which, kv, dk, dv, q_rows, dq, left, right, *refs):
        def put(mat, value, by_plane=False):
            if added is None:
                out, value = refs[0].at[mat], value.astype(BF)
            else:
                out = refs[3].at[mat]
            if by_plane:
                for plane in range(planes):
                    for quad in range(4):
                        at, to = (plane * 4 + quad) * size, (quad * planes + plane) * size
                        piece = value[at : at + size]
                        if added is not None:
                            piece = piece + refs[0][mat, to : to + size].astype(F32)
                        out[to : to + size] = piece.astype(BF)
            else:
                if added is not None:
                    value = value + refs[0][mat].astype(F32)
                out[...] = value.astype(BF)

        @pl.when(which[0] == 0)
        def _():
            put(0, dot_tn(kv[...], dk[...]))
            put(1, dot_tn(kv[...], dv[...]))

        @pl.when(which[0] == 1)
        def _():
            put(0, dot_tn(q_rows[...], dq[...]))
            put(1, dot_tn(left[...], right[...]), True)

        if added is not None:
            for mat in range(2):
                keep, send = refs[1].at[:, mat : mat + 1], refs[2].at[:, mat : mat + 1]
                split_pairs(info, refs[3].at[mat], keep, send, quarter)

    rows = operands[0].shape[0] + operands[3].shape[0]
    operands = [info, role] + list(operands)
    outs = [((2, width, width), BF)]
    scratch = []
    if added is not None:
        operands.append(added)
        outs = [((2, 2, quarter, width), BF)] * 2
        scratch = [pltpu.VMEM((2, width, width), BF)]
    result = call(
        kernel,
        "attention_weight_grad",
        operands,
        outs,
        scratch=scratch,
        flops=2 * rows * width * width,
        smem=2,
        after=after,
    )
    return result[0] if added is None else result


def add_pairs(info, kept, got, after=()):
    _, mats, rows, cols = kept.shape

    def kernel(info, kept_ref, got_ref, *refs):
        keep, send = refs[len(after) :]
        quad = info[WALK]
        at = jnp.where(info[ROLE] == 0, quad // 2, lax.rem(quad, 2))
        for index, out in ((at, keep), (1 - at, send)):
            out[0] = (kept_ref[index, 0].astype(F32) + got_ref[index, 0].astype(F32)).astype(BF)

    pairs = pl.BlockSpec((2, 1, rows, cols), lambda i: (0, i, 0, 0))
    one = pl.BlockSpec((1, rows, cols), lambda i: (i, 0, 0))
    return pl.pallas_call(
        kernel,
        grid=(mats,),
        out_shape=[jax.ShapeDtypeStruct((mats, rows, cols), BF)] * 2,
        in_specs=[pl.BlockSpec(memory_space=pltpu.SMEM), pairs, pairs]
        + [pl.BlockSpec(memory_space=pl.ANY)] * len(after),
        out_specs=[one, one],
        compiler_params=pltpu.CompilerParams(vmem_limit_bytes=16 * MIB),
        cost_estimate=SMALL,
        name="add_pairs",
    )(info, kept, got, *after)


def put_planes(info, held, keep, send):
    kind = lax.rem(info[PLANE], 2)
    for at in range(held.shape[0] // 2):
        keep[at] = held[2 * at + kind].astype(keep.dtype)
        send[at] = held[2 * at + 1 - kind].astype(send.dtype)


def ffn_blocks_kernel(info, kept_low, got_low, kept_high, got_high, keep, send):
    kind = lax.rem(info[PLANE], 2)
    for at, (kept, got) in enumerate(((kept_low, got_low), (kept_high, got_high))):
        for plane, out in ((kind, keep), (1 - kind, send)):
            out[at] = (kept[plane].astype(F32) + got[plane].astype(F32)).astype(out.dtype)


def attention_blocks_kernel(info, kept, got, keep, send, total, held):
    planes, _, rows, cols = held.shape
    size = rows // planes
    total[...] = kept[...].astype(F32) + got[...].astype(F32)
    for plane in range(planes):
        held[plane, 0] = total[0, :, plane * cols : (plane + 1) * cols]

    @pl.when(info[ROLE] == 0)
    def _():
        for plane in range(planes):
            held[plane, 1] = total[1, :, plane * cols : (plane + 1) * cols]

    @pl.when(info[ROLE] == 1)
    def _():
        for plane in range(planes):
            for at in range(planes):
                held[plane, 1, at * size : (at + 1) * size] = total[
                    1, plane * size : (plane + 1) * size, at * cols : (at + 1) * cols
                ]

    put_planes(info, held, keep, send)


def middle_kernel(info, kept, got, keep, send):
    mine = info[PLANE] // 2
    keep[...] = kept[mine] + got[mine].astype(F32)
    send[...] = (kept[1 - mine] + got[1 - mine].astype(F32)).astype(BF)


def ffn_total_kernel(info, own, other, keep, send, total):
    total[...] = own[...] + other[...].astype(F32)
    half = keep.shape[0]
    for index, out in ((info[ROLE], keep), (1 - info[ROLE], send)):
        out[...] = total[pl.ds(pl.multiple_of(index * half, half), half)]


def attention_total_kernel(info, own, other, keep, send, total, planes):
    total[...] = own[...] + other[...].astype(F32)
    half = keep.shape[1]
    for index, out in ((info[ROLE], keep), (1 - info[ROLE], send)):
        at = pl.ds(pl.multiple_of(index * half, half), half)
        out[0] = total[0, at]

        @pl.when(info[ROLE] == 0)
        def _(out=out, at=at):
            out[1] = total[1, at]

        @pl.when(info[ROLE] == 1)
        def _(out=out, index=index):
            size = half // planes
            for chunk in range(planes):
                start = pl.multiple_of(2 * chunk * size + index * size, size)
                out[1, chunk * size : (chunk + 1) * size] = total[1, pl.ds(start, size)]


def attention_final_kernel(info, kept, got, key_g, value_g, query_g, out_g, planes):
    def put(zero, one):
        key_g[...] = zero[0]
        value_g[...] = zero[1]
        query_g[...] = one[0]
        size = out_g.shape[0]
        chunks = [one[1, at * size : (at + 1) * size] for at in range(planes)]
        out_g[...] = jnp.concatenate(chunks, axis=1)

    @pl.when(info[ROLE] == 0)
    def _():
        put(kept, got)

    @pl.when(info[ROLE] == 1)
    def _():
        put(got, kept)


def ffn_final_kernel(info, kept, got, in_g, out_g):
    @pl.when(info[ROLE] == 0)
    def _():
        in_g[...] = kept[...]
        out_g[...] = got[...]

    @pl.when(info[ROLE] == 1)
    def _():
        in_g[...] = got[...]
        out_g[...] = kept[...]


def empty_row(width):
    heads = width // HD
    row = np.zeros((1, width + TILE), np.float32)
    row[:, width : width + heads] = NEG_FILL
    return jnp.asarray(row)


def blend_two_kernel(info, keep, got, sel, value):
    width = value.shape[1] - TILE
    tiles, lse = blend_values((keep, got), sel, width)
    for pair, tile in enumerate(tiles):
        value[:, pair * TILE : (pair + 1) * TILE] = tile
    value[:, width:] = as_parts(lse, width // HD).astype(BF)


def first_pieces(places, lengths, memory, weights, unit, block_len):
    sm, vm = pl.BlockSpec(memory_space=pltpu.SMEM), pl.BlockSpec(memory_space=pltpu.VMEM)
    rows, width = weights[0].shape
    return pl.pallas_call(
        functools.partial(first_pieces_kernel, unit=unit, block_len=block_len),
        out_shape=[
            jax.ShapeDtypeStruct((INFO,), jnp.int32),
            jax.ShapeDtypeStruct((4, rows // 4, width), BF),
            jax.ShapeDtypeStruct(memory.shape[1:], BF),
        ],
        in_specs=[sm, sm] + [pl.BlockSpec(memory_space=pl.ANY)] * 9,
        out_specs=[sm, vm, vm],
        scratch_shapes=[pltpu.SemaphoreType.DMA((5,))],
        compiler_params=pltpu.CompilerParams(vmem_limit_bytes=60 * MIB),
        cost_estimate=SMALL,
        name="first_pieces",
    )(places, lengths, memory, *weights)


def make_local(axis_seq, axis_head):
    unit = axis_seq // SLOTS
    fast = axis_seq == 8

    def swap(value, step):
        return lax.ppermute(value, "seq", [(i, i ^ step) for i in range(axis_seq)])

    def cross(value, order):
        steps = (2, 4) if order == 0 else (4, 2)
        return lax.ppermute(value, "seq", [(i, i ^ steps[i % 2]) for i in range(axis_seq)])

    def over(value, step):
        return lax.ppermute(value, "head", [(i, i ^ step) for i in range(axis_head)])

    def from_planes(value):
        got = [value]
        step = 1
        while step < axis_head:
            got += [over(value, step) if part is value else over(part, step) for part in got]
            step *= 2
        return got

    def direct_planes(value):
        return [value] + [over(value, step) for step in range(1, axis_head)]

    def local(
        tokens,
        memory,
        seq_lengths,
        pack_query,
        pack_key,
        pack_value,
        pack_out,
        unpack_query,
        unpack_key,
        unpack_value,
        unpack_out,
        ffn_in,
        ffn_in_bias,
        ffn_out,
        ffn_out_bias,
        mem_gain,
        mem_bias,
        attn_gain,
        attn_bias,
        out_gain,
        out_bias,
        cot_tokens,
        cot_memory,
    ):
        seq_index = lax.axis_index("seq")
        head_index = lax.axis_index("head")
        _, block_len, width = tokens.shape
        hidden_width = ffn_in.shape[1]
        my_lane, role = seq_index % unit, seq_index % 2
        quarter, head_cols = width // 4, width // axis_head
        info, pieces, mem = first_pieces(
            jnp.stack([seq_index, head_index]),
            seq_lengths,
            memory,
            [pack_key.T, pack_value.T, pack_query.T, pack_out]
            + [unpack_key.T, unpack_value.T, unpack_query.T, unpack_out],
            unit,
            block_len,
        )
        last = []

        def run(kernel, name, operands, outs, also=(), **more):
            after = list(last) + list(also)
            result = call(kernel, name, [info] + operands, outs, after=after, **more)
            last[:] = [result[0]]
            return result

        def run_grid(function, *operands):
            result = function(info, *operands, after=list(last))
            last[:] = [result[0] if isinstance(result, (list, tuple)) else result]
            return result

        def mine(value):
            return lax.dynamic_index_in_dim(value, head_index, 0, keepdims=False)

        def gather_unit(value):
            step = 1
            while step < unit:
                other = swap(value, step)
                low = (my_lane // step) % 2 == 0
                value = jnp.concatenate(
                    [jnp.where(low, value, other), jnp.where(low, other, value)], axis=0
                )
                step *= 2
            return value

        def scatter_unit(value, add, step):
            while step >= 1:
                half = value.shape[0] // 2
                low = (my_lane // step) % 2 == 0
                keep = jnp.where(low, value[:half], value[half:])
                send = jnp.where(low, value[half:], value[:half])
                value = add([keep, swap(send, step)])
                step //= 2
            return value

        def fetch_start(value):
            return [value] + [swap(value, j * unit) for j in range(1, SLOTS)]

        def fetch_finish(parts, also=()):
            shapes = [(parts[0].shape, BF)]
            sem = [pltpu.SemaphoreType.DMA]
            return run(pick_kernel, "pick_slot", parts, shapes, anys=SLOTS, scratch=sem, also=also)[0]

        def sum_rows(values):
            total = values[0].astype(F32)
            for value in values[1:]:
                total = total + value.astype(F32)
            return total.astype(BF)

        packed_width = width + TILE
        row_count = memory.shape[1]
        slot_count = unit * row_count
        half_rows = slot_count // 2
        sel = selectors(width)
        deep = [((row_count, packed_width), BF)] * SLOTS
        flat = [((row_count, width), BF)] * SLOTS

        def blend_two(values):
            return run(blend_two_kernel, "blend", values + [sel], [(values[0].shape, BF)])[0]

        def to_slots(keep, got, kernel, extra, outs, add, empty, also=()):
            if unit > 2:
                keep = scatter_unit(add([keep, got]), add, unit // 4)
                got = jnp.broadcast_to(empty, keep.shape).astype(BF)
            scratch = [pltpu.VMEM(keep.shape, BF)] if extra else []
            parts = run(kernel, "to_slots", [keep, got] + extra, outs, scratch=scratch, also=also)
            return [parts[0]] + [swap(parts[j], j * unit) for j in range(1, SLOTS)]

        def spread(piece, first, second, third):
            parts = [piece, first, second, third]
            return parts + [swap(part, 1) for part in parts]

        def all_planes(pieces):
            return run(
                stack_kernel, "all_planes", pieces, [((axis_head,) + pieces[0].shape, BF)]
            )[0]

        held_out = pltpu.VMEM((axis_head, 4, head_cols // 4, width), BF)
        held_pair = pltpu.VMEM((2, 2) + held_out.shape, BF)
        pair_sems = pltpu.SemaphoreType.DMA((2, 2, 4 * axis_head))
        out_sems = pltpu.SemaphoreType.DMA((4 * axis_head,))
        ffn_sems = pltpu.SemaphoreType.DMA((axis_head, 8))
        tok_low, slot_low = ((block_len, width), BF), ((slot_count, width), BF)
        row_low, half_low = ((row_count, width), BF), ((half_rows, width), BF)
        tok_f32 = ((block_len, width), F32)

        mem_parts = fetch_start(mem)
        planes = from_planes(pieces)
        piece_ffn, tok, cot_tok, cot_mem = run(
            other_pieces_kernel,
            "other_pieces",
            [ffn_in_bias, ffn_in, ffn_out, tokens, cot_tokens, cot_memory],
            [((width + 16, hidden_width), BF), tok_low, tok_low, row_low],
            anys=5,
            scratch=[pltpu.SemaphoreType.DMA((6,))],
        )
        mem_picked = fetch_finish(mem_parts)
        shape = (2, axis_head) + pieces.shape[1:]
        rows_pack, rows_un = run(planes_kernel, "weight_planes", planes, [(shape, BF)] * 2)

        pack_first, pack_second = cross(rows_pack, 0), cross(rows_pack, 1)
        pack_third = cross(pack_first, 1)
        w_pack = spread(rows_pack, pack_first, pack_second, pack_third)
        rows_un = tie(rows_un, pack_third)
        un_first, un_second = cross(rows_un, 0), cross(rows_un, 1)
        ffn_rows = lax.all_gather(tie(piece_ffn, rows_pack), "head", axis=0)
        mem_slot = gather_unit(mem_picked)
        k_pack, v_pack, q_pack, keep, send = run(
            pack_forward_kernel,
            "pack_forward",
            [tok, mem_slot] + w_pack,
            [tok_low, tok_low, slot_low] + [((half_rows, packed_width), BF)] * 2,
            anys=8,
            scratch=[pltpu.VMEM((slot_count, packed_width), BF), held_pair, pair_sems],
        )
        got = swap(send, unit // 2)
        un_first = tie(un_first, keep)
        w_un = spread(rows_un, un_first, un_second, cross(un_first, 1))
        parts = to_slots(keep, got, blend_kernel, [sel], deep, blend_two, empty_row(width), [un_second])
        mem_result, mix_low, pack_ctx, pack_lse, grad_memsum, mem_vectors = run(
            memory_kernel,
            "memory_rows",
            parts + [sel, mem, cot_mem, mem_gain, mem_bias] + w_pack,
            [row_low, row_low, row_low]
            + [((row_count, TILE), F32), ((row_count, width), F32), ((8, width), F32)],
            anys=8,
            scratch=[held_out, out_sems],
            also=[w_un[3]],
        )
        mix_parts = fetch_start(mix_low)
        mix_picked = fetch_finish(mix_parts, w_un)
        mix_slot = gather_unit(mix_picked)
        ffn_rows = tie(ffn_rows, mix_slot)
        ffn_parts = [ffn_rows, swap(ffn_rows, 1)]
        k_un, v_un, q_un, tok_ctx, tok_lse, attn_normed, attn_inv = run(
            unpack_forward_kernel,
            "unpack_forward",
            [tok, mix_slot] + w_un,
            [slot_low, slot_low, tok_low, tok_low]
            + [((16, block_len), F32), tok_f32, ((block_len, 1), F32)],
            anys=8,
            scratch=[held_pair, pair_sems],
        )
        by_plane = (axis_head, block_len, hidden_width)
        held_ffn = pltpu.VMEM((2, axis_head, width, hidden_width), BF)
        plane_sems = pltpu.SemaphoreType.DMA((axis_head,))
        (
            out_result,
            attn_low,
            ffn_grad,
            mix_grad,
            mix_sum,
            out_vectors,
            hid_vec,
            gelu_out,
            hid_grad,
        ) = run(
            ffn_kernel,
            "ffn",
            [attn_normed, attn_inv, cot_tok, mem_result]
            + [attn_gain, attn_bias, out_gain, out_bias, ffn_out_bias]
            + ffn_parts,
            [((block_len + row_count, width), BF), tok_low, tok_low, tok_low, tok_f32]
            + [((8, width), F32), ((axis_head, 1, hidden_width), F32)]
            + [(by_plane, BF), (by_plane, BF)],
            anys=2,
            out_any=2,
            scratch=[
                held_ffn,
                pltpu.VMEM((axis_head, 16, hidden_width), BF),
                pltpu.VMEM((block_len, width), F32),
                pltpu.VMEM(by_plane, BF),
                pltpu.VMEM(by_plane, BF),
                ffn_sems,
                plane_sems,
                pltpu.SemaphoreType.DMA((axis_head, 2)),
            ],
        )
        out_rows = lax.all_gather(out_result, "head", axis=0)
        out_tokens, out_memory = out_rows[:, :block_len], out_rows[:, block_len:]

        role_info, other_info = role[None], 1 - role[None]
        ffn_operands = (attn_low, hid_grad, gelu_out, ffn_grad)

        def vectors_step(value, other):
            return run(total_kernel, "vectors", [value, other], [(value.shape, F32)])[0]

        small = run(
            vectors_kernel,
            "vectors",
            [mem_vectors, out_vectors, hid_vec],
            [((16, width), F32)],
        )[0]
        small_got = swap(small, 1)
        uq_grad, uk_part, uv_part, keep, send, tok_part = run(
            unpack_backward_kernel,
            "unpack_backward",
            [q_un, k_un, v_un, tok_ctx, tok_lse, mix_grad, mix_sum] + w_un,
            [tok_low, slot_low, slot_low, half_low, half_low, tok_f32],
            anys=8,
            scratch=[held_pair, pair_sems],
        )
        un_operands = (mix_slot, uk_part, uv_part, tok, uq_grad, tok_ctx, mix_grad)
        got = swap(send, unit // 2)
        small = vectors_step(small, small_got)
        small_got = swap(small, 2)
        if fast:
            ffn_sent = run_grid(ffn_weight_grad, other_info, ffn_operands, None)
            ffn_got = [swap(sent, 1) for sent in ffn_sent]
        parts = to_slots(keep, got, sum_kernel, [], flat, sum_rows, jnp.zeros((), BF))
        if fast:
            ffn_low, low_sent, ffn_high, high_sent = run_grid(
                ffn_weight_grad, role_info, ffn_operands, ffn_got
            )
        small = vectors_step(small, small_got)
        mem_mix_grad, packed = run(
            memory_back_kernel,
            "memory_rows_backward",
            parts + [sel, grad_memsum, pack_ctx, pack_lse] + w_pack,
            [row_low, ((row_count, packed_width), BF)],
            anys=8,
            scratch=[held_out, out_sems],
        )
        back_parts = fetch_start(packed)
        if fast:
            un_sent = run_grid(attention_weight_grad, other_info, un_operands, axis_head, None)
        back_picked = fetch_finish(back_parts, [out_rows])
        if fast:
            low_got = cross(tie(low_sent, back_picked), 0)
            un_got = swap(tie(un_sent, back_picked), 1)
        back = gather_unit(back_picked)
        pq_part, pk_grad, pv_grad, grad_tokens, keep, send = run(
            pack_backward_kernel,
            "pack_backward",
            [back, sel, q_pack, k_pack, v_pack, tok_part] + w_pack,
            [slot_low, tok_low, tok_low, ((block_len + 16, width), BF), half_low, half_low],
            anys=8,
            scratch=[held_pair, pair_sems],
        )
        grad_tokens = lax.all_gather(grad_tokens, "head", axis=0)[:, :block_len]
        pack_operands = (tok, pk_grad, pv_grad, mem_slot, pq_part, pack_ctx, mem_mix_grad)
        got = swap(send, unit // 2)
        if fast:
            ffn_low, low_sent = run_grid(add_pairs, ffn_low, low_got)
            high_got = cross(tie(high_sent, ffn_low), 0)
            un_kept, un_sent = run_grid(
                attention_weight_grad, role_info, un_operands, axis_head, un_got
            )
            pack_sent = run_grid(attention_weight_grad, other_info, pack_operands, axis_head, None)
        step = 4
        while step < axis_seq:
            small = vectors_step(small, swap(small, step))
            step *= 2
        parts = to_slots(keep, got, sum_kernel, [], flat, sum_rows, jnp.zeros((), BF))

        rows = (quarter, hidden_width)
        half = (quarter // 2, hidden_width)
        pair_rows = (2, quarter, head_cols)
        pair_half = (2, quarter // 2, head_cols)

        def pairs_of(shape):
            return [((2,) + shape, F32), ((2,) + shape, BF)]

        def middle(kept, got, shape):
            keep, send = run(
                middle_kernel, "plane_middle", [kept, got], [(shape, F32), (shape, BF)]
            )
            return keep, over(send, 2)

        def ffn_blocks(kept, got):
            operands = [kept[0], got[0], kept[1], got[1]]
            keep, send = run(ffn_blocks_kernel, "plane_blocks", operands, pairs_of(rows))
            return keep, over(send, 1)

        def ffn_total(kept, got):
            scratch = [pltpu.VMEM(rows, F32)]
            keep, send = run(
                ffn_total_kernel, "plane_total", [kept, got], [(half, F32)] * 2, scratch=scratch
            )
            return [keep, swap(send, 1)]

        def ffn_final(halves):
            outs = [(half, F32)] * 2
            return run(ffn_final_kernel, "weight_rows", halves, outs, also=[grad_tokens])

        def attention_blocks(kept, got):
            keep, send = run(
                attention_blocks_kernel,
                "plane_blocks",
                [kept, got],
                pairs_of(pair_rows),
                scratch=[
                    pltpu.VMEM((2, quarter, width), F32),
                    pltpu.VMEM((axis_head,) + pair_rows, F32),
                ],
            )
            return keep, over(send, 1)

        def attention_total(kept, got):
            keep, send = run(
                functools.partial(attention_total_kernel, planes=axis_head),
                "plane_total",
                [kept, got],
                [(pair_half, F32)] * 2,
                scratch=[pltpu.VMEM(pair_rows, F32)],
            )
            return [keep, swap(send, 1)]

        def attention_final(halves):
            return run(
                functools.partial(attention_final_kernel, planes=axis_head),
                "weight_rows",
                halves,
                [(pair_half[1:], F32)] * 3 + [((quarter // 2 // axis_head, width), F32)],
            )

        def scatter(value, axis, dim):
            return lax.psum_scatter(value, axis, scatter_dimension=dim, tiled=True)

        def by_columns(grad):
            grad = scatter(grad, "seq", 0).reshape(-1, axis_head, head_cols)
            return scatter(grad.transpose(1, 0, 2), "head", 0)[0].astype(F32)

        def by_rows(grad):
            grad = scatter(grad.reshape(axis_head, -1, width), "seq", 1)
            return scatter(grad, "head", 0)[0].astype(F32)

        def product(left, right):
            return dot_tn(left, right).astype(BF)

        def attention_simple(operands):
            kv, dk, dv, q_rows, dq, left, right = operands
            first = [by_columns(product(a, b)) for a, b in ((kv, dk), (kv, dv), (q_rows, dq))]
            return first + [by_rows(product(left, right))]

        if fast:
            ffn_high, high_sent = run_grid(add_pairs, ffn_high, high_got)
            low_got, high_got = cross(tie(low_sent, ffn_high), 1), cross(high_sent, 1)
            pack_got = swap(tie(pack_sent, ffn_high), 1)
            pack_kept, pack_sent = run_grid(
                attention_weight_grad, role_info, pack_operands, axis_head, pack_got
            )
        done = [out_tokens, out_memory]
        total = run(
            memory_total_kernel, "memory_total", [grad_memsum] + parts, [row_low], also=done
        )[0]
        grad_planes = from_planes(total)
        if fast:
            un_got = cross(tie(un_sent, total), 0)
            blocks = ffn_blocks([ffn_low, ffn_high], [low_got, high_got])
            pack_got = cross(tie(pack_sent, blocks[0]), 0)
            un_kept, un_sent = run_grid(add_pairs, un_kept, un_got)
            un_got = cross(un_sent, 1)
            pack_kept, pack_sent = run_grid(add_pairs, pack_kept, pack_got)
            pack_got = cross(pack_sent, 1)
            blocks = middle(*blocks, rows)
            un_blocks = attention_blocks(un_kept, un_got)
            pack_blocks = attention_blocks(pack_kept, pack_got)
            halves = ffn_total(*blocks)
            grad_memory = all_planes(grad_planes)
            un_blocks = middle(*un_blocks, pair_rows)
            pack_blocks = middle(*pack_blocks, pair_rows)
            small_planes = direct_planes(tie(small, grad_memory))
            fi_grad, fo_grad = ffn_final(halves)
            un_halves = attention_total(*un_blocks)
            small = run(
                plane_vectors_kernel,
                "vectors",
                small_planes,
                [(small.shape, F32)],
                scratch=[pltpu.VMEM((axis_head,) + small.shape, F32)],
            )[0]
            pack_halves = attention_total(*pack_blocks)
            un_grads = attention_final(un_halves)
            pack_grads = attention_final(pack_halves)
        else:
            grad_memory = all_planes(grad_planes)
            small_planes = direct_planes(small)
            small = run(
                plane_vectors_kernel,
                "vectors",
                small_planes,
                [(small.shape, F32)],
                scratch=[pltpu.VMEM((axis_head,) + small.shape, F32)],
            )[0]
            un_grads = attention_simple(un_operands)
            pack_grads = attention_simple(pack_operands)
            fi_grad = jnp.stack([product(attn_low, hid_grad[p]) for p in range(axis_head)])
            fi_grad = scatter(scatter(fi_grad, "seq", 1), "head", 0)[0].astype(F32)
            fo_grad = jnp.stack([product(gelu_out[p], ffn_grad) for p in range(axis_head)])
            fo_grad = scatter(scatter(fo_grad, "seq", 1), "head", 0)[0].astype(F32)

        share = width // axis_seq
        vectors = lax.dynamic_slice_in_dim(small[:7], seq_index * share, share, 1)
        fib = mine(small[7 : 7 + axis_head].reshape(axis_head, -1))
        fib = lax.dynamic_slice_in_dim(fib, seq_index * share, share, 0)
        return (
            out_tokens,
            out_memory,
            grad_tokens,
            grad_memory,
            pack_grads[2],
            pack_grads[0],
            pack_grads[1],
            pack_grads[3],
            un_grads[2],
            un_grads[0],
            un_grads[1],
            un_grads[3],
            fi_grad,
            fib,
            fo_grad,
            vectors[0],
            vectors[1],
            vectors[2],
            vectors[3],
            vectors[4],
            vectors[5],
            vectors[6],
        )

    return local


def solution(mesh):
    rows = P(None, "seq", None)
    by_col, by_row, both = P(None, "head"), P("head", None), P("seq", "head")
    wide_rows = P(("head", "seq"), None)
    in_specs = (
        (rows, rows, P())
        + (by_col, by_col, by_col, by_row)
        + (by_col, by_col, by_col, by_row)
        + (by_col, P("head"), by_row)
        + (P(),) * 7
        + (rows, rows)
    )
    out_specs = (
        (rows,) * 4
        + (both, both, both, wide_rows)
        + (both, both, both, wide_rows)
        + (both, P(("head", "seq")), wide_rows)
        + (P("seq"),) * 7
    )
    local = make_local(mesh.shape["seq"], mesh.shape["head"])
    return jax.shard_map(local, mesh=mesh, in_specs=in_specs, out_specs=out_specs, check_vma=False)
```
